32 devices in a mesh: groups: 2 (over y), rows: 4 (over z), cols: 2 (over x), pair: 2 (over core).
Axes of the slice: x: 2, y: 2, z: 4, core: 2. Of those that a mesh axis runs over, the one named last changes fastest.
Arguments:
- frames: bfloat16 [2, 240, 60, 256], P('pair', ('groups', 'rows'), 'cols'), parts along dimension 1, may hold values from -28 to 28
- conv_first: bfloat16 [9, 256, 256], replicated, may hold values from -0.125 to 0.125
- conv_second: bfloat16 [9, 256, 256], replicated, may hold values from -0.125 to 0.125
- candidates: int32 [8, 2, 9], P(('groups', 'rows'), 'cols'), parts along dimension 0, may hold values from -1 to 8, as said below
- counts: int32 [8, 2], P(('groups', 'rows'), 'cols'), parts along dimension 0, may hold values from 1 to 6, as said below
- cotangent: float32 [2, 240, 60], P(None, ('groups', 'rows', 'pair'), 'cols'), parts along dimension 1, may hold values from -1536 to 1536
Outputs:
- flow: float32 [2, 240, 60], P(None, ('groups', 'rows', 'pair'), 'cols'), parts along dimension 1
- grad_first: float32 [240, 60, 256], P(('groups', 'rows', 'pair'), 'cols'), parts along dimension 0
- grad_second: float32 [240, 60, 256], P(('groups', 'rows', 'pair'), 'cols'), parts along dimension 0
The draws below stay inside these ranges and needn't reach their ends.
There are 2 independent parts, one for each index of `groups`. The reference program is written for one: setup_inputs(seed, part) draws one part's arguments, and reference() takes and returns one part's arrays. A program takes and returns all parts, laid end to end along the dimension named above; an argument that names none is the same for every part. Nothing has to cross between parts.
Inputs may be any that keep to these rules, and one draw needn't show every extreme that they name: `candidates`: for each query tile the first counts entries are different codes of tiles of its 3 x 3 neighbourhood that lie inside the grid, the first of them 4 (the tile itself); the remaining entries are -1. `counts`: some tile lists every tile of its neighbourhood inside the grid, 6.
All inputs are finite; a program needn't handle non-finite values.
Results may differ from the reference program's by a relative error of at most 0.0095.
The reference program's roundings to bfloat16 on the way (of `hidden` and `dscore`) count: a program that leaves them out, or rounds other values in their place, can miss the bound.
Values may be sent and summed in bfloat16 or wider, within the bound.
No kernel may reach another device: no remote copies, remote signals or barrier semaphores. Data moves between devices by JAX's collectives and lax.ppermute only.
A program may use at most 64 MiB of HBM per device.

```python
import jax
import jax.numpy as jnp
from jax import lax

C = 256
TILE = 30
SLOTS = 9
NTR = 4
NTC = 2
H = 120
W = 60


def candidate_table(key):
    key = jax.random.fold_in(key, 11)
    keys_all = jax.random.split(key, 5)
    shape_full = (NTR, NTC, SLOTS)
    tile_row = lax.broadcasted_iota(jnp.int32, shape_full, 0)
    tile_col = lax.broadcasted_iota(jnp.int32, shape_full, 1)
    tile_code = lax.broadcasted_iota(jnp.int32, shape_full, 2)
    near_row = tile_row + tile_code // 3 - 1
    near_col = tile_col + tile_code % 3 - 1
    inside = (near_row >= 0) & (near_row < NTR) & (near_col >= 0) & (near_col < NTC)
    ranking = jax.random.randint(keys_all[0], shape_full, 0, 4096) * 16 + tile_code
    ranking = jnp.where(tile_code == 4, -1, ranking)
    ranking = jnp.where(inside, ranking, 1000000 + tile_code)
    ordered = jnp.argsort(ranking, axis=2).astype(jnp.int32)
    usable = jnp.sum(inside.astype(jnp.int32), axis=2)
    factor_one = jax.random.randint(keys_all[1], (NTR, NTC), 0, 9)
    factor_two = jax.random.randint(keys_all[2], (NTR, NTC), 0, 9)
    wanted = 1 + factor_one * factor_two // 4
    number = jnp.minimum(wanted, usable)
    if NTR >= 3:
        row_low, row_high = (1, NTR - 1)
    else:
        row_low, row_high = (0, NTR)
    if NTC >= 3:
        col_low, col_high = (1, NTC - 1)
    else:
        col_low, col_high = (0, NTC)
    busiest_row = jax.random.randint(keys_all[3], (), row_low, row_high)
    busiest_col = jax.random.randint(keys_all[4], (), col_low, col_high)
    plane_row = lax.broadcasted_iota(jnp.int32, (NTR, NTC), 0)
    plane_col = lax.broadcasted_iota(jnp.int32, (NTR, NTC), 1)
    number = jnp.where((plane_row == busiest_row) & (plane_col == busiest_col), usable, number)
    listed = jnp.where(tile_code < number[:, :, None], ordered, -1)
    return (listed.astype(jnp.int32), number.astype(jnp.int32))


def draw_candidates(key, part):
    return candidate_table(key)[0]


def draw_counts(key, part):
    return candidate_table(key)[1]


def draw_frames(key, part):
    key = jax.random.fold_in(key, 5)
    keys_all = jax.random.split(key, 1)
    result = jax.random.truncated_normal(keys_all[0], -4.0, 4.0, (2, H, W, C), jnp.float32)
    return result.astype(jnp.bfloat16)


def shard_levels(key, extent, cuts, low, top_value):
    def one(position, blocks):
        steps = jax.random.uniform(jax.random.fold_in(jax.random.fold_in(key, 6), position), (blocks,), jnp.float32, low / len(cuts), top_value / len(cuts))
        return jnp.repeat(jnp.exp(steps), extent[position] // blocks).reshape((-1,) + (1,) * (len(extent) - position - 1))

    level = one(*cuts[0])
    for cut in cuts[1:]:
        level = level * one(*cut)
    return level


def noise(rng, extent, scale, reach, cuts=(), held_as=jnp.bfloat16):
    drawn = scale * jax.random.normal(rng, extent, jnp.float32)
    if cuts:
        drawn = drawn * shard_levels(rng, extent, cuts, -0.22, 0.18)
    return jnp.clip(drawn, -reach, reach).astype(held_as)


def setup_inputs(seed: int = 0, part: int = 0) -> dict:
    keys = jax.random.split(jax.random.key(seed), 7)
    part_keys = jax.random.split(jax.random.fold_in(keys[6], part), 7)
    return {
        "frames": draw_frames(jax.random.fold_in(jax.random.fold_in(keys[6], part), 71), part),
        "conv_first": noise(keys[1], (9, C, C), (9 * C) ** -0.5, 0.125),
        "conv_second": noise(keys[2], (9, C, C), (9 * C) ** -0.5, 0.125),
        "candidates": draw_candidates(jax.random.fold_in(jax.random.fold_in(keys[6], part), 71), part),
        "counts": draw_counts(jax.random.fold_in(jax.random.fold_in(keys[6], part), 71), part),
        "cotangent": noise(part_keys[5], (2, H, W), 256.0, 1536.0, ((1, 8), (2, 2)), jnp.float32),
    }


def conv_valid(field_ext, weights, out_rows, out_cols):
    channels = field_ext.shape[2]
    accumulated = jnp.zeros((out_rows * out_cols, weights.shape[2]), jnp.float32)
    for tap_index in range(9):
        row_start = tap_index // 3
        col_start = tap_index % 3
        window = field_ext[row_start:row_start + out_rows, col_start:col_start + out_cols]
        accumulated = accumulated + jnp.dot(window.reshape(out_rows * out_cols, channels), weights[tap_index], preferred_element_type=jnp.float32)
    return accumulated.reshape(out_rows, out_cols, weights.shape[2])


def encode(frame, conv_first, conv_second):
    height = frame.shape[0]
    width = frame.shape[1]
    padded = jnp.pad(frame, ((1, 1), (1, 1), (0, 0)))
    hidden = jax.nn.relu(conv_valid(padded, conv_first, height, width)).astype(jnp.bfloat16)
    padded_hidden = jnp.pad(hidden, ((1, 1), (1, 1), (0, 0)))
    return (frame.astype(jnp.float32) + conv_valid(padded_hidden, conv_second, height, width)).astype(jnp.bfloat16)


def softmax_stats(query, fetch, code_list, count, key_row, key_col):
    scale = query.shape[1] ** -0.5
    cells = query.shape[0]

    def step(slot_index, state):
        best, norm_sum, sum_row, sum_col = state
        tile_code = code_list[slot_index]
        targets = fetch(tile_code)
        pos_row = (tile_code // 3 - 1).astype(jnp.float32) + key_row
        pos_col = (tile_code % 3 - 1).astype(jnp.float32) + key_col
        scores = lax.dot_general(query, targets, (((1,), (1,)), ((), ())), preferred_element_type=jnp.float32) * scale
        new_best = jnp.maximum(best, jnp.max(scores, axis=1))
        factor = jnp.exp(best - new_best)
        expo = jnp.exp(scores - new_best[:, None])
        norm_sum = norm_sum * factor + jnp.sum(expo, axis=1)
        sum_row = sum_row * factor + jnp.sum(expo * pos_row[None, :], axis=1)
        sum_col = sum_col * factor + jnp.sum(expo * pos_col[None, :], axis=1)
        return new_best, norm_sum, sum_row, sum_col

    start = (jnp.full((cells,), -jnp.inf, jnp.float32), jnp.zeros((cells,), jnp.float32), jnp.zeros((cells,), jnp.float32), jnp.zeros((cells,), jnp.float32))
    return lax.fori_loop(0, count, step, start)


def gradient_pass(query, fetch, code_list, count, key_row, key_col, query_row, query_col, cot_row, cot_col, stats, accumulator, deposit):
    scale = query.shape[1] ** -0.5
    best, norm_sum, sum_row, sum_col = stats
    flow_row = sum_row / norm_sum - query_row
    flow_col = sum_col / norm_sum - query_col
    mean_pull = cot_row * flow_row + cot_col * flow_col

    def step(slot_index, state):
        grad_query, acc_state = state
        tile_code = code_list[slot_index]
        targets = fetch(tile_code)
        pos_row = (tile_code // 3 - 1).astype(jnp.float32) + key_row
        pos_col = (tile_code % 3 - 1).astype(jnp.float32) + key_col
        scores = lax.dot_general(query, targets, (((1,), (1,)), ((), ())), preferred_element_type=jnp.float32) * scale
        probs = jnp.exp(scores - best[:, None]) / norm_sum[:, None]
        pull = cot_row[:, None] * (pos_row[None, :] - query_row[:, None]) + cot_col[:, None] * (pos_col[None, :] - query_col[:, None])
        dscore = (probs * (pull - mean_pull[:, None]) * scale).astype(jnp.bfloat16)
        grad_query = grad_query + jnp.dot(dscore, targets, preferred_element_type=jnp.float32)
        contrib = lax.dot_general(dscore, query, (((0,), (0,)), ((), ())), preferred_element_type=jnp.float32)
        return grad_query, deposit(acc_state, tile_code, contrib)

    start = (jnp.zeros(query.shape, jnp.float32), accumulator)
    return flow_row, flow_col, lax.fori_loop(0, count, step, start)


def to_tiles(grid_field):
    return grid_field.reshape(NTR, TILE, NTC, TILE, -1).transpose(0, 2, 1, 3, 4).reshape(NTR * NTC, TILE * TILE, -1)


def from_tiles(tiles):
    return tiles.reshape(NTR, NTC, TILE, TILE, -1).transpose(0, 2, 1, 3, 4).reshape(NTR * TILE, NTC * TILE, -1)


def reference(frames, conv_first, conv_second, candidates, counts, cotangent):
    first = encode(frames[0], conv_first, conv_second)
    second = encode(frames[1], conv_first, conv_second)
    query_tiles = to_tiles(first)
    target_tiles = jnp.pad(to_tiles(second).reshape(NTR, NTC, TILE * TILE, C), ((1, 1), (1, 1), (0, 0), (0, 0))).reshape((NTR + 2) * (NTC + 2), TILE * TILE, C)
    cot_tiles = to_tiles(cotangent.transpose(1, 2, 0))
    code_lists = candidates.reshape(NTR * NTC, SLOTS)
    count_list = counts.reshape(NTR * NTC)
    cell_index = jnp.arange(TILE * TILE, dtype=jnp.int32)
    key_row = (cell_index // TILE).astype(jnp.float32) / TILE
    key_col = (cell_index % TILE).astype(jnp.float32) / TILE

    def per_tile(accumulator, tile_index):
        tile_row = tile_index // NTC
        tile_col = tile_index % NTC

        def place(tile_code):
            return ((tile_row + tile_code // 3) * (NTC + 2) + tile_col + tile_code % 3).astype(jnp.int32)

        def fetch(tile_code):
            return lax.dynamic_index_in_dim(target_tiles, place(tile_code), 0, keepdims=False)

        def deposit(acc_in, tile_code, contrib):
            spot = place(tile_code)
            current = lax.dynamic_index_in_dim(acc_in, spot, 0, keepdims=False)
            return lax.dynamic_update_index_in_dim(acc_in, current + contrib, spot, 0)

        query = lax.dynamic_index_in_dim(query_tiles, tile_index, 0, keepdims=False)
        pulls = lax.dynamic_index_in_dim(cot_tiles, tile_index, 0, keepdims=False)
        code_list = lax.dynamic_index_in_dim(code_lists, tile_index, 0, keepdims=False)
        count = lax.dynamic_index_in_dim(count_list, tile_index, 0, keepdims=False)
        stats = softmax_stats(query, fetch, code_list, count, key_row, key_col)
        flow_row, flow_col, (grad_query, accumulator) = gradient_pass(query, fetch, code_list, count, key_row, key_col, key_row, key_col, pulls[:, 0], pulls[:, 1], stats, accumulator, deposit)
        return accumulator, (jnp.stack([flow_row, flow_col], axis=1), grad_query)

    start = jnp.zeros(((NTR + 2) * (NTC + 2), TILE * TILE, C), jnp.float32)
    accumulator, (flow_tiles, grad_tiles) = lax.scan(per_tile, start, jnp.arange(NTR * NTC, dtype=jnp.int32))
    flow = from_tiles(flow_tiles).transpose(2, 0, 1)
    grad_first = from_tiles(grad_tiles)
    inner = accumulator.reshape(NTR + 2, NTC + 2, TILE * TILE, C)[1:-1, 1:-1].reshape(NTR * NTC, TILE * TILE, C)
    grad_second = from_tiles(inner)
    return flow, grad_first, grad_second
```

```python
import functools
import math

import jax
import jax.numpy as jnp
from jax import lax
from jax.experimental import pallas as pl
from jax.experimental.pallas import tpu as pltpu
from jax.sharding import PartitionSpec as P

TILE = 30
HALF = 15
PADW = 32
HC = HALF * PADW
BODY = HALF + 2
EXT = HALF + 4
HID = HALF + 2
AXES = ("rows", "cols", "pair")
VMEM = pl.BlockSpec(memory_space=pltpu.VMEM)
SMEM = pl.BlockSpec(memory_space=pltpu.SMEM)
ANY = pl.BlockSpec(memory_space=pl.ANY)


def send(value, step):
    n_r, n_c = lax.axis_size("rows"), lax.axis_size("cols")
    pairs = []
    for r in range(n_r):
        for k in range(n_c):
            for c in range(2):
                r2, k2, c2 = step(r, k, c)
                if 0 <= r2 < n_r and 0 <= k2 < n_c:
                    pairs.append(((r * n_c + k) * 2 + c, (r2 * n_c + k2) * 2 + c2))
    return lax.ppermute(value, AXES, pairs)


def partner(value):
    return send(value, lambda r, k, c: (r, k, 1 - c))


def updown(value):
    return send(value, lambda r, k, c: (r + 1 - 2 * c, k, c))


def sideways(value):
    if lax.axis_size("cols") == 2:
        return [send(value, lambda r, k, c: (r, 1 - k, c))]
    return [
        send(value, lambda r, k, c: (r, k + 1, c)),
        send(value, lambda r, k, c: (r, k - 1, c)),
    ]


def gather_tiles(half):
    level = [jnp.stack([half, partner(half)])]
    for side in sideways(half):
        level.append(jnp.stack([side, partner(side)]))
    got = [updown(t) for t in level]
    other = [partner(t) for t in got]
    return level, got, other


def encode_kernel(frame, n_r, n_c, sc, mine, got, xl, xr, z, w1, w2, out, ext, xcat, hid, hcat):
    core, row, col = sc[0], sc[1], sc[2]
    first_row = 2 * (1 - core)
    use_own = core == frame
    own_rows = mine[pl.ds((BODY - 4) * core, BODY)]
    body = jnp.where(use_own, own_rows, got[...]).astype(jnp.float32)
    slot = jnp.where(use_own, 0, 1)
    left = jnp.where(col > 0, xl[slot].astype(jnp.float32), 0.0)
    right = jnp.where(col < n_c - 1, xr[slot].astype(jnp.float32), 0.0)
    ext[pl.ds(first_row, BODY), 2 : 2 + TILE] = body
    ext[pl.ds(first_row, BODY), 0:2] = left
    ext[pl.ds(first_row, BODY), 2 + TILE : 4 + TILE] = right
    ext[pl.ds(BODY * core, 2), 0 : 4 + TILE] = z[1 - slot].astype(jnp.float32)
    ch = body.shape[-1]
    for b in range(3):
        xcat[:, b * ch : (b + 1) * ch] = (
            ext[:, b : b + PADW].astype(jnp.bfloat16).reshape(EXT * PADW, ch)
        )
    acc = jnp.zeros((HID * PADW, ch), jnp.float32)
    for a in range(3):
        acc += jnp.dot(
            xcat[a * PADW : (a + HID) * PADW], w1[a], preferred_element_type=jnp.float32
        )
    hr = lax.broadcasted_iota(jnp.int32, (HID, PADW, ch), 0) + (row * TILE + core * HALF - 1)
    hc = lax.broadcasted_iota(jnp.int32, (HID, PADW, ch), 1) + (col * TILE - 1)
    inside = (hr >= 0) & (hr < n_r * TILE) & (hc >= 0) & (hc < n_c * TILE)
    hidden = jnp.where(inside, jnp.maximum(acc, 0.0).reshape(HID, PADW, ch), 0.0)
    hid[0 : HID * PADW] = hidden.reshape(HID * PADW, ch)
    hid[HID * PADW :] = jnp.zeros((8, ch), jnp.float32)
    for b in range(3):
        hcat[:, b * ch : (b + 1) * ch] = hid[b : b + HID * PADW].astype(jnp.bfloat16)
    acc2 = ext[2 : 2 + HALF, 2 : 2 + PADW].reshape(HC, ch)
    for a in range(3):
        acc2 += jnp.dot(hcat[a * PADW : a * PADW + HC], w2[a], preferred_element_type=jnp.float32)
    oc = lax.broadcasted_iota(jnp.int32, (HALF, PADW, ch), 1)
    out[...] = (
        jnp.where(oc < TILE, acc2.reshape(HALF, PADW, ch), 0.0)
        .astype(jnp.bfloat16)
        .reshape(HC, ch)
    )


def encode(frame, n_r, n_c, sc, mine, got, xl, xr, z, w1, w2):
    ch = mine.shape[-1]
    return pl.pallas_call(
        functools.partial(encode_kernel, frame, n_r, n_c),
        out_shape=jax.ShapeDtypeStruct((HC, ch), jnp.bfloat16),
        in_specs=[SMEM] + [VMEM] * 7,
        out_specs=VMEM,
        scratch_shapes=[
            pltpu.VMEM((EXT, 40, ch), jnp.float32),
            pltpu.VMEM((EXT * PADW, 3 * ch), jnp.bfloat16),
            pltpu.VMEM((HID * PADW + 8, ch), jnp.float32),
            pltpu.VMEM((HID * PADW, 3 * ch), jnp.bfloat16),
        ],
        compiler_params=pltpu.CompilerParams(vmem_limit_bytes=40 * 2**20),
        cost_estimate=pl.CostEstimate(
            flops=2 * HC * 9 * ch * ch * 2, bytes_accessed=4 * 10**6, transcendentals=0
        ),
        name=f"encode_frame{frame}",
    )(sc, mine, got, xl, xr, z, w1, w2)


def load_all(level, got, other, buf, sems, core):
    n_cs = len(level)
    copies = []
    for j in range(n_cs):
        up, down = j, 2 * n_cs + j
        copies.append(pltpu.make_async_copy(level[j], buf.at[n_cs + j], sems.at[n_cs + j]))
        copies.append(
            pltpu.make_async_copy(got[j], buf.at[jnp.where(core == 0, up, down)], sems.at[up])
        )
        copies.append(
            pltpu.make_async_copy(other[j], buf.at[jnp.where(core == 0, down, up)], sems.at[down])
        )
    for copy in copies:
        copy.start()
    for copy in copies:
        copy.wait()


def slot_steps(slot, n_cs, n_c, col):
    dr = slot // n_cs - 1
    j = slot % n_cs
    if n_c == 2:
        dc = jnp.where(j == 0, 0, 1 - 2 * col)
    else:
        dc = jnp.where(j == 0, 0, 2 * j - 3)
    return dr, dc


def query_kernel(n_c, n_cs, c2, sc, cand, count, q, ctg, *refs):
    level, got, other = refs[:n_cs], refs[n_cs : 2 * n_cs], refs[2 * n_cs : 3 * n_cs]
    flow, stats, dq, buf, sems, s_scr, m_run, n_run, r_run, c_run, d_scr, acc, q4 = refs[3 * n_cs :]
    core, col = sc[0], sc[2]
    slots = 3 * n_cs
    load_all(level, got, other, buf, sems, core)
    m_run[...] = jnp.full(m_run.shape, -jnp.inf, jnp.float32)
    for ref in (n_run, r_run, c_run):
        ref[...] = jnp.zeros(ref.shape, jnp.float32)
    acc[...] = jnp.zeros(acc.shape, jnp.float32)
    rb = 16
    lane = lax.broadcasted_iota(jnp.int32, (rb, 128), 1)
    lane_ok = lane % PADW < TILE
    lane_last = lane_ok & (lane < HC - 384)
    in_row = lane < HC - 384

    def listed(slot):
        dr, dc = slot_steps(slot, n_cs, n_c, col)
        code = 3 * (dr + 1) + dc + 1
        hit = jnp.int32(0)
        for s in range(9):
            hit = jnp.where((cand[s] == code) & (s < count[0]), 1, hit)
        return dr, dc, hit

    def half_of(dr, i):
        return jnp.where(dr == 0, core ^ i, jnp.where(dr < 0, i, 1 - i))

    def stats_step(slot, carry):
        dr, dc, hit = listed(slot)

        @pl.when(hit == 1)
        def _():
            for i in range(2):
                s_scr[slot, :, i * 512 : i * 512 + HC] = lax.dot_general(
                    q[...], buf[slot, i], (((1,), (1,)), ((), ())), preferred_element_type=jnp.float32
                )
            base = [
                (30 * dr + 15 * half_of(dr, i)).astype(jnp.float32) for i in range(2)
            ]
            col_base = (30 * dc).astype(jnp.float32)
            for g in range(HC // rb):
                rows = slice(g * rb, (g + 1) * rb)
                s = [s_scr[slot, rows, v * 128 : v * 128 + 128] for v in range(8)]
                top = jnp.maximum(
                    jnp.maximum(jnp.maximum(s[0], s[1]), s[2]),
                    jnp.maximum(jnp.maximum(s[4], s[5]), s[6]),
                )
                top = jnp.maximum(
                    jnp.where(lane_ok, top, -jnp.inf),
                    jnp.where(lane_last, jnp.maximum(s[3], s[7]), -jnp.inf),
                )
                best = jnp.max(top, axis=1, keepdims=True) * c2
                old = m_run[rows]
                new = jnp.maximum(old, best)
                m_run[rows] = new
                factor = jnp.exp2(old - new)
                e = [jnp.exp2(x * c2 - new) for x in s]
                total, weighted = [], []
                for i in range(2):
                    e0, e1, e2, e3 = e[4 * i : 4 * i + 4]
                    a3 = jnp.where(in_row, e3, 0.0)
                    a2 = a3 + e2
                    a1 = a2 + e1
                    total.append(a1 + e0)
                    weighted.append(4.0 * (a1 + a2 + a3))
                both = total[0] + total[1]
                n_run[rows] = n_run[rows] * factor + both
                r_run[rows] = r_run[rows] * factor + (
                    weighted[0] + weighted[1] + base[0] * total[0] + base[1] * total[1]
                )
                c_run[rows] = c_run[rows] * factor + col_base * both

        return carry

    lax.fori_loop(0, slots, stats_step, 0)

    wide = lax.broadcasted_iota(jnp.int32, (HC, 128), 1)
    ok = wide % PADW < TILE
    norm = n_run[...]
    n_sum = jnp.sum(jnp.where(ok, norm, 0.0), axis=1, keepdims=True)
    r_sum = jnp.sum(
        jnp.where(ok, r_run[...] + (wide // PADW).astype(jnp.float32) * norm, 0.0),
        axis=1,
        keepdims=True,
    )
    c_sum = jnp.sum(
        jnp.where(ok, c_run[...] + (wide % PADW).astype(jnp.float32) * norm, 0.0),
        axis=1,
        keepdims=True,
    )
    cell = lax.broadcasted_iota(jnp.int32, (HC, 128), 0)
    q_row = (cell // PADW + HALF * core).astype(jnp.float32)
    q_col = (cell % PADW).astype(jnp.float32)
    mean_r = r_sum / n_sum
    mean_c = c_sum / n_sum
    pulls = jnp.transpose(
        jnp.concatenate([ctg[...], jnp.zeros((120, HC), jnp.float32)], axis=0)
    )
    scale = 1.0 / (TILE * math.sqrt(q.shape[1]))
    cr = pulls[:, 0:1] * scale
    cc = pulls[:, 1:2] * scale
    shift = cr * mean_r + cc * mean_c
    level2 = jnp.where(q_col < TILE, m_run[...] + jnp.log2(n_sum), 1e30)
    q4[0] = level2
    q4[1] = jnp.broadcast_to(cr, (HC, 128))
    q4[2] = jnp.broadcast_to(cc, (HC, 128))
    q4[3] = jnp.broadcast_to(shift, (HC, 128))
    flags = jnp.zeros((HC, 128), jnp.float32)
    for slot in range(slots):
        dr, dc, hit = listed(slot)
        code = 3 * (dr + 1) + dc + 1
        flags = jnp.where((cell == code) & (hit == 1), 1.0, flags)
    packed = flags
    for k, value in enumerate(
        (level2, cr, cc, shift, flags, (mean_r - q_row) / TILE, (mean_c - q_col) / TILE)
    ):
        packed = jnp.where(wide == k, value, packed)
    turned = jnp.transpose(packed)
    stats[...] = turned[0:8]
    flow[...] = turned[5:7]

    def grad_step(slot, carry):
        dr, dc, hit = listed(slot)

        @pl.when(hit == 1)
        def _():
            lane_row = (lane // PADW).astype(jnp.float32)
            lane_col = (lane % PADW + 30 * dc).astype(jnp.float32)
            for i in range(2):
                base = lane_row + (30 * dr + 15 * half_of(dr, i)).astype(jnp.float32)
                for g in range(HC // rb):
                    rows = slice(g * rb, (g + 1) * rb)
                    lev, gr, gc, sh = (q4[k, rows] for k in range(4))
                    pull = gr * base + (gc * lane_col - sh)
                    for v in range(4):
                        s = s_scr[slot, rows, i * 512 + v * 128 : i * 512 + v * 128 + 128]
                        p = jnp.exp2(s * c2 - lev)
                        d = jnp.where(lane_last if v == 3 else lane_ok, p * pull, 0.0)
                        d_scr[rows, v * 128 : v * 128 + 128] = d.astype(jnp.bfloat16)
                        if v < 3:
                            pull = pull + 4.0 * gr
                acc[...] += jnp.dot(
                    d_scr[:, 0:HC], buf[slot, i], preferred_element_type=jnp.float32
                )

        return carry

    lax.fori_loop(0, slots, grad_step, 0)
    dq[...] = acc[...].reshape(HALF, PADW, acc.shape[1])[:, :TILE]


def query_side(n_c, sc, cand, count, q, ctg, level, got, other):
    n_cs = len(level)
    ch = q.shape[1]
    slots = 3 * n_cs
    c2 = math.log2(math.e) / math.sqrt(ch)
    pairs = slots * 2 * HC * HC
    return pl.pallas_call(
        functools.partial(query_kernel, n_c, n_cs, c2),
        out_shape=(
            jax.ShapeDtypeStruct((2, HC), jnp.float32),
            jax.ShapeDtypeStruct((8, HC), jnp.float32),
            jax.ShapeDtypeStruct((HALF, TILE, ch), jnp.float32),
        ),
        in_specs=[SMEM, SMEM, SMEM, VMEM, VMEM] + [ANY] * slots,
        out_specs=(VMEM, VMEM, VMEM),
        scratch_shapes=[
            pltpu.VMEM((slots, 2, HC, ch), jnp.bfloat16),
            pltpu.SemaphoreType.DMA((slots,)),
            pltpu.VMEM((slots, HC, 1024), jnp.float32),
            pltpu.VMEM((HC, 128), jnp.float32),
            pltpu.VMEM((HC, 128), jnp.float32),
            pltpu.VMEM((HC, 128), jnp.float32),
            pltpu.VMEM((HC, 128), jnp.float32),
            pltpu.VMEM((HC, 512), jnp.bfloat16),
            pltpu.VMEM((HC, ch), jnp.float32),
            pltpu.VMEM((4, HC, 128), jnp.float32),
        ],
        compiler_params=pltpu.CompilerParams(vmem_limit_bytes=48 * 2**20),
        cost_estimate=pl.CostEstimate(
            flops=4 * pairs * ch, bytes_accessed=6 * 10**6, transcendentals=2 * pairs
        ),
        name="query_side",
    )(sc, cand, count, q, ctg, *level, *got, *other)


def target_kernel(n_c, n_cs, c2, sc, tgt, *refs):
    slots = 3 * n_cs
    feats = refs[:slots]
    stats = refs[slots : 2 * slots]
    out, buf, sems, st, st_sems, s_scr, d_scr, v_scr, acc = refs[2 * slots :]
    core, col = sc[0], sc[2]
    load_all(feats[:n_cs], feats[n_cs : 2 * n_cs], feats[2 * n_cs :], buf, sems, core)
    load_all(stats[:n_cs], stats[n_cs : 2 * n_cs], stats[2 * n_cs :], st, st_sems, core)
    acc[...] = jnp.zeros(acc.shape, jnp.float32)

    def step(slot, carry):
        dr, dc = slot_steps(slot, n_cs, n_c, col)
        code = 8 - (3 * (dr + 1) + dc + 1)
        where_at = lax.broadcasted_iota(jnp.int32, (8, HC), 1)
        which = lax.broadcasted_iota(jnp.int32, (8, HC), 0)
        flag = jnp.sum(jnp.where((where_at == code) & (which == 4), st[slot, 0], 0.0))

        @pl.when(flag > 0.5)
        def _():
            col_t = (
                lax.broadcasted_iota(jnp.int32, (PADW, HC), 0) - 30 * dc
            ).astype(jnp.float32)
            for i in range(2):
                s_scr[...] = lax.dot_general(
                    tgt[...], buf[slot, i], (((1,), (1,)), ((), ())), preferred_element_type=jnp.float32
                )
                lev, gr, gc, sh = (st[slot, i, k : k + 1, :] for k in range(4))
                v_scr[...] = gc * col_t - sh
                for g in range(HALF):
                    rows = slice(g * PADW, (g + 1) * PADW)
                    row_t = (g + HALF * core - 30 * dr).astype(jnp.float32)
                    p = jnp.exp2(s_scr[rows] * c2 - lev)
                    d = p * (v_scr[...] + gr * row_t)
                    d_scr[rows] = d.astype(jnp.bfloat16)
                acc[...] += jnp.dot(d_scr[...], buf[slot, i], preferred_element_type=jnp.float32)

        return carry

    lax.fori_loop(0, slots, step, 0)
    out[...] = acc[...].reshape(HALF, PADW, acc.shape[1])[:, :TILE]


def target_side(n_c, sc, tgt, feats, stats):
    level, got, other = feats
    n_cs = len(level)
    ch = tgt.shape[1]
    slots = 3 * n_cs
    c2 = math.log2(math.e) / math.sqrt(ch)
    pairs = slots * 2 * HC * HC
    return pl.pallas_call(
        functools.partial(target_kernel, n_c, n_cs, c2),
        out_shape=jax.ShapeDtypeStruct((HALF, TILE, ch), jnp.float32),
        in_specs=[SMEM, VMEM] + [ANY] * (2 * slots),
        out_specs=VMEM,
        scratch_shapes=[
            pltpu.VMEM((slots, 2, HC, ch), jnp.bfloat16),
            pltpu.SemaphoreType.DMA((slots,)),
            pltpu.VMEM((slots, 2, 8, HC), jnp.float32),
            pltpu.SemaphoreType.DMA((slots,)),
            pltpu.VMEM((HC, HC), jnp.float32),
            pltpu.VMEM((HC, HC), jnp.bfloat16),
            pltpu.VMEM((PADW, HC), jnp.float32),
            pltpu.VMEM((HC, ch), jnp.float32),
        ],
        compiler_params=pltpu.CompilerParams(vmem_limit_bytes=48 * 2**20),
        cost_estimate=pl.CostEstimate(
            flops=4 * pairs * ch, bytes_accessed=6 * 10**6, transcendentals=pairs
        ),
        name="target_side",
    )(sc, tgt, *level, *got, *other, *stats[0], *stats[1], *stats[2])


def shards(frames, conv_first, conv_second, candidates, counts, cotangent):
    mine = frames[0]
    ch = mine.shape[2]
    n_r, n_c = lax.axis_size("rows"), lax.axis_size("cols")
    core, row, col = (lax.axis_index(a) for a in ("pair", "rows", "cols"))
    sc = jnp.stack([core, row, col]).astype(jnp.int32)
    w1 = conv_first.reshape(3, 3 * ch, ch)
    w2 = conv_second.reshape(3, 3 * ch, ch)
    got = partner(lax.dynamic_slice_in_dim(mine, (BODY - 4) * (1 - core), BODY, 0))
    own = lax.dynamic_slice_in_dim(mine, (BODY - 4) * core, BODY, 0)
    bodies = (own, got)
    if n_c == 2:
        edge = jnp.stack([jnp.where(col == 0, b[:, TILE - 2 :], b[:, :2]) for b in bodies])
        xl = xr = send(edge, lambda r, k, c: (r, 1 - k, c))
    else:
        xl = send(jnp.stack([b[:, TILE - 2 :] for b in bodies]), lambda r, k, c: (r, k + 1, c))
        xr = send(jnp.stack([b[:, :2] for b in bodies]), lambda r, k, c: (r, k - 1, c))
    lines = []
    for i, b in enumerate(bodies):
        at = HALF * core
        left = jnp.where(col > 0, lax.dynamic_slice_in_dim(xl[i], at, 2, 0), 0)
        right = jnp.where(col < n_c - 1, lax.dynamic_slice_in_dim(xr[i], at, 2, 0), 0)
        lines.append(
            jnp.concatenate([left, lax.dynamic_slice_in_dim(b, at, 2, 0), right], axis=1)
        )
    z = send(jnp.stack(lines), lambda r, k, c: (r - 1 + 2 * c, k, 1 - c))
    second = encode(1, n_r, n_c, sc, mine, got, xl, xr, z, w1, w2)
    first = encode(0, n_r, n_c, sc, mine, got, xl, xr, z, w1, w2)
    ctg = jnp.pad(cotangent, ((0, 6), (0, 0), (0, PADW - TILE))).reshape(8, HC)
    targets = gather_tiles(second)
    queries = gather_tiles(first)
    flow, stats, grad_first = query_side(
        n_c, sc, candidates.reshape(9), counts.reshape(1), first, ctg, *targets
    )
    grad_second = target_side(n_c, sc, second, queries, gather_tiles(stats))
    return flow.reshape(2, HALF, PADW)[:, :, :TILE], grad_first, grad_second


def solution(mesh):
    in_specs = (
        P("pair", ("groups", "rows"), "cols", None),
        P(),
        P(),
        P(("groups", "rows"), "cols", None),
        P(("groups", "rows"), "cols"),
        P(None, ("groups", "rows", "pair"), "cols"),
    )
    out_specs = (
        P(None, ("groups", "rows", "pair"), "cols"),
        P(("groups", "rows", "pair"), "cols", None),
        P(("groups", "rows", "pair"), "cols", None),
    )
    return jax.shard_map(shards, mesh=mesh, in_specs=in_specs, out_specs=out_specs, check_vma=False)
```

```python
import functools
import math

import jax
import jax.numpy as jnp
from jax import lax
from jax.experimental import pallas as pl
from jax.experimental.pallas import tpu as pltpu
from jax.sharding import PartitionSpec as P

TILE = 30
HALF = 15
PADW = 32
HC = HALF * PADW
BODY = HALF + 2
EXT = HALF + 4
HID = HALF + 2
AXES = ("rows", "cols", "pair")
VMEM = pl.BlockSpec(memory_space=pltpu.VMEM)
SMEM = pl.BlockSpec(memory_space=pltpu.SMEM)
RB = 16
ANY = pl.BlockSpec(memory_space=pl.ANY)


def send(value, step):
    n_r, n_c = lax.axis_size("rows"), lax.axis_size("cols")
    pairs = []
    for r in range(n_r):
        for k in range(n_c):
            for c in range(2):
                r2, k2, c2 = step(r, k, c)
                if 0 <= r2 < n_r and 0 <= k2 < n_c:
                    pairs.append(((r * n_c + k) * 2 + c, (r2 * n_c + k2) * 2 + c2))
    return lax.ppermute(value, AXES, pairs)


def partner(value):
    return send(value, lambda r, k, c: (r, k, 1 - c))


def updown(value):
    return send(value, lambda r, k, c: (r + 1 - 2 * c, k, c))


def sideways(value):
    if lax.axis_size("cols") == 2:
        return [send(value, lambda r, k, c: (r, 1 - k, c))]
    return [
        send(value, lambda r, k, c: (r, k + 1, c)),
        send(value, lambda r, k, c: (r, k - 1, c)),
    ]


def after(value, *others):
    return lax.optimization_barrier((value, others))[0]


def encode_kernel(frame, n_r, n_c, sc, mine, got, xl, xr, z, w1, w2, out, ext, xcat, hid, hcat):
    core, row, col = sc[0], sc[1], sc[2]
    first_row = 2 * (1 - core)
    use_own = core == frame
    own_rows = mine[pl.ds((BODY - 4) * core, BODY)]
    got_rows = got[pl.ds((BODY - 4) * core, BODY)]
    body = jnp.where(use_own, own_rows, got_rows).astype(jnp.float32)
    slot = jnp.where(use_own, 0, 1)
    left = jnp.where(col > 0, xl[slot].astype(jnp.float32), 0.0)
    right = jnp.where(col < n_c - 1, xr[slot].astype(jnp.float32), 0.0)
    ext[pl.ds(first_row, BODY), 2 : 2 + TILE] = body
    ext[pl.ds(first_row, BODY), 0:2] = left
    ext[pl.ds(first_row, BODY), 2 + TILE : 4 + TILE] = right
    ext[pl.ds(BODY * core, 2), 0 : 4 + TILE] = z[1 - slot].astype(jnp.float32)
    ch = body.shape[-1]
    for b in range(3):
        xcat[:, b * ch : (b + 1) * ch] = (
            ext[:, b : b + PADW].astype(jnp.bfloat16).reshape(EXT * PADW, ch)
        )
    acc = jnp.zeros((HID * PADW, ch), jnp.float32)
    for a in range(3):
        acc += jnp.dot(
            xcat[a * PADW : (a + HID) * PADW], w1[a], preferred_element_type=jnp.float32
        )
    hr = lax.broadcasted_iota(jnp.int32, (HID, PADW, ch), 0) + (row * TILE + core * HALF - 1)
    hc = lax.broadcasted_iota(jnp.int32, (HID, PADW, ch), 1) + (col * TILE - 1)
    inside = (hr >= 0) & (hr < n_r * TILE) & (hc >= 0) & (hc < n_c * TILE)
    hidden = jnp.where(inside, jnp.maximum(acc, 0.0).reshape(HID, PADW, ch), 0.0)
    hid[0 : HID * PADW] = hidden.reshape(HID * PADW, ch)
    hid[HID * PADW :] = jnp.zeros((8, ch), jnp.float32)
    for b in range(3):
        hcat[:, b * ch : (b + 1) * ch] = hid[b : b + HID * PADW].astype(jnp.bfloat16)
    acc2 = ext[2 : 2 + HALF, 2 : 2 + PADW].reshape(HC, ch)
    for a in range(3):
        acc2 += jnp.dot(hcat[a * PADW : a * PADW + HC], w2[a], preferred_element_type=jnp.float32)
    oc = lax.broadcasted_iota(jnp.int32, (HALF, PADW, ch), 1)
    out[...] = (
        jnp.where(oc < TILE, acc2.reshape(HALF, PADW, ch), 0.0)
        .astype(jnp.bfloat16)
        .reshape(HC, ch)
    )


def encode(frame, n_r, n_c, sc, mine, got, xl, xr, z, w1, w2):
    ch = mine.shape[-1]
    return pl.pallas_call(
        functools.partial(encode_kernel, frame, n_r, n_c),
        out_shape=jax.ShapeDtypeStruct((HC, ch), jnp.bfloat16),
        in_specs=[SMEM] + [VMEM] * 7,
        out_specs=VMEM,
        scratch_shapes=[
            pltpu.VMEM((EXT, 40, ch), jnp.float32),
            pltpu.VMEM((EXT * PADW, 3 * ch), jnp.bfloat16),
            pltpu.VMEM((HID * PADW + 8, ch), jnp.float32),
            pltpu.VMEM((HID * PADW, 3 * ch), jnp.bfloat16),
        ],
        compiler_params=pltpu.CompilerParams(vmem_limit_bytes=40 * 2**20),
        cost_estimate=pl.CostEstimate(
            flops=2 * HC * 9 * ch * ch * 2, bytes_accessed=4 * 10**6, transcendentals=0
        ),
        name=f"encode_frame{frame}",
    )(sc, mine, got, xl, xr, z, w1, w2)


def load_all(level, got, other, buf, sems, core):
    n_cs = len(level)
    for j in range(n_cs):
        up, down = j, 2 * n_cs + j
        first, last = jnp.where(core == 0, up, down), jnp.where(core == 0, down, up)
        pltpu.make_async_copy(level[j], buf.at[n_cs + j], sems.at[n_cs + j]).start()
        pltpu.make_async_copy(got[j], buf.at[first], sems.at[first]).start()
        pltpu.make_async_copy(other[j], buf.at[last], sems.at[last]).start()


def wait_for(tile, buf, sems, slot):
    pltpu.make_async_copy(tile, buf.at[slot], sems.at[slot]).wait()


def slot_steps(slot, n_cs, n_c, col):
    dr = slot // n_cs - 1
    j = slot % n_cs
    if n_c == 2:
        dc = jnp.where(j == 0, 0, 1 - 2 * col)
    else:
        dc = jnp.where(j == 0, 0, 2 * j - 3)
    return dr, dc


def listed(slot, n_cs, n_c, col, cand, count):
    dr, dc = slot_steps(slot, n_cs, n_c, col)
    code = 3 * (dr + 1) + dc + 1
    hit = jnp.int32(0)
    for s in range(9):
        hit = jnp.where((cand[s] == code) & (s < count[0]), 1, hit)
    return dr, dc, code, hit


def half_of(dr, i, core):
    return jnp.where(dr == 0, core ^ i, jnp.where(dr < 0, i, 1 - i))


def lanes(rows):
    lane = lax.broadcasted_iota(jnp.int32, (rows, 128), 1)
    return lane, lane % PADW < TILE, lane < HC - 384


def add_tile(c2, slot, dr, dc, core, q, buf, s_scr, state):
    for i in range(2):
        s_scr[:, i * 512 : i * 512 + HC] = lax.dot_general(
            q[...], buf[slot, i], (((1,), (1,)), ((), ())), preferred_element_type=jnp.float32
        )
    base = [(30 * dr + 15 * half_of(dr, i, core)).astype(jnp.float32) for i in range(2)]
    col_base = (30 * dc).astype(jnp.float32)
    lane, lane_ok, in_row = lanes(RB)
    for g in range(HC // RB):
        rows = slice(g * RB, (g + 1) * RB)
        s = [s_scr[rows, v * 128 : v * 128 + 128] for v in range(8)]
        top = jnp.maximum(
            jnp.maximum(jnp.maximum(s[0], s[1]), s[2]),
            jnp.maximum(jnp.maximum(s[4], s[5]), s[6]),
        )
        top = jnp.maximum(
            jnp.where(lane_ok, top, -jnp.inf),
            jnp.where(lane_ok & in_row, jnp.maximum(s[3], s[7]), -jnp.inf),
        )
        best = jnp.max(top, axis=1, keepdims=True) * c2
        old = state[0, rows]
        new = jnp.maximum(old, best)
        state[0, rows] = new
        factor = jnp.exp2(old - new)
        e = [jnp.exp2(x * c2 - new) for x in s]
        total, weighted = [], []
        for i in range(2):
            e0, e1, e2, e3 = e[4 * i : 4 * i + 4]
            a3 = jnp.where(in_row, e3, 0.0)
            a2 = a3 + e2
            a1 = a2 + e1
            total.append(a1 + e0)
            weighted.append(4.0 * (a1 + a2 + a3))
        both = total[0] + total[1]
        state[1, rows] = state[1, rows] * factor + both
        state[2, rows] = state[2, rows] * factor + (
            weighted[0] + weighted[1] + base[0] * total[0] + base[1] * total[1]
        )
        state[3, rows] = state[3, rows] * factor + col_base * both


def near_kernel(n_c, n_cs, c2, sc, cand, count, q, *refs):
    level, (state, buf, sems, s_scr) = refs[:n_cs], refs[n_cs:]
    core, col = sc[0], sc[2]
    for j in range(n_cs):
        pltpu.make_async_copy(level[j], buf.at[j], sems.at[j]).start()
    state[0] = jnp.full(state.shape[1:], -jnp.inf, jnp.float32)
    for k in range(1, 4):
        state[k] = jnp.zeros(state.shape[1:], jnp.float32)

    def step(j, carry):
        dr, dc, _, hit = listed(n_cs + j, n_cs, n_c, col, cand, count)
        wait_for(level[0], buf, sems, j)

        @pl.when(hit == 1)
        def _():
            add_tile(c2, j, dr, dc, core, q, buf, s_scr, state)

        return carry

    lax.fori_loop(0, n_cs, step, 0)


def far_kernel(n_c, n_cs, c2, sc, cand, count, q, ctg, begun, *refs):
    got, other = refs[:n_cs], refs[n_cs : 2 * n_cs]
    flow, stats, packed_out, buf, sems, s_scr, state = refs[2 * n_cs :]
    core, col = sc[0], sc[2]
    for j in range(n_cs):
        first, last = jnp.where(core == 0, j, n_cs + j), jnp.where(core == 0, n_cs + j, j)
        pltpu.make_async_copy(got[j], buf.at[first], sems.at[first]).start()
        pltpu.make_async_copy(other[j], buf.at[last], sems.at[last]).start()
    state[...] = begun[...]

    def step(j, carry):
        slot = jnp.where(j < n_cs, j, n_cs + j)
        dr, dc, _, hit = listed(slot, n_cs, n_c, col, cand, count)
        wait_for(got[0], buf, sems, j)

        @pl.when(hit == 1)
        def _():
            add_tile(c2, j, dr, dc, core, q, buf, s_scr, state)

        return carry

    lax.fori_loop(0, 2 * n_cs, step, 0)
    wide, ok, _ = lanes(HC)
    norm = state[1]
    n_sum = jnp.sum(jnp.where(ok, norm, 0.0), axis=1, keepdims=True)
    r_sum = jnp.sum(
        jnp.where(ok, state[2] + (wide // PADW).astype(jnp.float32) * norm, 0.0),
        axis=1,
        keepdims=True,
    )
    c_sum = jnp.sum(
        jnp.where(ok, state[3] + (wide % PADW).astype(jnp.float32) * norm, 0.0),
        axis=1,
        keepdims=True,
    )
    cell = lax.broadcasted_iota(jnp.int32, (HC, 128), 0)
    q_row = (cell // PADW + HALF * core).astype(jnp.float32)
    q_col = (cell % PADW).astype(jnp.float32)
    mean_r = r_sum / n_sum
    mean_c = c_sum / n_sum
    pulls = jnp.transpose(
        jnp.concatenate([ctg[...], jnp.zeros((120, HC), jnp.float32)], axis=0)
    )
    scale = 1.0 / (TILE * math.sqrt(q.shape[1]))
    cr = pulls[:, 0:1] * scale
    cc = pulls[:, 1:2] * scale
    shift = cr * mean_r + cc * mean_c
    level2 = jnp.where(q_col < TILE, state[0] + jnp.log2(n_sum), 1e30)
    flags = jnp.zeros((HC, 128), jnp.float32)
    for slot in range(3 * n_cs):
        _, _, code, hit = listed(slot, n_cs, n_c, col, cand, count)
        flags = jnp.where((cell == code) & (hit == 1), 1.0, flags)
    packed = flags
    for k, value in enumerate(
        (level2, cr, cc, shift, flags, (mean_r - q_row) / TILE, (mean_c - q_col) / TILE)
    ):
        packed = jnp.where(wide == k, value, packed)
    packed_out[...] = packed
    turned = jnp.transpose(packed)
    stats[...] = turned[0:8]
    flow[...] = turned[5:7]


def grad_kernel(n_c, n_cs, c2, sc, cand, count, q, packed, *refs):
    level, got, other = refs[:n_cs], refs[n_cs : 2 * n_cs], refs[2 * n_cs : 3 * n_cs]
    out, buf, sems, s_scr, d_scr, acc, q4 = refs[3 * n_cs :]
    core, col = sc[0], sc[2]
    load_all(level, got, other, buf, sems, core)
    acc[...] = jnp.zeros(acc.shape, jnp.float32)
    for k in range(4):
        q4[k] = jnp.broadcast_to(packed[:, k : k + 1], (HC, 128))
    lane, lane_ok, in_row = lanes(RB)

    def step(slot, carry):
        dr, dc, _, hit = listed(slot, n_cs, n_c, col, cand, count)
        wait_for(level[0], buf, sems, slot)

        @pl.when(hit == 1)
        def _():
            lane_row = (lane // PADW).astype(jnp.float32)
            lane_col = (lane % PADW + 30 * dc).astype(jnp.float32)
            for i in range(2):
                s_scr[:, 0:HC] = lax.dot_general(
                    q[...], buf[slot, i], (((1,), (1,)), ((), ())), preferred_element_type=jnp.float32
                )
                base = lane_row + (30 * dr + 15 * half_of(dr, i, core)).astype(jnp.float32)
                for g in range(HC // RB):
                    rows = slice(g * RB, (g + 1) * RB)
                    lev, gr, gc, sh = (q4[k, rows] for k in range(4))
                    pull = gr * base + (gc * lane_col - sh)
                    for v in range(4):
                        p = jnp.exp2(s_scr[rows, v * 128 : v * 128 + 128] * c2 - lev)
                        d = jnp.where(lane_ok & in_row if v == 3 else lane_ok, p * pull, 0.0)
                        d_scr[rows, v * 128 : v * 128 + 128] = d.astype(jnp.bfloat16)
                        if v < 3:
                            pull = pull + 4.0 * gr
                acc[...] += jnp.dot(
                    d_scr[:, 0:HC], buf[slot, i], preferred_element_type=jnp.float32
                )

        return carry

    lax.fori_loop(0, 3 * n_cs, step, 0)
    out[...] = acc[...].reshape(HALF, PADW, acc.shape[1])[:, :TILE]


def query_near(n_c, sc, cand, count, q, level):
    n_cs, ch = len(level), q.shape[1]
    pairs = n_cs * 2 * HC * HC
    return pl.pallas_call(
        functools.partial(near_kernel, n_c, n_cs, math.log2(math.e) / math.sqrt(ch)),
        out_shape=jax.ShapeDtypeStruct((4, HC, 128), jnp.float32),
        in_specs=[SMEM, SMEM, SMEM, VMEM] + [ANY] * n_cs,
        out_specs=VMEM,
        scratch_shapes=[
            pltpu.VMEM((n_cs, 2, HC, ch), jnp.bfloat16),
            pltpu.SemaphoreType.DMA((n_cs,)),
            pltpu.VMEM((HC, 1024), jnp.float32),
        ],
        compiler_params=pltpu.CompilerParams(vmem_limit_bytes=32 * 2**20),
        cost_estimate=pl.CostEstimate(
            flops=2 * pairs * ch, bytes_accessed=6 * 10**6, transcendentals=pairs
        ),
        name="query_near",
    )(sc, cand, count, q, *level)


def query_far(n_c, sc, cand, count, q, ctg, begun, got, other):
    n_cs, ch = len(got), q.shape[1]
    pairs = 2 * n_cs * 2 * HC * HC
    return pl.pallas_call(
        functools.partial(far_kernel, n_c, n_cs, math.log2(math.e) / math.sqrt(ch)),
        out_shape=(
            jax.ShapeDtypeStruct((2, HC), jnp.float32),
            jax.ShapeDtypeStruct((8, HC), jnp.float32),
            jax.ShapeDtypeStruct((HC, 128), jnp.float32),
        ),
        in_specs=[SMEM, SMEM, SMEM, VMEM, VMEM, VMEM] + [ANY] * (2 * n_cs),
        out_specs=(VMEM, VMEM, VMEM),
        scratch_shapes=[
            pltpu.VMEM((2 * n_cs, 2, HC, ch), jnp.bfloat16),
            pltpu.SemaphoreType.DMA((2 * n_cs,)),
            pltpu.VMEM((HC, 1024), jnp.float32),
            pltpu.VMEM((4, HC, 128), jnp.float32),
        ],
        compiler_params=pltpu.CompilerParams(vmem_limit_bytes=32 * 2**20),
        cost_estimate=pl.CostEstimate(
            flops=2 * pairs * ch, bytes_accessed=8 * 10**6, transcendentals=pairs
        ),
        name="query_far",
    )(sc, cand, count, q, ctg, begun, *got, *other)


def query_grad(n_c, sc, cand, count, q, packed, level, got, other):
    n_cs, ch = len(level), q.shape[1]
    slots = 3 * n_cs
    pairs = slots * 2 * HC * HC
    return pl.pallas_call(
        functools.partial(grad_kernel, n_c, n_cs, math.log2(math.e) / math.sqrt(ch)),
        out_shape=jax.ShapeDtypeStruct((HALF, TILE, ch), jnp.float32),
        in_specs=[SMEM, SMEM, SMEM, VMEM, VMEM] + [ANY] * slots,
        out_specs=VMEM,
        scratch_shapes=[
            pltpu.VMEM((slots, 2, HC, ch), jnp.bfloat16),
            pltpu.SemaphoreType.DMA((slots,)),
            pltpu.VMEM((HC, 512), jnp.float32),
            pltpu.VMEM((HC, 512), jnp.bfloat16),
            pltpu.VMEM((HC, ch), jnp.float32),
            pltpu.VMEM((4, HC, 128), jnp.float32),
        ],
        compiler_params=pltpu.CompilerParams(vmem_limit_bytes=32 * 2**20),
        cost_estimate=pl.CostEstimate(
            flops=4 * pairs * ch, bytes_accessed=8 * 10**6, transcendentals=2 * pairs
        ),
        name="query_grad",
    )(sc, cand, count, q, packed, *level, *got, *other)


def target_kernel(n_c, n_cs, c2, sc, tgt, *refs):
    slots = 3 * n_cs
    feats = refs[:slots]
    stats = refs[slots : 2 * slots]
    out, buf, sems, st, st_sems, s_scr, d_scr, v_scr, acc = refs[2 * slots :]
    core, col = sc[0], sc[2]
    load_all(feats[:n_cs], feats[n_cs : 2 * n_cs], feats[2 * n_cs :], buf, sems, core)
    load_all(stats[:n_cs], stats[n_cs : 2 * n_cs], stats[2 * n_cs :], st, st_sems, core)
    acc[...] = jnp.zeros(acc.shape, jnp.float32)

    def step(slot, carry):
        dr, dc = slot_steps(slot, n_cs, n_c, col)
        wait_for(feats[0], buf, sems, slot)
        wait_for(stats[0], st, st_sems, slot)
        code = 8 - (3 * (dr + 1) + dc + 1)
        where_at = lax.broadcasted_iota(jnp.int32, (8, HC), 1)
        which = lax.broadcasted_iota(jnp.int32, (8, HC), 0)
        flag = jnp.sum(jnp.where((where_at == code) & (which == 4), st[slot, 0], 0.0))

        @pl.when(flag > 0.5)
        def _():
            col_t = (
                lax.broadcasted_iota(jnp.int32, (PADW, HC), 0) - 30 * dc
            ).astype(jnp.float32)
            for i in range(2):
                s_scr[...] = lax.dot_general(
                    tgt[...], buf[slot, i], (((1,), (1,)), ((), ())), preferred_element_type=jnp.float32
                )
                lev, gr, gc, sh = (st[slot, i, k : k + 1, :] for k in range(4))
                v_scr[...] = gc * col_t - sh
                for g in range(HALF):
                    rows = slice(g * PADW, (g + 1) * PADW)
                    row_t = (g + HALF * core - 30 * dr).astype(jnp.float32)
                    p = jnp.exp2(s_scr[rows] * c2 - lev)
                    d = p * (v_scr[...] + gr * row_t)
                    d_scr[rows] = d.astype(jnp.bfloat16)
                acc[...] += jnp.dot(d_scr[...], buf[slot, i], preferred_element_type=jnp.float32)

        return carry

    lax.fori_loop(0, slots, step, 0)
    out[...] = acc[...].reshape(HALF, PADW, acc.shape[1])[:, :TILE]


def target_side(n_c, sc, tgt, feats, stats):
    level, got, other = feats
    n_cs = len(level)
    ch = tgt.shape[1]
    slots = 3 * n_cs
    c2 = math.log2(math.e) / math.sqrt(ch)
    pairs = slots * 2 * HC * HC
    return pl.pallas_call(
        functools.partial(target_kernel, n_c, n_cs, c2),
        out_shape=jax.ShapeDtypeStruct((HALF, TILE, ch), jnp.float32),
        in_specs=[SMEM, VMEM] + [ANY] * (2 * slots),
        out_specs=VMEM,
        scratch_shapes=[
            pltpu.VMEM((slots, 2, HC, ch), jnp.bfloat16),
            pltpu.SemaphoreType.DMA((slots,)),
            pltpu.VMEM((slots, 2, 8, HC), jnp.float32),
            pltpu.SemaphoreType.DMA((slots,)),
            pltpu.VMEM((HC, HC), jnp.float32),
            pltpu.VMEM((HC, HC), jnp.bfloat16),
            pltpu.VMEM((PADW, HC), jnp.float32),
            pltpu.VMEM((HC, ch), jnp.float32),
        ],
        compiler_params=pltpu.CompilerParams(vmem_limit_bytes=48 * 2**20),
        cost_estimate=pl.CostEstimate(
            flops=4 * pairs * ch, bytes_accessed=6 * 10**6, transcendentals=pairs
        ),
        name="target_side",
    )(sc, tgt, *level, *got, *other, *stats[0], *stats[1], *stats[2])


def shards(frames, conv_first, conv_second, candidates, counts, cotangent):
    mine = frames[0]
    ch = mine.shape[2]
    n_r, n_c = lax.axis_size("rows"), lax.axis_size("cols")
    core, row, col = (lax.axis_index(a) for a in ("pair", "rows", "cols"))
    sc = jnp.stack([core, row, col]).astype(jnp.int32)
    w1 = conv_first.reshape(3, 3 * ch, ch)
    w2 = conv_second.reshape(3, 3 * ch, ch)
    got_all = partner(mine)
    own = lax.dynamic_slice_in_dim(mine, (BODY - 4) * core, BODY, 0)
    got = lax.dynamic_slice_in_dim(got_all, (BODY - 4) * core, BODY, 0)
    bodies = (own, got)
    if n_c == 2:
        edge = jnp.stack([jnp.where(col == 0, b[:, TILE - 2 :], b[:, :2]) for b in bodies])
        xl = xr = send(edge, lambda r, k, c: (r, 1 - k, c))
    else:
        xl = send(jnp.stack([b[:, TILE - 2 :] for b in bodies]), lambda r, k, c: (r, k + 1, c))
        xr = send(jnp.stack([b[:, :2] for b in bodies]), lambda r, k, c: (r, k - 1, c))
    lines = []
    for i, b in enumerate(bodies):
        at = HALF * core
        left = jnp.where(col > 0, lax.dynamic_slice_in_dim(xl[i], at, 2, 0), 0)
        right = jnp.where(col < n_c - 1, lax.dynamic_slice_in_dim(xr[i], at, 2, 0), 0)
        lines.append(
            jnp.concatenate([left, lax.dynamic_slice_in_dim(b, at, 2, 0), right], axis=1)
        )
    z = send(jnp.stack(lines), lambda r, k, c: (r - 1 + 2 * c, k, 1 - c))
    cand, count = candidates.reshape(9), counts.reshape(1)
    ctg = jnp.pad(cotangent, ((0, 6), (0, 0), (0, PADW - TILE))).reshape(8, HC)
    second = encode(1, n_r, n_c, sc, mine, got_all, xl, xr, z, w1, w2)
    side = sideways(second)
    own_tile = jnp.stack([second, partner(second)])
    own_got = updown(own_tile)
    first = encode(0, n_r, n_c, sc, after(mine, own_tile), got_all, xl, xr, z, w1, w2)
    side = [after(x, first) for x in side]
    level = [own_tile] + [jnp.stack([x, partner(x)]) for x in side]
    got = [own_got] + [updown(t) for t in level[1:]]
    q_side = sideways(after(first, level))
    q_own = jnp.stack([first, partner(first)])
    begun = query_near(n_c, sc, cand, count, after(first, q_own), level)
    got = list(after(tuple(got), begun))
    other = [partner(t) for t in got]
    q_level = [q_own] + [jnp.stack([x, partner(x)]) for x in after(tuple(q_side), got)]
    q_got = [updown(t) for t in q_level]
    flow, stats, packed = query_far(n_c, sc, cand, count, first, ctg, begun, got, other)
    st_level = [jnp.stack([stats, partner(stats)])]
    st_level += [jnp.stack([x, partner(x)]) for x in sideways(stats)]
    st_got = [updown(t) for t in st_level]
    grad_first = query_grad(n_c, sc, cand, count, first, packed, level, got, other)
    q_got = list(after(tuple(q_got), packed))
    q_other = [partner(t) for t in q_got]
    st_got = list(after(tuple(st_got), grad_first))
    st_other = [partner(t) for t in st_got]
    grad_second = target_side(
        n_c, sc, second, (q_level, q_got, q_other), (st_level, st_got, st_other)
    )
    return flow.reshape(2, HALF, PADW)[:, :, :TILE], grad_first, grad_second


def solution(mesh):
    in_specs = (
        P("pair", ("groups", "rows"), "cols", None),
        P(),
        P(),
        P(("groups", "rows"), "cols", None),
        P(("groups", "rows"), "cols"),
        P(None, ("groups", "rows", "pair"), "cols"),
    )
    out_specs = (
        P(None, ("groups", "rows", "pair"), "cols"),
        P(("groups", "rows", "pair"), "cols", None),
        P(("groups", "rows", "pair"), "cols", None),
    )
    return jax.shard_map(shards, mesh=mesh, in_specs=in_specs, out_specs=out_specs, check_vma=False)
```

```python
import functools
import math

import jax
import jax.numpy as jnp
from jax import lax
from jax.experimental import pallas as pl
from jax.experimental.pallas import tpu as pltpu
from jax.sharding import PartitionSpec as P

TILE = 30
HALF = 15
PADW = 32
HC = HALF * PADW
BODY = HALF + 2
EXT = HALF + 4
HID = HALF + 2
AXES = ("rows", "cols", "pair")
VMEM = pl.BlockSpec(memory_space=pltpu.VMEM)
SMEM = pl.BlockSpec(memory_space=pltpu.SMEM)
RB = 16
COST = pl.CostEstimate(flops=10**6, bytes_accessed=10**4, transcendentals=0)
ANY = pl.BlockSpec(memory_space=pl.ANY)


def send(value, step):
    n_r, n_c = lax.axis_size("rows"), lax.axis_size("cols")
    pairs = []
    for r in range(n_r):
        for k in range(n_c):
            for c in range(2):
                r2, k2, c2 = step(r, k, c)
                if 0 <= r2 < n_r and 0 <= k2 < n_c:
                    pairs.append(((r * n_c + k) * 2 + c, (r2 * n_c + k2) * 2 + c2))
    return lax.ppermute(value, AXES, pairs)


def partner(value):
    return send(value, lambda r, k, c: (r, k, 1 - c))


def updown(value):
    return send(value, lambda r, k, c: (r + 1 - 2 * c, k, c))


def sideways(value):
    if lax.axis_size("cols") == 2:
        return [send(value, lambda r, k, c: (r, 1 - k, c))]
    return [
        send(value, lambda r, k, c: (r, k + 1, c)),
        send(value, lambda r, k, c: (r, k - 1, c)),
    ]


def after(value, *others):
    return lax.optimization_barrier((value, others))[0]


def encode_kernel(frame, n_r, n_c, sc, mine, got, xl, xr, z, w1, w2, out, ext, xcat, hid, hcat):
    core, row, col = sc[0], sc[1], sc[2]
    first_row = 2 * (1 - core)
    use_own = core == frame
    own_rows = mine[pl.ds((BODY - 4) * core, BODY)]
    got_rows = got[pl.ds((BODY - 4) * core, BODY)]
    body = jnp.where(use_own, own_rows, got_rows).astype(jnp.float32)
    slot = jnp.where(use_own, 0, 1)
    rows = pl.ds((BODY - 4) * core, BODY)
    left = jnp.where(col > 0, xl[slot, rows].astype(jnp.float32), 0.0)
    right = jnp.where(col < n_c - 1, xr[slot, rows].astype(jnp.float32), 0.0)
    ext[pl.ds(first_row, BODY), 2 : 2 + TILE] = body
    ext[pl.ds(first_row, BODY), 0:2] = left
    ext[pl.ds(first_row, BODY), 2 + TILE : 4 + TILE] = right
    ext[pl.ds(BODY * core, 2), 0 : 4 + TILE] = z[1 - slot].astype(jnp.float32)
    ch = body.shape[-1]
    for b in range(3):
        xcat[:, b * ch : (b + 1) * ch] = (
            ext[:, b : b + PADW].astype(jnp.bfloat16).reshape(EXT * PADW, ch)
        )
    acc = jnp.zeros((HID * PADW, ch), jnp.float32)
    for a in range(3):
        acc += jnp.dot(
            xcat[a * PADW : (a + HID) * PADW], w1[a], preferred_element_type=jnp.float32
        )
    hr = lax.broadcasted_iota(jnp.int32, (HID, PADW, ch), 0) + (row * TILE + core * HALF - 1)
    hc = lax.broadcasted_iota(jnp.int32, (HID, PADW, ch), 1) + (col * TILE - 1)
    inside = (hr >= 0) & (hr < n_r * TILE) & (hc >= 0) & (hc < n_c * TILE)
    hidden = jnp.where(inside, jnp.maximum(acc, 0.0).reshape(HID, PADW, ch), 0.0)
    hid[0 : HID * PADW] = hidden.reshape(HID * PADW, ch)
    hid[HID * PADW :] = jnp.zeros((8, ch), jnp.float32)
    for b in range(3):
        hcat[:, b * ch : (b + 1) * ch] = hid[b : b + HID * PADW].astype(jnp.bfloat16)
    acc2 = ext[2 : 2 + HALF, 2 : 2 + PADW].reshape(HC, ch)
    for a in range(3):
        acc2 += jnp.dot(hcat[a * PADW : a * PADW + HC], w2[a], preferred_element_type=jnp.float32)
    oc = lax.broadcasted_iota(jnp.int32, (HALF, PADW, ch), 1)
    out[...] = (
        jnp.where(oc < TILE, acc2.reshape(HALF, PADW, ch), 0.0)
        .astype(jnp.bfloat16)
        .reshape(HC, ch)
    )


def fetch_kernel(a, b, a_out, b_out, sems):
    copies = [
        pltpu.make_async_copy(a, a_out, sems.at[0]),
        pltpu.make_async_copy(b, b_out, sems.at[1]),
    ]
    for copy in copies:
        copy.start()
    for copy in copies:
        copy.wait()


def fetch(a, b):
    return pl.pallas_call(
        fetch_kernel,
        out_shape=[pltpu.VMEM(x.shape, x.dtype) for x in (a, b)],
        in_specs=[ANY, ANY],
        out_specs=[VMEM, VMEM],
        scratch_shapes=[pltpu.SemaphoreType.DMA((2,))],
        compiler_params=pltpu.CompilerParams(vmem_limit_bytes=2**20),
        cost_estimate=COST,
        name="fetch_weights",
    )(a, b)


def encode(frame, n_r, n_c, sc, mine, got, xl, xr, z, w1, w2):
    ch = mine.shape[-1]
    return pl.pallas_call(
        functools.partial(encode_kernel, frame, n_r, n_c),
        out_shape=jax.ShapeDtypeStruct((HC, ch), jnp.bfloat16),
        in_specs=[SMEM] + [VMEM] * 7,
        out_specs=VMEM,
        scratch_shapes=[
            pltpu.VMEM((EXT, 40, ch), jnp.float32),
            pltpu.VMEM((EXT * PADW, 3 * ch), jnp.bfloat16),
            pltpu.VMEM((HID * PADW + 8, ch), jnp.float32),
            pltpu.VMEM((HID * PADW, 3 * ch), jnp.bfloat16),
        ],
        compiler_params=pltpu.CompilerParams(vmem_limit_bytes=12 * 2**20),
        cost_estimate=COST,
        name=f"encode_frame{frame}",
    )(sc, mine, got, xl, xr, z, w1, w2)


def load_rows(level, got, other, buf, sems, core):
    first = 2 * core
    pltpu.make_async_copy(level, buf.at[1], sems.at[1]).start()
    pltpu.make_async_copy(got, buf.at[first], sems.at[first]).start()
    pltpu.make_async_copy(other, buf.at[2 - first], sems.at[2 - first]).start()


def load_far(got, other, buf, sems, core):
    n_cs = len(got)
    for j in range(n_cs):
        first, last = jnp.where(core == 0, j, n_cs + j), jnp.where(core == 0, n_cs + j, j)
        pltpu.make_async_copy(got[j], buf.at[first], sems.at[first]).start()
        pltpu.make_async_copy(other[j], buf.at[last], sems.at[last]).start()


def wait_for(tile, buf, sems, slot):
    pltpu.make_async_copy(tile, buf.at[slot], sems.at[slot]).wait()


def slot_steps(slot, n_cs, n_c, col):
    dr = slot // n_cs - 1
    j = slot % n_cs
    if n_c == 2:
        dc = jnp.where(j == 0, 0, 1 - 2 * col)
    else:
        dc = jnp.where(j == 0, 0, 2 * j - 3)
    return dr, dc


def listed(slot, n_cs, n_c, col, cand, count):
    dr, dc = slot_steps(slot, n_cs, n_c, col)
    code = 3 * (dr + 1) + dc + 1
    hit = jnp.int32(0)
    for s in range(9):
        hit = jnp.where((cand[s] == code) & (s < count[0]), 1, hit)
    return dr, dc, code, hit


def half_of(dr, i, core):
    return jnp.where(dr == 0, core ^ i, jnp.where(dr < 0, i, 1 - i))


def lanes(rows):
    lane = lax.broadcasted_iota(jnp.int32, (rows, 128), 1)
    return lane, lane % PADW < TILE, lane < HC - 384


def add_tile(c2, slot, dr, dc, core, q, buf, s_scr, state):
    for i in range(2):
        s_scr[:, i * 512 : i * 512 + HC] = lax.dot_general(
            q[...], buf[slot, i], (((1,), (1,)), ((), ())), preferred_element_type=jnp.float32
        )
    base = [(30 * dr + 15 * half_of(dr, i, core)).astype(jnp.float32) for i in range(2)]
    col_base = (30 * dc).astype(jnp.float32)
    lane, lane_ok, in_row = lanes(RB)
    for g in range(HC // RB):
        rows = slice(g * RB, (g + 1) * RB)
        s = [s_scr[rows, v * 128 : v * 128 + 128] for v in range(8)]
        top = jnp.maximum(
            jnp.maximum(jnp.maximum(s[0], s[1]), s[2]),
            jnp.maximum(jnp.maximum(s[4], s[5]), s[6]),
        )
        top = jnp.maximum(
            jnp.where(lane_ok, top, -jnp.inf),
            jnp.where(lane_ok & in_row, jnp.maximum(s[3], s[7]), -jnp.inf),
        )
        best = jnp.max(top, axis=1, keepdims=True) * c2
        old = state[0, rows]
        new = jnp.maximum(old, best)
        state[0, rows] = new
        factor = jnp.exp2(old - new)
        e = [jnp.exp2(x * c2 - new) for x in s]
        total, weighted = [], []
        for i in range(2):
            e0, e1, e2, e3 = e[4 * i : 4 * i + 4]
            a3 = jnp.where(in_row, e3, 0.0)
            a2 = a3 + e2
            a1 = a2 + e1
            total.append(a1 + e0)
            weighted.append(4.0 * (a1 + a2 + a3))
        both = total[0] + total[1]
        state[1, rows] = state[1, rows] * factor + both
        state[2, rows] = state[2, rows] * factor + (
            weighted[0] + weighted[1] + base[0] * total[0] + base[1] * total[1]
        )
        state[3, rows] = state[3, rows] * factor + col_base * both


def near_kernel(n_c, n_cs, c2, sc, cand, count, q, *refs):
    level, (state, buf, sems, s_scr) = refs[:n_cs], refs[n_cs:]
    core, col = sc[0], sc[2]
    for j in range(n_cs):
        pltpu.make_async_copy(level[j], buf.at[j], sems.at[j]).start()
    state[0] = jnp.full(state.shape[1:], -jnp.inf, jnp.float32)
    for k in range(1, 4):
        state[k] = jnp.zeros(state.shape[1:], jnp.float32)

    def step(j, carry):
        dr, dc, _, hit = listed(n_cs + j, n_cs, n_c, col, cand, count)
        wait_for(level[0], buf, sems, j)

        @pl.when(hit == 1)
        def _():
            add_tile(c2, j, dr, dc, core, q, buf, s_scr, state)

        return carry

    lax.fori_loop(0, n_cs, step, 0)


def far_kernel(n_c, n_cs, c2, sc, cand, count, q, ctg, begun, *refs):
    got, other = refs[:n_cs], refs[n_cs : 2 * n_cs]
    flow, stats, packed_out, buf, sems, s_scr, state = refs[2 * n_cs :]
    core, col = sc[0], sc[2]
    load_far(got, other, buf, sems, core)
    state[...] = begun[...]

    def step(j, carry):
        slot = jnp.where(j < n_cs, j, n_cs + j)
        dr, dc, _, hit = listed(slot, n_cs, n_c, col, cand, count)
        wait_for(got[0], buf, sems, j)

        @pl.when(hit == 1)
        def _():
            add_tile(c2, j, dr, dc, core, q, buf, s_scr, state)

        return carry

    lax.fori_loop(0, 2 * n_cs, step, 0)
    wide, ok, _ = lanes(HC)
    norm = state[1]
    n_sum = jnp.sum(jnp.where(ok, norm, 0.0), axis=1, keepdims=True)
    r_sum = jnp.sum(
        jnp.where(ok, state[2] + (wide // PADW).astype(jnp.float32) * norm, 0.0),
        axis=1,
        keepdims=True,
    )
    c_sum = jnp.sum(
        jnp.where(ok, state[3] + (wide % PADW).astype(jnp.float32) * norm, 0.0),
        axis=1,
        keepdims=True,
    )
    cell = lax.broadcasted_iota(jnp.int32, (HC, 128), 0)
    q_row = (cell // PADW + HALF * core).astype(jnp.float32)
    q_col = (cell % PADW).astype(jnp.float32)
    mean_r = r_sum / n_sum
    mean_c = c_sum / n_sum
    pulls = jnp.transpose(
        jnp.concatenate([ctg[...], jnp.zeros((120, HC), jnp.float32)], axis=0)
    )
    scale = 1.0 / (TILE * math.sqrt(q.shape[1]))
    cr = pulls[:, 0:1] * scale
    cc = pulls[:, 1:2] * scale
    shift = cr * mean_r + cc * mean_c
    level2 = jnp.where(q_col < TILE, state[0] + jnp.log2(n_sum), 1e30)
    flags = jnp.zeros((HC, 128), jnp.float32)
    for slot in range(3 * n_cs):
        _, _, code, hit = listed(slot, n_cs, n_c, col, cand, count)
        flags = jnp.where((cell == code) & (hit == 1), 1.0, flags)
    packed = flags
    for k, value in enumerate(
        (level2, cr, cc, shift, flags, (mean_r - q_row) / TILE, (mean_c - q_col) / TILE)
    ):
        packed = jnp.where(wide == k, value, packed)
    packed_out[...] = packed
    turned = jnp.transpose(packed)
    stats[...] = turned[0:8]
    flow[...] = turned[5:7]


def spread(packed, q4):
    for k in range(4):
        q4[k] = jnp.broadcast_to(packed[:, k : k + 1], (HC, 128))


def grad_tile(c2, slot, dr, dc, core, q, buf, s_scr, d_scr, acc, q4):
    lane, lane_ok, in_row = lanes(RB)
    lane_row = (lane // PADW).astype(jnp.float32)
    lane_col = (lane % PADW + 30 * dc).astype(jnp.float32)
    for i in range(2):
        s_scr[:, 0:HC] = lax.dot_general(
            q[...], buf[slot, i], (((1,), (1,)), ((), ())), preferred_element_type=jnp.float32
        )
        base = lane_row + (30 * dr + 15 * half_of(dr, i, core)).astype(jnp.float32)
        for g in range(HC // RB):
            rows = slice(g * RB, (g + 1) * RB)
            lev, gr, gc, sh = (q4[k, rows] for k in range(4))
            pull = gr * base + (gc * lane_col - sh)
            for v in range(4):
                p = jnp.exp2(s_scr[rows, v * 128 : v * 128 + 128] * c2 - lev)
                d = jnp.where(lane_ok & in_row if v == 3 else lane_ok, p * pull, 0.0)
                d_scr[rows, v * 128 : v * 128 + 128] = d.astype(jnp.bfloat16)
                if v < 3:
                    pull = pull + 4.0 * gr
        acc[...] += jnp.dot(d_scr[:, 0:HC], buf[slot, i], preferred_element_type=jnp.float32)


def grad_near_kernel(n_c, n_cs, c2, sc, cand, count, q, packed, *refs):
    level, (acc, buf, sems, s_scr, d_scr, q4) = refs[:n_cs], refs[n_cs:]
    core, col = sc[0], sc[2]
    for j in range(n_cs):
        pltpu.make_async_copy(level[j], buf.at[j], sems.at[j]).start()
    acc[...] = jnp.zeros(acc.shape, jnp.float32)
    spread(packed, q4)

    def step(j, carry):
        dr, dc, _, hit = listed(n_cs + j, n_cs, n_c, col, cand, count)
        wait_for(level[0], buf, sems, j)

        @pl.when(hit == 1)
        def _():
            grad_tile(c2, j, dr, dc, core, q, buf, s_scr, d_scr, acc, q4)

        return carry

    lax.fori_loop(0, n_cs, step, 0)


def grad_far_kernel(n_c, n_cs, c2, sc, cand, count, q, packed, begun, *refs):
    got, other = refs[:n_cs], refs[n_cs : 2 * n_cs]
    out, buf, sems, s_scr, d_scr, q4, acc = refs[2 * n_cs :]
    core, col = sc[0], sc[2]
    load_far(got, other, buf, sems, core)
    acc[...] = begun[...]
    spread(packed, q4)

    def step(j, carry):
        slot = jnp.where(j < n_cs, j, n_cs + j)
        dr, dc, _, hit = listed(slot, n_cs, n_c, col, cand, count)
        wait_for(got[0], buf, sems, j)

        @pl.when(hit == 1)
        def _():
            grad_tile(c2, j, dr, dc, core, q, buf, s_scr, d_scr, acc, q4)

        return carry

    lax.fori_loop(0, 2 * n_cs, step, 0)
    out[...] = acc[...].reshape(HALF, PADW, acc.shape[1])[:, :TILE]


def query_near(n_c, sc, cand, count, q, level):
    n_cs, ch = len(level), q.shape[1]
    return pl.pallas_call(
        functools.partial(near_kernel, n_c, n_cs, math.log2(math.e) / math.sqrt(ch)),
        out_shape=jax.ShapeDtypeStruct((4, HC, 128), jnp.float32),
        in_specs=[SMEM, SMEM, SMEM, VMEM] + [ANY] * n_cs,
        out_specs=VMEM,
        scratch_shapes=[
            pltpu.VMEM((n_cs, 2, HC, ch), jnp.bfloat16),
            pltpu.SemaphoreType.DMA((n_cs,)),
            pltpu.VMEM((HC, 1024), jnp.float32),
        ],
        compiler_params=pltpu.CompilerParams(vmem_limit_bytes=12 * 2**20),
        cost_estimate=COST,
        name="query_near",
    )(sc, cand, count, q, *level)


def query_far(n_c, sc, cand, count, q, ctg, begun, got, other):
    n_cs, ch = len(got), q.shape[1]
    return pl.pallas_call(
        functools.partial(far_kernel, n_c, n_cs, math.log2(math.e) / math.sqrt(ch)),
        out_shape=(
            jax.ShapeDtypeStruct((2, HC), jnp.float32),
            jax.ShapeDtypeStruct((8, HC), jnp.float32),
            jax.ShapeDtypeStruct((HC, 128), jnp.float32),
        ),
        in_specs=[SMEM, SMEM, SMEM, VMEM, VMEM, VMEM] + [ANY] * (2 * n_cs),
        out_specs=(VMEM, VMEM, VMEM),
        scratch_shapes=[
            pltpu.VMEM((2 * n_cs, 2, HC, ch), jnp.bfloat16),
            pltpu.SemaphoreType.DMA((2 * n_cs,)),
            pltpu.VMEM((HC, 1024), jnp.float32),
            pltpu.VMEM((4, HC, 128), jnp.float32),
        ],
        compiler_params=pltpu.CompilerParams(vmem_limit_bytes=12 * 2**20),
        cost_estimate=COST,
        name="query_far",
    )(sc, cand, count, q, ctg, begun, *got, *other)


def grad_near(n_c, sc, cand, count, q, packed, level):
    n_cs, ch = len(level), q.shape[1]
    return pl.pallas_call(
        functools.partial(grad_near_kernel, n_c, n_cs, math.log2(math.e) / math.sqrt(ch)),
        out_shape=jax.ShapeDtypeStruct((HC, ch), jnp.float32),
        in_specs=[SMEM, SMEM, SMEM, VMEM, VMEM] + [ANY] * n_cs,
        out_specs=VMEM,
        scratch_shapes=[
            pltpu.VMEM((n_cs, 2, HC, ch), jnp.bfloat16),
            pltpu.SemaphoreType.DMA((n_cs,)),
            pltpu.VMEM((HC, 512), jnp.float32),
            pltpu.VMEM((HC, 512), jnp.bfloat16),
            pltpu.VMEM((4, HC, 128), jnp.float32),
        ],
        compiler_params=pltpu.CompilerParams(vmem_limit_bytes=12 * 2**20),
        cost_estimate=COST,
        name="grad_near",
    )(sc, cand, count, q, packed, *level)


def grad_far(n_c, sc, cand, count, q, packed, begun, got, other):
    n_cs, ch = len(got), q.shape[1]
    return pl.pallas_call(
        functools.partial(grad_far_kernel, n_c, n_cs, math.log2(math.e) / math.sqrt(ch)),
        out_shape=jax.ShapeDtypeStruct((HALF, TILE, ch), jnp.float32),
        in_specs=[SMEM, SMEM, SMEM, VMEM, VMEM, VMEM] + [ANY] * (2 * n_cs),
        out_specs=VMEM,
        scratch_shapes=[
            pltpu.VMEM((2 * n_cs, 2, HC, ch), jnp.bfloat16),
            pltpu.SemaphoreType.DMA((2 * n_cs,)),
            pltpu.VMEM((HC, 512), jnp.float32),
            pltpu.VMEM((HC, 512), jnp.bfloat16),
            pltpu.VMEM((4, HC, 128), jnp.float32),
            pltpu.VMEM((HC, ch), jnp.float32),
        ],
        compiler_params=pltpu.CompilerParams(vmem_limit_bytes=12 * 2**20),
        cost_estimate=COST,
        name="grad_far",
    )(sc, cand, count, q, packed, begun, *got, *other)


def target_kernel(n_c, n_cs, c2, sc, tgt, *refs):
    feats, stats = refs[:3], refs[3:6]
    out, buf, sems, st, st_sems, s_scr, d_scr, v_scr, acc = refs[6:]
    core, col = sc[0], sc[2]
    load_rows(*stats, st, st_sems, core)
    load_rows(*feats, buf, sems, core)
    acc[...] = jnp.zeros(acc.shape, jnp.float32)

    def step(slot, carry):
        dr, dc = slot_steps(slot, n_cs, n_c, col)
        a, j = slot // n_cs, slot % n_cs

        @pl.when(j == 0)
        def _():
            wait_for(feats[0], buf, sems, a)
            wait_for(stats[0], st, st_sems, a)

        code = 8 - (3 * (dr + 1) + dc + 1)
        where_at = lax.broadcasted_iota(jnp.int32, (8, HC), 1)
        which = lax.broadcasted_iota(jnp.int32, (8, HC), 0)
        flag = jnp.sum(jnp.where((where_at == code) & (which == 4), st[a, j, 0], 0.0))

        @pl.when(flag > 0.5)
        def _():
            col_t = (
                lax.broadcasted_iota(jnp.int32, (PADW, HC), 0) - 30 * dc
            ).astype(jnp.float32)
            for i in range(2):
                s_scr[...] = lax.dot_general(
                    tgt[...], buf[a, j, i], (((1,), (1,)), ((), ())), preferred_element_type=jnp.float32
                )
                lev, gr, gc, sh = (st[a, j, i, k : k + 1, :] for k in range(4))
                v_scr[...] = gc * col_t - sh
                for g in range(HALF):
                    rows = slice(g * PADW, (g + 1) * PADW)
                    row_t = (g + HALF * core - 30 * dr).astype(jnp.float32)
                    p = jnp.exp2(s_scr[rows] * c2 - lev)
                    d = p * (v_scr[...] + gr * row_t)
                    d_scr[rows] = d.astype(jnp.bfloat16)
                acc[...] += jnp.dot(d_scr[...], buf[a, j, i], preferred_element_type=jnp.float32)

        return carry

    lax.fori_loop(0, 3 * n_cs, step, 0)
    out[...] = acc[...].reshape(HALF, PADW, acc.shape[1])[:, :TILE]


def target_side(n_c, sc, tgt, feats, stats):
    n_cs, ch = feats[0].shape[0], tgt.shape[1]
    return pl.pallas_call(
        functools.partial(target_kernel, n_c, n_cs, math.log2(math.e) / math.sqrt(ch)),
        out_shape=jax.ShapeDtypeStruct((HALF, TILE, ch), jnp.float32),
        in_specs=[SMEM, VMEM] + [ANY] * 6,
        out_specs=VMEM,
        scratch_shapes=[
            pltpu.VMEM((3, n_cs, 2, HC, ch), jnp.bfloat16),
            pltpu.SemaphoreType.DMA((3,)),
            pltpu.VMEM((3, n_cs, 2, 8, HC), jnp.float32),
            pltpu.SemaphoreType.DMA((3,)),
            pltpu.VMEM((HC, HC), jnp.float32),
            pltpu.VMEM((HC, HC), jnp.bfloat16),
            pltpu.VMEM((PADW, HC), jnp.float32),
            pltpu.VMEM((HC, ch), jnp.float32),
        ],
        compiler_params=pltpu.CompilerParams(vmem_limit_bytes=12 * 2**20),
        cost_estimate=COST,
        name="target_side",
    )(sc, tgt, *feats, *stats)


def shards(frames, conv_first, conv_second, candidates, counts, cotangent):
    mine = frames[0]
    ch = mine.shape[2]
    n_r, n_c = lax.axis_size("rows"), lax.axis_size("cols")
    core, row, col = (lax.axis_index(a) for a in ("pair", "rows", "cols"))
    sc = jnp.stack([core, row, col]).astype(jnp.int32)
    cand, count = candidates.reshape(9), counts.reshape(1)
    ctg = jnp.pad(cotangent, ((0, 6), (0, 0), (0, PADW - TILE))).reshape(8, HC)
    other_frame = partner(mine)
    both = (mine, other_frame)
    if n_c == 2:
        edge = jnp.stack([jnp.where(col == 0, f[:, TILE - 2 :], f[:, :2]) for f in both])
        xl = xr = send(edge, lambda r, k, c: (r, 1 - k, c))
    else:
        xl = send(jnp.stack([f[:, TILE - 2 :] for f in both]), lambda r, k, c: (r, k + 1, c))
        xr = send(jnp.stack([f[:, :2] for f in both]), lambda r, k, c: (r, k - 1, c))
    w1, w2 = fetch(after(conv_first, both), conv_second)
    w1, w2 = w1.reshape(3, 3 * ch, ch), w2.reshape(3, 3 * ch, ch)
    xl_, xr_ = after((xl, xr), w1)
    lines = []
    for i, f in enumerate(both):
        ends = [jnp.where(core == 0, x[:2], x[TILE - 2 :]) for x in (xl_[i], f, xr_[i])]
        ends[0] = jnp.where(col > 0, ends[0], 0)
        ends[2] = jnp.where(col < n_c - 1, ends[2], 0)
        lines.append(jnp.concatenate(ends, axis=1))
    z = send(jnp.stack(lines), lambda r, k, c: (r - 1 + 2 * c, k, 1 - c))
    second = encode(1, n_r, n_c, sc, mine, other_frame, xl, xr, z, w1, w2)
    side = sideways(second)
    own_tile = jnp.stack([second, partner(second)])
    own_got = updown(own_tile)
    first = encode(0, n_r, n_c, sc, after(mine, own_tile), other_frame, xl, xr, z, w1, w2)
    q_side = sideways(first)
    side = after(tuple(side), (first, own_got))
    level = [own_tile] + [jnp.stack([x, partner(x)]) for x in side]
    got = [own_got] + [updown(t) for t in level[1:]]
    begun = query_near(n_c, sc, cand, count, first, level)
    got = list(after(tuple(got), begun))
    other = [partner(t) for t in got]
    flow, stats, packed = query_far(n_c, sc, cand, count, first, ctg, begun, got, other)
    q_own = jnp.stack([first, partner(after(first, begun))])
    q_side = after(tuple(q_side), packed)
    q_level = jnp.stack([q_own] + [jnp.stack([x, partner(x)]) for x in q_side])
    q_got = updown(q_level)
    st_side = sideways(stats)
    st_own = jnp.stack([stats, partner(stats)])
    part = grad_near(n_c, sc, cand, count, first, after(packed, (st_own, q_level)), level)
    st_side = after(tuple(st_side), part)
    st_level = jnp.stack([st_own] + [jnp.stack([x, partner(x)]) for x in st_side])
    st_got = updown(st_level)
    grad_first = grad_far(n_c, sc, cand, count, first, after(packed, st_level), part, got, other)
    q_got, st_got = after((q_got, st_got), grad_first)
    q_other, st_other = partner(q_got), partner(st_got)
    grad_second = target_side(
        n_c, sc, second, (q_level, q_got, q_other), (st_level, st_got, st_other)
    )
    return flow.reshape(2, HALF, PADW)[:, :, :TILE], grad_first, grad_second


def solution(mesh):
    in_specs = (
        P("pair", ("groups", "rows"), "cols", None),
        P(),
        P(),
        P(("groups", "rows"), "cols", None),
        P(("groups", "rows"), "cols"),
        P(None, ("groups", "rows", "pair"), "cols"),
    )
    out_specs = (
        P(None, ("groups", "rows", "pair"), "cols"),
        P(("groups", "rows", "pair"), "cols", None),
        P(("groups", "rows", "pair"), "cols", None),
    )
    return jax.shard_map(shards, mesh=mesh, in_specs=in_specs, out_specs=out_specs, check_vma=False)
```

```python
import functools
import math

import jax
import jax.numpy as jnp
from jax import lax
from jax.experimental import pallas as pl
from jax.experimental.pallas import tpu as pltpu
from jax.sharding import PartitionSpec as P

TILE = 30
HALF = 15
PADW = 32
HC = HALF * PADW
BODY = HALF + 2
EXT = HALF + 4
HID = HALF + 2
AXES = ("rows", "cols", "pair")
VMEM = pl.BlockSpec(memory_space=pltpu.VMEM)
SMEM = pl.BlockSpec(memory_space=pltpu.SMEM)
RB = 16
COST = pl.CostEstimate(flops=10**6, bytes_accessed=10**4, transcendentals=0)
ANY = pl.BlockSpec(memory_space=pl.ANY)
HBM = pl.BlockSpec(memory_space=pltpu.HBM)


def send(value, step):
    n_r, n_c = lax.axis_size("rows"), lax.axis_size("cols")
    pairs = []
    for r in range(n_r):
        for k in range(n_c):
            for c in range(2):
                r2, k2, c2 = step(r, k, c)
                if 0 <= r2 < n_r and 0 <= k2 < n_c:
                    pairs.append(((r * n_c + k) * 2 + c, (r2 * n_c + k2) * 2 + c2))
    return lax.ppermute(value, AXES, pairs)


def partner(value):
    return send(value, lambda r, k, c: (r, k, 1 - c))


def updown(value):
    return send(value, lambda r, k, c: (r + 1 - 2 * c, k, c))


def sideways(value):
    if lax.axis_size("cols") == 2:
        return [send(value, lambda r, k, c: (r, 1 - k, c))]
    return [
        send(value, lambda r, k, c: (r, k + 1, c)),
        send(value, lambda r, k, c: (r, k - 1, c)),
    ]


def after(value, *others):
    return lax.optimization_barrier((value, others))[0]


def encode_kernel(frame, n_r, n_c, sc, mine, got, xl, xr, z, w1, w2, out, ext, xcat, hid, hcat):
    core, row, col = sc[0], sc[1], sc[2]
    first_row = 2 * (1 - core)
    use_own = core == frame
    own_rows = mine[pl.ds((BODY - 4) * core, BODY)]
    got_rows = got[pl.ds((BODY - 4) * core, BODY)]
    body = jnp.where(use_own, own_rows, got_rows).astype(jnp.float32)
    slot = jnp.where(use_own, 0, 1)
    rows = pl.ds((BODY - 4) * core, BODY)
    left = jnp.where(col > 0, xl[slot, rows].astype(jnp.float32), 0.0)
    right = jnp.where(col < n_c - 1, xr[slot, rows].astype(jnp.float32), 0.0)
    ext[pl.ds(first_row, BODY), 2 : 2 + TILE] = body
    ext[pl.ds(first_row, BODY), 0:2] = left
    ext[pl.ds(first_row, BODY), 2 + TILE : 4 + TILE] = right
    ext[pl.ds(BODY * core, 2), 0 : 4 + TILE] = z[1 - slot].astype(jnp.float32)
    ch = body.shape[-1]
    for b in range(3):
        xcat[:, b * ch : (b + 1) * ch] = (
            ext[:, b : b + PADW].astype(jnp.bfloat16).reshape(EXT * PADW, ch)
        )
    acc = jnp.zeros((HID * PADW, ch), jnp.float32)
    for a in range(3):
        acc += jnp.dot(
            xcat[a * PADW : (a + HID) * PADW], w1[a], preferred_element_type=jnp.float32
        )
    hr = lax.broadcasted_iota(jnp.int32, (HID, PADW, ch), 0) + (row * TILE + core * HALF - 1)
    hc = lax.broadcasted_iota(jnp.int32, (HID, PADW, ch), 1) + (col * TILE - 1)
    inside = (hr >= 0) & (hr < n_r * TILE) & (hc >= 0) & (hc < n_c * TILE)
    hidden = jnp.where(inside, jnp.maximum(acc, 0.0).reshape(HID, PADW, ch), 0.0)
    hid[0 : HID * PADW] = hidden.reshape(HID * PADW, ch)
    hid[HID * PADW :] = jnp.zeros((8, ch), jnp.float32)
    for b in range(3):
        hcat[:, b * ch : (b + 1) * ch] = hid[b : b + HID * PADW].astype(jnp.bfloat16)
    acc2 = ext[2 : 2 + HALF, 2 : 2 + PADW].reshape(HC, ch)
    for a in range(3):
        acc2 += jnp.dot(hcat[a * PADW : a * PADW + HC], w2[a], preferred_element_type=jnp.float32)
    oc = lax.broadcasted_iota(jnp.int32, (HALF, PADW, ch), 1)
    out[...] = (
        jnp.where(oc < TILE, acc2.reshape(HALF, PADW, ch), 0.0)
        .astype(jnp.bfloat16)
        .reshape(HC, ch)
    )


def fetch_kernel(a, b, a_out, b_out, sems):
    copies = [
        pltpu.make_async_copy(a, a_out, sems.at[0]),
        pltpu.make_async_copy(b, b_out, sems.at[1]),
    ]
    for copy in copies:
        copy.start()
    for copy in copies:
        copy.wait()


def fetch(a, b):
    return pl.pallas_call(
        fetch_kernel,
        out_shape=[pltpu.VMEM(x.shape, x.dtype) for x in (a, b)],
        in_specs=[ANY, ANY],
        out_specs=[VMEM, VMEM],
        scratch_shapes=[pltpu.SemaphoreType.DMA((2,))],
        compiler_params=pltpu.CompilerParams(vmem_limit_bytes=2**20),
        cost_estimate=COST,
        name="fetch_weights",
    )(a, b)


def encode(frame, n_r, n_c, sc, mine, got, xl, xr, z, w1, w2):
    ch = mine.shape[-1]
    return pl.pallas_call(
        functools.partial(encode_kernel, frame, n_r, n_c),
        out_shape=jax.ShapeDtypeStruct((HC, ch), jnp.bfloat16),
        in_specs=[SMEM] + [VMEM] * 7,
        out_specs=VMEM,
        scratch_shapes=[
            pltpu.VMEM((EXT, 40, ch), jnp.float32),
            pltpu.VMEM((EXT * PADW, 3 * ch), jnp.bfloat16),
            pltpu.VMEM((HID * PADW + 8, ch), jnp.float32),
            pltpu.VMEM((HID * PADW, 3 * ch), jnp.bfloat16),
        ],
        compiler_params=pltpu.CompilerParams(vmem_limit_bytes=12 * 2**20),
        cost_estimate=COST,
        name=f"encode_frame{frame}",
    )(sc, mine, got, xl, xr, z, w1, w2)


def load(tiles, buf, sems, at):
    pltpu.make_async_copy(tiles, buf.at[at], sems.at[at]).start()


def load_rows(level, got, other, buf, sems, core):
    load(level, buf, sems, 1)
    load(got, buf, sems, 2 * core)
    load(other, buf, sems, 2 - 2 * core)


def wait_for(tiles, buf, sems, at):
    pltpu.make_async_copy(tiles, buf.at[at], sems.at[at]).wait()


def half_tile(buf, a, j, i):
    return buf[a, pl.ds(pl.multiple_of((2 * j + i) * HC, HC), HC)]


def slot_steps(slot, n_cs, n_c, col):
    dr = slot // n_cs - 1
    j = slot % n_cs
    if n_c == 2:
        dc = jnp.where(j == 0, 0, 1 - 2 * col)
    else:
        dc = jnp.where(j == 0, 0, 2 * j - 3)
    return dr, dc


def listed(slot, n_cs, n_c, col, cand, count):
    dr, dc = slot_steps(slot, n_cs, n_c, col)
    code = 3 * (dr + 1) + dc + 1
    hit = jnp.int32(0)
    for s in range(9):
        hit = jnp.where((cand[s] == code) & (s < count[0]), 1, hit)
    return dr, dc, code, hit


def half_of(dr, i, core):
    return jnp.where(dr == 0, core ^ i, jnp.where(dr < 0, i, 1 - i))


def lanes(rows):
    lane = lax.broadcasted_iota(jnp.int32, (rows, 128), 1)
    return lane, lane % PADW < TILE, lane < HC - 384


def add_tile(c2, a, j, dr, dc, core, q, buf, s_scr, state):
    for i in range(2):
        s_scr[:, i * 512 : i * 512 + HC] = lax.dot_general(
            q[...], half_tile(buf, a, j, i), (((1,), (1,)), ((), ())), preferred_element_type=jnp.float32
        )
    base = [(30 * dr + 15 * half_of(dr, i, core)).astype(jnp.float32) for i in range(2)]
    col_base = (30 * dc).astype(jnp.float32)
    lane, lane_ok, in_row = lanes(RB)
    for g in range(HC // RB):
        rows = slice(g * RB, (g + 1) * RB)
        s = [s_scr[rows, v * 128 : v * 128 + 128] for v in range(8)]
        top = jnp.maximum(
            jnp.maximum(jnp.maximum(s[0], s[1]), s[2]),
            jnp.maximum(jnp.maximum(s[4], s[5]), s[6]),
        )
        top = jnp.maximum(
            jnp.where(lane_ok, top, -jnp.inf),
            jnp.where(lane_ok & in_row, jnp.maximum(s[3], s[7]), -jnp.inf),
        )
        best = jnp.max(top, axis=1, keepdims=True) * c2
        old = state[0, rows]
        new = jnp.maximum(old, best)
        state[0, rows] = new
        factor = jnp.exp2(old - new)
        e = [jnp.exp2(x * c2 - new) for x in s]
        total, weighted = [], []
        for i in range(2):
            e0, e1, e2, e3 = e[4 * i : 4 * i + 4]
            a3 = jnp.where(in_row, e3, 0.0)
            a2 = a3 + e2
            a1 = a2 + e1
            total.append(a1 + e0)
            weighted.append(4.0 * (a1 + a2 + a3))
        both = total[0] + total[1]
        state[1, rows] = state[1, rows] * factor + both
        state[2, rows] = state[2, rows] * factor + (
            weighted[0] + weighted[1] + base[0] * total[0] + base[1] * total[1]
        )
        state[3, rows] = state[3, rows] * factor + col_base * both


def near_kernel(n_c, n_cs, c2, sc, cand, count, q, level, state, buf, sems, s_scr):
    core, col = sc[0], sc[2]
    load(level, buf, sems, 0)
    state[0] = jnp.full(state.shape[1:], -jnp.inf, jnp.float32)
    for k in range(1, 4):
        state[k] = jnp.zeros(state.shape[1:], jnp.float32)

    def step(j, carry):
        dr, dc, _, hit = listed(n_cs + j, n_cs, n_c, col, cand, count)

        @pl.when(j == 0)
        def _():
            wait_for(level, buf, sems, 0)

        @pl.when(hit == 1)
        def _():
            add_tile(c2, 0, j, dr, dc, core, q, buf, s_scr, state)

        return carry

    lax.fori_loop(0, n_cs, step, 0)


def far_kernel(n_c, n_cs, c2, sc, cand, count, q, ctg, begun, got, other, *refs):
    flow, stats, packed_out, buf, sems, s_scr, state = refs
    core, col = sc[0], sc[2]
    load(got, buf, sems, core)
    load(other, buf, sems, 1 - core)
    state[...] = begun[...]

    def step(i, carry):
        a, j = i // n_cs, i % n_cs
        dr, dc, _, hit = listed(2 * a * n_cs + j, n_cs, n_c, col, cand, count)

        @pl.when(j == 0)
        def _():
            wait_for(got, buf, sems, a)

        @pl.when(hit == 1)
        def _():
            add_tile(c2, a, j, dr, dc, core, q, buf, s_scr, state)

        return carry

    lax.fori_loop(0, 2 * n_cs, step, 0)
    wide, ok, _ = lanes(HC)
    norm = state[1]
    n_sum = jnp.sum(jnp.where(ok, norm, 0.0), axis=1, keepdims=True)
    r_sum = jnp.sum(
        jnp.where(ok, state[2] + (wide // PADW).astype(jnp.float32) * norm, 0.0),
        axis=1,
        keepdims=True,
    )
    c_sum = jnp.sum(
        jnp.where(ok, state[3] + (wide % PADW).astype(jnp.float32) * norm, 0.0),
        axis=1,
        keepdims=True,
    )
    cell = lax.broadcasted_iota(jnp.int32, (HC, 128), 0)
    q_row = (cell // PADW + HALF * core).astype(jnp.float32)
    q_col = (cell % PADW).astype(jnp.float32)
    mean_r = r_sum / n_sum
    mean_c = c_sum / n_sum
    pulls = jnp.transpose(
        jnp.concatenate([ctg[...], jnp.zeros((120, HC), jnp.float32)], axis=0)
    )
    scale = 1.0 / (TILE * math.sqrt(q.shape[1]))
    cr = pulls[:, 0:1] * scale
    cc = pulls[:, 1:2] * scale
    shift = cr * mean_r + cc * mean_c
    level2 = jnp.where(q_col < TILE, state[0] + jnp.log2(n_sum), 1e30)
    flags = jnp.zeros((HC, 128), jnp.float32)
    for slot in range(3 * n_cs):
        _, _, code, hit = listed(slot, n_cs, n_c, col, cand, count)
        flags = jnp.where((cell == code) & (hit == 1), 1.0, flags)
    packed = flags
    for k, value in enumerate(
        (level2, cr, cc, shift, flags, (mean_r - q_row) / TILE, (mean_c - q_col) / TILE)
    ):
        packed = jnp.where(wide == k, value, packed)
    packed_out[...] = packed
    turned = jnp.transpose(packed)
    stats[...] = turned[0:8]
    flow[...] = turned[5:7]


def spread(packed, q4):
    for k in range(4):
        q4[k] = jnp.broadcast_to(packed[:, k : k + 1], (HC, 128))


def grad_tile(c2, a, j, dr, dc, core, q, buf, s_scr, d_scr, acc, q4):
    lane, lane_ok, in_row = lanes(RB)
    lane_row = (lane // PADW).astype(jnp.float32)
    lane_col = (lane % PADW + 30 * dc).astype(jnp.float32)
    for i in range(2):
        s_scr[:, 0:HC] = lax.dot_general(
            q[...], half_tile(buf, a, j, i), (((1,), (1,)), ((), ())), preferred_element_type=jnp.float32
        )
        base = lane_row + (30 * dr + 15 * half_of(dr, i, core)).astype(jnp.float32)
        for g in range(HC // RB):
            rows = slice(g * RB, (g + 1) * RB)
            lev, gr, gc, sh = (q4[k, rows] for k in range(4))
            pull = gr * base + (gc * lane_col - sh)
            for v in range(4):
                p = jnp.exp2(s_scr[rows, v * 128 : v * 128 + 128] * c2 - lev)
                d = jnp.where(lane_ok & in_row if v == 3 else lane_ok, p * pull, 0.0)
                d_scr[rows, v * 128 : v * 128 + 128] = d.astype(jnp.bfloat16)
                if v < 3:
                    pull = pull + 4.0 * gr
        acc[...] += jnp.dot(d_scr[:, 0:HC], half_tile(buf, a, j, i), preferred_element_type=jnp.float32)


def grad_kernel(n_c, n_cs, c2, sc, cand, count, q, packed, level, got, other, *refs):
    out, buf, sems, s_scr, d_scr, q4, acc = refs
    core, col = sc[0], sc[2]
    load_rows(level, got, other, buf, sems, core)
    acc[...] = jnp.zeros(acc.shape, jnp.float32)
    spread(packed, q4)

    def step(slot, carry):
        a, j = slot // n_cs, slot % n_cs
        dr, dc, _, hit = listed(slot, n_cs, n_c, col, cand, count)

        @pl.when(j == 0)
        def _():
            wait_for(level, buf, sems, a)

        @pl.when(hit == 1)
        def _():
            grad_tile(c2, a, j, dr, dc, core, q, buf, s_scr, d_scr, acc, q4)

        return carry

    lax.fori_loop(0, 3 * n_cs, step, 0)
    out[...] = acc[...].reshape(HALF, PADW, acc.shape[1])[:, :TILE]


def tiles_call(kernel, n_c, ch, rows, n_cs, out_shape, scratch, vmem_ins, ins, tiles):
    return pl.pallas_call(
        functools.partial(kernel, n_c, n_cs, math.log2(math.e) / math.sqrt(ch)),
        out_shape=out_shape,
        in_specs=[SMEM] * 3 + [VMEM] * vmem_ins + [HBM] * len(tiles),
        out_specs=jax.tree.map(lambda _: VMEM, out_shape),
        scratch_shapes=[
            pltpu.VMEM((rows, n_cs * 2 * HC, ch), jnp.bfloat16),
            pltpu.SemaphoreType.DMA((rows,)),
        ]
        + scratch,
        compiler_params=pltpu.CompilerParams(vmem_limit_bytes=12 * 2**20),
        cost_estimate=COST,
        name=kernel.__name__,
    )(*ins, *tiles)


def query_near(n_c, sc, cand, count, q, level):
    ch, n_cs = q.shape[1], level.shape[0] // (2 * HC)
    out_shape = jax.ShapeDtypeStruct((4, HC, 128), jnp.float32)
    scratch = [pltpu.VMEM((HC, 1024), jnp.float32)]
    return tiles_call(
        near_kernel, n_c, ch, 1, n_cs, out_shape, scratch, 1, (sc, cand, count, q), (level,)
    )


def query_far(n_c, sc, cand, count, q, ctg, begun, got, other):
    ch, n_cs = q.shape[1], got.shape[0] // (2 * HC)
    out_shape = (
        jax.ShapeDtypeStruct((2, HC), jnp.float32),
        jax.ShapeDtypeStruct((8, HC), jnp.float32),
        jax.ShapeDtypeStruct((HC, 128), jnp.float32),
    )
    scratch = [pltpu.VMEM((HC, 1024), jnp.float32), pltpu.VMEM((4, HC, 128), jnp.float32)]
    ins = (sc, cand, count, q, ctg, begun)
    return tiles_call(far_kernel, n_c, ch, 2, n_cs, out_shape, scratch, 3, ins, (got, other))


def query_grad(n_c, sc, cand, count, q, packed, level, got, other):
    ch, n_cs = q.shape[1], level.shape[0] // (2 * HC)
    out_shape = jax.ShapeDtypeStruct((HALF, TILE, ch), jnp.float32)
    scratch = [
        pltpu.VMEM((HC, 512), jnp.float32),
        pltpu.VMEM((HC, 512), jnp.bfloat16),
        pltpu.VMEM((4, HC, 128), jnp.float32),
        pltpu.VMEM((HC, ch), jnp.float32),
    ]
    ins, tiles = (sc, cand, count, q, packed), (level, got, other)
    return tiles_call(grad_kernel, n_c, ch, 3, n_cs, out_shape, scratch, 2, ins, tiles)


def target_kernel(n_c, n_cs, c2, sc, tgt, *refs):
    feats, stats = refs[:3], refs[3:6]
    out, buf, sems, st, st_sems, s_scr, d_scr, v_scr, acc = refs[6:]
    core, col = sc[0], sc[2]
    load_rows(*stats, st, st_sems, core)
    load_rows(*feats, buf, sems, core)
    acc[...] = jnp.zeros(acc.shape, jnp.float32)

    def step(slot, carry):
        dr, dc = slot_steps(slot, n_cs, n_c, col)
        a, j = slot // n_cs, slot % n_cs

        @pl.when(j == 0)
        def _():
            wait_for(feats[0], buf, sems, a)
            wait_for(stats[0], st, st_sems, a)

        code = 8 - (3 * (dr + 1) + dc + 1)
        where_at = lax.broadcasted_iota(jnp.int32, (8, HC), 1)
        which = lax.broadcasted_iota(jnp.int32, (8, HC), 0)
        flag = jnp.sum(jnp.where((where_at == code) & (which == 4), st[a, pl.ds(pl.multiple_of(16 * j, 16), 8)], 0.0))

        @pl.when(flag > 0.5)
        def _():
            col_t = (
                lax.broadcasted_iota(jnp.int32, (PADW, HC), 0) - 30 * dc
            ).astype(jnp.float32)
            for i in range(2):
                s_scr[...] = lax.dot_general(
                    tgt[...], half_tile(buf, a, j, i), (((1,), (1,)), ((), ())), preferred_element_type=jnp.float32
                )
                four = st[a, pl.ds(pl.multiple_of((2 * j + i) * 8, 8), 8)]
                lev, gr, gc, sh = (four[k : k + 1] for k in range(4))
                v_scr[...] = gc * col_t - sh
                for g in range(HALF):
                    rows = slice(g * PADW, (g + 1) * PADW)
                    row_t = (g + HALF * core - 30 * dr).astype(jnp.float32)
                    p = jnp.exp2(s_scr[rows] * c2 - lev)
                    d = p * (v_scr[...] + gr * row_t)
                    d_scr[rows] = d.astype(jnp.bfloat16)
                acc[...] += jnp.dot(d_scr[...], half_tile(buf, a, j, i), preferred_element_type=jnp.float32)

        return carry

    lax.fori_loop(0, 3 * n_cs, step, 0)
    out[...] = acc[...].reshape(HALF, PADW, acc.shape[1])[:, :TILE]


def target_side(n_c, sc, tgt, feats, stats):
    n_cs, ch = feats[0].shape[0] // (2 * HC), tgt.shape[1]
    return pl.pallas_call(
        functools.partial(target_kernel, n_c, n_cs, math.log2(math.e) / math.sqrt(ch)),
        out_shape=jax.ShapeDtypeStruct((HALF, TILE, ch), jnp.float32),
        in_specs=[SMEM, VMEM] + [HBM] * 6,
        out_specs=VMEM,
        scratch_shapes=[
            pltpu.VMEM((3, n_cs * 2 * HC, ch), jnp.bfloat16),
            pltpu.SemaphoreType.DMA((3,)),
            pltpu.VMEM((3, n_cs * 2 * 8, HC), jnp.float32),
            pltpu.SemaphoreType.DMA((3,)),
            pltpu.VMEM((HC, HC), jnp.float32),
            pltpu.VMEM((HC, HC), jnp.bfloat16),
            pltpu.VMEM((PADW, HC), jnp.float32),
            pltpu.VMEM((HC, ch), jnp.float32),
        ],
        compiler_params=pltpu.CompilerParams(vmem_limit_bytes=12 * 2**20),
        cost_estimate=COST,
        name="target_side",
    )(sc, tgt, *feats, *stats)


def shards(frames, conv_first, conv_second, candidates, counts, cotangent):
    mine = frames[0]
    ch = mine.shape[2]
    n_r, n_c = lax.axis_size("rows"), lax.axis_size("cols")
    core, row, col = (lax.axis_index(a) for a in ("pair", "rows", "cols"))
    sc = jnp.stack([core, row, col]).astype(jnp.int32)
    cand, count = candidates.reshape(9), counts.reshape(1)
    ctg = jnp.pad(cotangent, ((0, 6), (0, 0), (0, PADW - TILE))).reshape(8, HC)
    other_frame = partner(mine)
    both = (mine, other_frame)
    if n_c == 2:
        edge = jnp.stack([jnp.where(col == 0, f[:, TILE - 2 :], f[:, :2]) for f in both])
        xl = xr = send(edge, lambda r, k, c: (r, 1 - k, c))
    else:
        xl = send(jnp.stack([f[:, TILE - 2 :] for f in both]), lambda r, k, c: (r, k + 1, c))
        xr = send(jnp.stack([f[:, :2] for f in both]), lambda r, k, c: (r, k - 1, c))
    w1, w2 = fetch(after(conv_first, both), conv_second)
    w1, w2 = w1.reshape(3, 3 * ch, ch), w2.reshape(3, 3 * ch, ch)
    xl_, xr_ = after((xl, xr), w1)
    lines = []
    for i, f in enumerate(both):
        ends = [jnp.where(core == 0, x[:2], x[TILE - 2 :]) for x in (xl_[i], f, xr_[i])]
        ends[0] = jnp.where(col > 0, ends[0], 0)
        ends[2] = jnp.where(col < n_c - 1, ends[2], 0)
        lines.append(jnp.concatenate(ends, axis=1))
    z = send(jnp.stack(lines), lambda r, k, c: (r - 1 + 2 * c, k, 1 - c))
    second = encode(1, n_r, n_c, sc, mine, other_frame, xl, xr, z, w1, w2)
    side = sideways(second)
    parts = [second, partner(second)]
    first = encode(0, n_r, n_c, sc, mine, other_frame, xl, xr, z, w1, w2)
    side = after(tuple(side), first)
    for x in side:
        parts += [x, partner(x)]
    level = jnp.concatenate(parts)
    got = updown(level)
    q_side = sideways(after(first, side))
    q_parts = [first, partner(after(first, side))]
    begun = query_near(n_c, sc, cand, count, first, level)
    for x in after(tuple(q_side), begun):
        q_parts += [x, partner(x)]
    q_level = jnp.concatenate(q_parts)
    q_got = updown(q_level)
    got = after(got, q_level)
    other = partner(got)
    flow, stats, packed = query_far(n_c, sc, cand, count, first, ctg, begun, got, other)
    st_side = sideways(stats)
    st_parts = [stats, partner(stats)]
    for x in st_side:
        st_parts += [x, partner(x)]
    st_level = jnp.concatenate(st_parts)
    st_got = updown(st_level)
    grad_first = query_grad(n_c, sc, cand, count, first, after(packed, st_level), level, got, other)
    q_got, st_got = after((q_got, st_got), grad_first)
    q_other, st_other = partner(q_got), partner(st_got)
    grad_second = target_side(
        n_c, sc, second, (q_level, q_got, q_other), (st_level, st_got, st_other)
    )
    return flow.reshape(2, HALF, PADW)[:, :, :TILE], grad_first, grad_second


def solution(mesh):
    in_specs = (
        P("pair", ("groups", "rows"), "cols", None),
        P(),
        P(),
        P(("groups", "rows"), "cols", None),
        P(("groups", "rows"), "cols"),
        P(None, ("groups", "rows", "pair"), "cols"),
    )
    out_specs = (
        P(None, ("groups", "rows", "pair"), "cols"),
        P(("groups", "rows", "pair"), "cols", None),
        P(("groups", "rows", "pair"), "cols", None),
    )
    return jax.shard_map(shards, mesh=mesh, in_specs=in_specs, out_specs=out_specs, check_vma=False)
```

```python
import functools
import math

import jax
import jax.numpy as jnp
from jax import lax
from jax.experimental import pallas as pl
from jax.experimental.pallas import tpu as pltpu
from jax.sharding import PartitionSpec as P

TILE = 30
HALF = 15
PADW = 32
HC = HALF * PADW
BODY = HALF + 2
EXT = HALF + 4
HID = HALF + 2
AXES = ("rows", "cols", "pair")
VMEM = pl.BlockSpec(memory_space=pltpu.VMEM)
SMEM = pl.BlockSpec(memory_space=pltpu.SMEM)
RB = 16
COST = pl.CostEstimate(flops=10**6, bytes_accessed=10**4, transcendentals=0)
ANY = pl.BlockSpec(memory_space=pl.ANY)
HBM = pl.BlockSpec(memory_space=pltpu.HBM)


def send(value, step):
    n_r, n_c = lax.axis_size("rows"), lax.axis_size("cols")
    pairs = []
    for r in range(n_r):
        for k in range(n_c):
            for c in range(2):
                r2, k2, c2 = step(r, k, c)
                if 0 <= r2 < n_r and 0 <= k2 < n_c:
                    pairs.append(((r * n_c + k) * 2 + c, (r2 * n_c + k2) * 2 + c2))
    return lax.ppermute(value, AXES, pairs)


def partner(value):
    return send(value, lambda r, k, c: (r, k, 1 - c))


def updown(value):
    return send(value, lambda r, k, c: (r + 1 - 2 * c, k, c))


def sideways(value):
    if lax.axis_size("cols") == 2:
        return [send(value, lambda r, k, c: (r, 1 - k, c))]
    return [
        send(value, lambda r, k, c: (r, k + 1, c)),
        send(value, lambda r, k, c: (r, k - 1, c)),
    ]


def after(value, *others):
    return lax.optimization_barrier((value, others))[0]


def encode_kernel(frame, n_r, n_c, sc, mine, got, xl, xr, z, w1, w2, out, ext, xcat, hid, hcat):
    core, row, col = sc[0], sc[1], sc[2]
    first_row = 2 * (1 - core)
    use_own = core == frame
    own_rows = mine[pl.ds((BODY - 4) * core, BODY)]
    got_rows = got[pl.ds((BODY - 4) * core, BODY)]
    body = jnp.where(use_own, own_rows, got_rows).astype(jnp.float32)
    slot = jnp.where(use_own, 0, 1)
    rows = pl.ds((BODY - 4) * core, BODY)
    left = jnp.where(col > 0, xl[slot, rows].astype(jnp.float32), 0.0)
    right = jnp.where(col < n_c - 1, xr[slot, rows].astype(jnp.float32), 0.0)
    ext[pl.ds(first_row, BODY), 2 : 2 + TILE] = body
    ext[pl.ds(first_row, BODY), 0:2] = left
    ext[pl.ds(first_row, BODY), 2 + TILE : 4 + TILE] = right
    ext[pl.ds(BODY * core, 2), 0 : 4 + TILE] = z[1 - slot].astype(jnp.float32)
    ch = body.shape[-1]
    for b in range(3):
        xcat[:, b * ch : (b + 1) * ch] = (
            ext[:, b : b + PADW].astype(jnp.bfloat16).reshape(EXT * PADW, ch)
        )
    acc = jnp.zeros((HID * PADW, ch), jnp.float32)
    for a in range(3):
        acc += jnp.dot(
            xcat[a * PADW : (a + HID) * PADW], w1[a], preferred_element_type=jnp.float32
        )
    hr = lax.broadcasted_iota(jnp.int32, (HID, PADW, ch), 0) + (row * TILE + core * HALF - 1)
    hc = lax.broadcasted_iota(jnp.int32, (HID, PADW, ch), 1) + (col * TILE - 1)
    inside = (hr >= 0) & (hr < n_r * TILE) & (hc >= 0) & (hc < n_c * TILE)
    hidden = jnp.where(inside, jnp.maximum(acc, 0.0).reshape(HID, PADW, ch), 0.0)
    hid[0 : HID * PADW] = hidden.reshape(HID * PADW, ch)
    hid[HID * PADW :] = jnp.zeros((8, ch), jnp.float32)
    for b in range(3):
        hcat[:, b * ch : (b + 1) * ch] = hid[b : b + HID * PADW].astype(jnp.bfloat16)
    acc2 = ext[2 : 2 + HALF, 2 : 2 + PADW].reshape(HC, ch)
    for a in range(3):
        acc2 += jnp.dot(hcat[a * PADW : a * PADW + HC], w2[a], preferred_element_type=jnp.float32)
    oc = lax.broadcasted_iota(jnp.int32, (HALF, PADW, ch), 1)
    out[...] = (
        jnp.where(oc < TILE, acc2.reshape(HALF, PADW, ch), 0.0)
        .astype(jnp.bfloat16)
        .reshape(HC, ch)
    )


def fetch_kernel(a, b, a_out, b_out, sems):
    copies = [
        pltpu.make_async_copy(a, a_out, sems.at[0]),
        pltpu.make_async_copy(b, b_out, sems.at[1]),
    ]
    for copy in copies:
        copy.start()
    for copy in copies:
        copy.wait()


def fetch(a, b):
    return pl.pallas_call(
        fetch_kernel,
        out_shape=[pltpu.VMEM(x.shape, x.dtype) for x in (a, b)],
        in_specs=[ANY, ANY],
        out_specs=[VMEM, VMEM],
        scratch_shapes=[pltpu.SemaphoreType.DMA((2,))],
        compiler_params=pltpu.CompilerParams(vmem_limit_bytes=2**20),
        cost_estimate=COST,
        name="fetch_weights",
    )(a, b)


def encode(frame, n_r, n_c, sc, mine, got, xl, xr, z, w1, w2):
    ch = mine.shape[-1]
    return pl.pallas_call(
        functools.partial(encode_kernel, frame, n_r, n_c),
        out_shape=jax.ShapeDtypeStruct((HC, ch), jnp.bfloat16),
        in_specs=[SMEM] + [VMEM] * 7,
        out_specs=VMEM,
        scratch_shapes=[
            pltpu.VMEM((EXT, 40, ch), jnp.float32),
            pltpu.VMEM((EXT * PADW, 3 * ch), jnp.bfloat16),
            pltpu.VMEM((HID * PADW + 8, ch), jnp.float32),
            pltpu.VMEM((HID * PADW, 3 * ch), jnp.bfloat16),
        ],
        compiler_params=pltpu.CompilerParams(vmem_limit_bytes=12 * 2**20),
        cost_estimate=COST,
        name=f"encode_frame{frame}",
    )(sc, mine, got, xl, xr, z, w1, w2)


def load(tiles, buf, sems, at):
    row = 0
    for tile in tiles:
        rows = tile.shape[0]
        pltpu.make_async_copy(tile, buf.at[at, pl.ds(row, rows)], sems.at[at]).start()
        row += rows


def load_rows(level, got, other, buf, sems, core):
    load(level, buf, sems, 1)
    load(got, buf, sems, 2 * core)
    load(other, buf, sems, 2 - 2 * core)


def wait_for(buf, sems, at):
    pltpu.make_async_copy(buf.at[at], buf.at[at], sems.at[at]).wait()


def half_tile(buf, a, j, i):
    return buf[a, pl.ds(pl.multiple_of((2 * j + i) * HC, HC), HC)]


def slot_steps(slot, n_cs, n_c, col):
    dr = slot // n_cs - 1
    j = slot % n_cs
    if n_c == 2:
        dc = jnp.where(j == 0, 0, 1 - 2 * col)
    else:
        dc = jnp.where(j == 0, 0, 2 * j - 3)
    return dr, dc


def listed(slot, n_cs, n_c, col, cand, count):
    dr, dc = slot_steps(slot, n_cs, n_c, col)
    code = 3 * (dr + 1) + dc + 1
    hit = jnp.int32(0)
    for s in range(9):
        hit = jnp.where((cand[s] == code) & (s < count[0]), 1, hit)
    return dr, dc, code, hit


def half_of(dr, i, core):
    return jnp.where(dr == 0, core ^ i, jnp.where(dr < 0, i, 1 - i))


def lanes(rows):
    lane = lax.broadcasted_iota(jnp.int32, (rows, 128), 1)
    return lane, lane % PADW < TILE, lane < HC - 384


def add_tile(c2, a, j, dr, dc, core, q, buf, s_scr, state):
    for i in range(2):
        s_scr[:, i * 512 : i * 512 + HC] = lax.dot_general(
            q[...], half_tile(buf, a, j, i), (((1,), (1,)), ((), ())), preferred_element_type=jnp.float32
        )
    base = [(30 * dr + 15 * half_of(dr, i, core)).astype(jnp.float32) for i in range(2)]
    col_base = (30 * dc).astype(jnp.float32)
    lane, lane_ok, in_row = lanes(RB)
    for g in range(HC // RB):
        rows = slice(g * RB, (g + 1) * RB)
        s = [s_scr[rows, v * 128 : v * 128 + 128] for v in range(8)]
        top = jnp.maximum(
            jnp.maximum(jnp.maximum(s[0], s[1]), s[2]),
            jnp.maximum(jnp.maximum(s[4], s[5]), s[6]),
        )
        top = jnp.maximum(
            jnp.where(lane_ok, top, -jnp.inf),
            jnp.where(lane_ok & in_row, jnp.maximum(s[3], s[7]), -jnp.inf),
        )
        best = jnp.max(top, axis=1, keepdims=True) * c2
        old = state[0, rows]
        new = jnp.maximum(old, best)
        state[0, rows] = new
        factor = jnp.exp2(old - new)
        e = [jnp.exp2(x * c2 - new) for x in s]
        total, weighted = [], []
        for i in range(2):
            e0, e1, e2, e3 = e[4 * i : 4 * i + 4]
            a3 = jnp.where(in_row, e3, 0.0)
            a2 = a3 + e2
            a1 = a2 + e1
            total.append(a1 + e0)
            weighted.append(4.0 * (a1 + a2 + a3))
        both = total[0] + total[1]
        state[1, rows] = state[1, rows] * factor + both
        state[2, rows] = state[2, rows] * factor + (
            weighted[0] + weighted[1] + base[0] * total[0] + base[1] * total[1]
        )
        state[3, rows] = state[3, rows] * factor + col_base * both


def near_kernel(n_c, n_cs, c2, sc, cand, count, q, *refs):
    level, (state, buf, sems, s_scr) = refs[:n_cs], refs[n_cs:]
    core, col = sc[0], sc[2]
    load(level, buf, sems, 0)
    state[0] = jnp.full(state.shape[1:], -jnp.inf, jnp.float32)
    for k in range(1, 4):
        state[k] = jnp.zeros(state.shape[1:], jnp.float32)

    def step(j, carry):
        dr, dc, _, hit = listed(n_cs + j, n_cs, n_c, col, cand, count)

        @pl.when(j == 0)
        def _():
            wait_for(buf, sems, 0)

        @pl.when(hit == 1)
        def _():
            add_tile(c2, 0, j, dr, dc, core, q, buf, s_scr, state)

        return carry

    lax.fori_loop(0, n_cs, step, 0)


def far_kernel(n_c, n_cs, c2, sc, cand, count, q, ctg, begun, *refs):
    got, other = refs[:n_cs], refs[n_cs : 2 * n_cs]
    flow, stats, packed_out, buf, sems, s_scr, state = refs[2 * n_cs :]
    core, col = sc[0], sc[2]
    load(got, buf, sems, core)
    load(other, buf, sems, 1 - core)
    state[...] = begun[...]

    def step(i, carry):
        a, j = i // n_cs, i % n_cs
        dr, dc, _, hit = listed(2 * a * n_cs + j, n_cs, n_c, col, cand, count)

        @pl.when(j == 0)
        def _():
            wait_for(buf, sems, a)

        @pl.when(hit == 1)
        def _():
            add_tile(c2, a, j, dr, dc, core, q, buf, s_scr, state)

        return carry

    lax.fori_loop(0, 2 * n_cs, step, 0)
    wide, ok, _ = lanes(HC)
    norm = state[1]
    n_sum = jnp.sum(jnp.where(ok, norm, 0.0), axis=1, keepdims=True)
    r_sum = jnp.sum(
        jnp.where(ok, state[2] + (wide // PADW).astype(jnp.float32) * norm, 0.0),
        axis=1,
        keepdims=True,
    )
    c_sum = jnp.sum(
        jnp.where(ok, state[3] + (wide % PADW).astype(jnp.float32) * norm, 0.0),
        axis=1,
        keepdims=True,
    )
    cell = lax.broadcasted_iota(jnp.int32, (HC, 128), 0)
    q_row = (cell // PADW + HALF * core).astype(jnp.float32)
    q_col = (cell % PADW).astype(jnp.float32)
    mean_r = r_sum / n_sum
    mean_c = c_sum / n_sum
    pulls = jnp.transpose(
        jnp.concatenate([ctg[...], jnp.zeros((120, HC), jnp.float32)], axis=0)
    )
    scale = 1.0 / (TILE * math.sqrt(q.shape[1]))
    cr = pulls[:, 0:1] * scale
    cc = pulls[:, 1:2] * scale
    shift = cr * mean_r + cc * mean_c
    level2 = jnp.where(q_col < TILE, state[0] + jnp.log2(n_sum), 1e30)
    flags = jnp.zeros((HC, 128), jnp.float32)
    for slot in range(3 * n_cs):
        _, _, code, hit = listed(slot, n_cs, n_c, col, cand, count)
        flags = jnp.where((cell == code) & (hit == 1), 1.0, flags)
    packed = flags
    for k, value in enumerate(
        (level2, cr, cc, shift, flags, (mean_r - q_row) / TILE, (mean_c - q_col) / TILE)
    ):
        packed = jnp.where(wide == k, value, packed)
    packed_out[...] = packed
    turned = jnp.transpose(packed)
    stats[...] = turned[0:8]
    flow[...] = turned[5:7]


def spread(packed, q4):
    for k in range(4):
        q4[k] = jnp.broadcast_to(packed[:, k : k + 1], (HC, 128))


def grad_tile(c2, a, j, dr, dc, core, q, buf, s_scr, d_scr, acc, q4):
    lane, lane_ok, in_row = lanes(RB)
    lane_row = (lane // PADW).astype(jnp.float32)
    lane_col = (lane % PADW + 30 * dc).astype(jnp.float32)
    for i in range(2):
        s_scr[:, 0:HC] = lax.dot_general(
            q[...], half_tile(buf, a, j, i), (((1,), (1,)), ((), ())), preferred_element_type=jnp.float32
        )
        base = lane_row + (30 * dr + 15 * half_of(dr, i, core)).astype(jnp.float32)
        for g in range(HC // RB):
            rows = slice(g * RB, (g + 1) * RB)
            lev, gr, gc, sh = (q4[k, rows] for k in range(4))
            pull = gr * base + (gc * lane_col - sh)
            for v in range(4):
                p = jnp.exp2(s_scr[rows, v * 128 : v * 128 + 128] * c2 - lev)
                d = jnp.where(lane_ok & in_row if v == 3 else lane_ok, p * pull, 0.0)
                d_scr[rows, v * 128 : v * 128 + 128] = d.astype(jnp.bfloat16)
                if v < 3:
                    pull = pull + 4.0 * gr
        acc[...] += jnp.dot(d_scr[:, 0:HC], half_tile(buf, a, j, i), preferred_element_type=jnp.float32)


def grad_kernel(n_c, n_cs, c2, sc, cand, count, q, packed, *refs):
    level, got, other = refs[:n_cs], refs[n_cs : 2 * n_cs], refs[2 * n_cs : 3 * n_cs]
    out, buf, sems, s_scr, d_scr, q4, acc = refs[3 * n_cs :]
    core, col = sc[0], sc[2]
    load_rows(level, got, other, buf, sems, core)
    acc[...] = jnp.zeros(acc.shape, jnp.float32)
    spread(packed, q4)

    def step(slot, carry):
        a, j = slot // n_cs, slot % n_cs
        dr, dc, _, hit = listed(slot, n_cs, n_c, col, cand, count)

        @pl.when(j == 0)
        def _():
            wait_for(buf, sems, a)

        @pl.when(hit == 1)
        def _():
            grad_tile(c2, a, j, dr, dc, core, q, buf, s_scr, d_scr, acc, q4)

        return carry

    lax.fori_loop(0, 3 * n_cs, step, 0)
    out[...] = acc[...].reshape(HALF, PADW, acc.shape[1])[:, :TILE]


def tiles_call(kernel, n_c, ch, rows, n_cs, out_shape, scratch, vmem_ins, ins, tiles):
    return pl.pallas_call(
        functools.partial(kernel, n_c, n_cs, math.log2(math.e) / math.sqrt(ch)),
        out_shape=out_shape,
        in_specs=[SMEM] * 3 + [VMEM] * vmem_ins + [HBM] * len(tiles),
        out_specs=jax.tree.map(lambda _: VMEM, out_shape),
        scratch_shapes=[
            pltpu.VMEM((rows, n_cs * 2 * HC, ch), jnp.bfloat16),
            pltpu.SemaphoreType.DMA((rows,)),
        ]
        + scratch,
        compiler_params=pltpu.CompilerParams(vmem_limit_bytes=12 * 2**20),
        cost_estimate=COST,
        name=kernel.__name__,
    )(*ins, *tiles)


def query_near(n_c, sc, cand, count, q, level):
    ch, n_cs = q.shape[1], len(level)
    out_shape = jax.ShapeDtypeStruct((4, HC, 128), jnp.float32)
    scratch = [pltpu.VMEM((HC, 1024), jnp.float32)]
    return tiles_call(
        near_kernel, n_c, ch, 1, n_cs, out_shape, scratch, 1, (sc, cand, count, q), level
    )


def query_far(n_c, sc, cand, count, q, ctg, begun, got, other):
    ch, n_cs = q.shape[1], len(got)
    out_shape = (
        jax.ShapeDtypeStruct((2, HC), jnp.float32),
        jax.ShapeDtypeStruct((8, HC), jnp.float32),
        jax.ShapeDtypeStruct((HC, 128), jnp.float32),
    )
    scratch = [pltpu.VMEM((HC, 1024), jnp.float32), pltpu.VMEM((4, HC, 128), jnp.float32)]
    ins = (sc, cand, count, q, ctg, begun)
    return tiles_call(far_kernel, n_c, ch, 2, n_cs, out_shape, scratch, 3, ins, (*got, *other))


def query_grad(n_c, sc, cand, count, q, packed, level, got, other):
    ch, n_cs = q.shape[1], len(level)
    out_shape = jax.ShapeDtypeStruct((HALF, TILE, ch), jnp.float32)
    scratch = [
        pltpu.VMEM((HC, 512), jnp.float32),
        pltpu.VMEM((HC, 512), jnp.bfloat16),
        pltpu.VMEM((4, HC, 128), jnp.float32),
        pltpu.VMEM((HC, ch), jnp.float32),
    ]
    ins, tiles = (sc, cand, count, q, packed), (*level, *got, *other)
    return tiles_call(grad_kernel, n_c, ch, 3, n_cs, out_shape, scratch, 2, ins, tiles)


def target_kernel(n_c, n_cs, c2, sc, tgt, *refs):
    feats, stats = refs[:3], refs[3:6]
    out, buf, sems, st, st_sems, s_scr, d_scr, v_scr, acc = refs[6:]
    core, col = sc[0], sc[2]
    load_rows(*([x] for x in stats), st, st_sems, core)
    load_rows(*([x] for x in feats), buf, sems, core)
    acc[...] = jnp.zeros(acc.shape, jnp.float32)

    def step(slot, carry):
        dr, dc = slot_steps(slot, n_cs, n_c, col)
        a, j = slot // n_cs, slot % n_cs

        @pl.when(j == 0)
        def _():
            wait_for(buf, sems, a)
            wait_for(st, st_sems, a)

        code = 8 - (3 * (dr + 1) + dc + 1)
        where_at = lax.broadcasted_iota(jnp.int32, (8, HC), 1)
        which = lax.broadcasted_iota(jnp.int32, (8, HC), 0)
        flag = jnp.sum(jnp.where((where_at == code) & (which == 4), st[a, pl.ds(pl.multiple_of(16 * j, 16), 8)], 0.0))

        @pl.when(flag > 0.5)
        def _():
            col_t = (
                lax.broadcasted_iota(jnp.int32, (PADW, HC), 0) - 30 * dc
            ).astype(jnp.float32)
            for i in range(2):
                s_scr[...] = lax.dot_general(
                    tgt[...], half_tile(buf, a, j, i), (((1,), (1,)), ((), ())), preferred_element_type=jnp.float32
                )
                four = st[a, pl.ds(pl.multiple_of((2 * j + i) * 8, 8), 8)]
                lev, gr, gc, sh = (four[k : k + 1] for k in range(4))
                v_scr[...] = gc * col_t - sh
                for g in range(HALF):
                    rows = slice(g * PADW, (g + 1) * PADW)
                    row_t = (g + HALF * core - 30 * dr).astype(jnp.float32)
                    p = jnp.exp2(s_scr[rows] * c2 - lev)
                    d = p * (v_scr[...] + gr * row_t)
                    d_scr[rows] = d.astype(jnp.bfloat16)
                acc[...] += jnp.dot(d_scr[...], half_tile(buf, a, j, i), preferred_element_type=jnp.float32)

        return carry

    lax.fori_loop(0, 3 * n_cs, step, 0)
    out[...] = acc[...].reshape(HALF, PADW, acc.shape[1])[:, :TILE]


def target_side(n_c, sc, tgt, feats, stats):
    n_cs, ch = feats[0].shape[0] // (2 * HC), tgt.shape[1]
    return pl.pallas_call(
        functools.partial(target_kernel, n_c, n_cs, math.log2(math.e) / math.sqrt(ch)),
        out_shape=jax.ShapeDtypeStruct((HALF, TILE, ch), jnp.float32),
        in_specs=[SMEM, VMEM] + [HBM] * 6,
        out_specs=VMEM,
        scratch_shapes=[
            pltpu.VMEM((3, n_cs * 2 * HC, ch), jnp.bfloat16),
            pltpu.SemaphoreType.DMA((3,)),
            pltpu.VMEM((3, n_cs * 2 * 8, HC), jnp.float32),
            pltpu.SemaphoreType.DMA((3,)),
            pltpu.VMEM((HC, HC), jnp.float32),
            pltpu.VMEM((HC, HC), jnp.bfloat16),
            pltpu.VMEM((PADW, HC), jnp.float32),
            pltpu.VMEM((HC, ch), jnp.float32),
        ],
        compiler_params=pltpu.CompilerParams(vmem_limit_bytes=12 * 2**20),
        cost_estimate=COST,
        name="target_side",
    )(sc, tgt, *feats, *stats)


def shards(frames, conv_first, conv_second, candidates, counts, cotangent):
    mine = frames[0]
    ch = mine.shape[2]
    n_r, n_c = lax.axis_size("rows"), lax.axis_size("cols")
    core, row, col = (lax.axis_index(a) for a in ("pair", "rows", "cols"))
    sc = jnp.stack([core, row, col]).astype(jnp.int32)
    cand, count = candidates.reshape(9), counts.reshape(1)
    ctg = jnp.pad(cotangent, ((0, 6), (0, 0), (0, PADW - TILE))).reshape(8, HC)
    other_frame = partner(mine)
    both = (mine, other_frame)
    if n_c == 2:
        edge = jnp.stack([jnp.where(col == 0, f[:, TILE - 2 :], f[:, :2]) for f in both])
        xl = xr = send(edge, lambda r, k, c: (r, 1 - k, c))
    else:
        xl = send(jnp.stack([f[:, TILE - 2 :] for f in both]), lambda r, k, c: (r, k + 1, c))
        xr = send(jnp.stack([f[:, :2] for f in both]), lambda r, k, c: (r, k - 1, c))
    w1, w2 = fetch(after(conv_first, both), conv_second)
    w1, w2 = w1.reshape(3, 3 * ch, ch), w2.reshape(3, 3 * ch, ch)
    xl_, xr_ = after((xl, xr), w1)
    lines = []
    for i, f in enumerate(both):
        ends = [jnp.where(core == 0, x[:2], x[TILE - 2 :]) for x in (xl_[i], f, xr_[i])]
        ends[0] = jnp.where(col > 0, ends[0], 0)
        ends[2] = jnp.where(col < n_c - 1, ends[2], 0)
        lines.append(jnp.concatenate(ends, axis=1))
    z = send(jnp.stack(lines), lambda r, k, c: (r - 1 + 2 * c, k, 1 - c))
    second = encode(1, n_r, n_c, sc, mine, other_frame, xl, xr, z, w1, w2)
    side = sideways(second)
    own = jnp.concatenate([second, partner(second)])
    first = encode(0, n_r, n_c, sc, mine, other_frame, xl, xr, z, w1, w2)
    own_got = updown(after(own, first))
    side = after(tuple(side), first)
    level = [own] + [jnp.concatenate([x, partner(x)]) for x in side]
    side_got = [updown(t) for t in level[1:]]
    q_side = sideways(after(first, side))
    q_parts = [first, partner(after(first, side))]
    begun = query_near(n_c, sc, cand, count, after(first, own_got), level)
    side_got = after(tuple(side_got), begun)
    for x in after(tuple(q_side), side_got):
        q_parts += [x, partner(x)]
    q_level = jnp.concatenate(q_parts)
    q_got = updown(q_level)
    own_got = after(own_got, begun)
    own_other = partner(own_got)
    got = [own_got, *side_got]
    other = [own_other] + [partner(t) for t in side_got]
    begun = after(begun, q_level)
    flow, stats, packed = query_far(n_c, sc, cand, count, first, ctg, begun, got, other)
    st_side = sideways(stats)
    st_parts = [stats, partner(stats)]
    for x in st_side:
        st_parts += [x, partner(x)]
    st_level = jnp.concatenate(st_parts)
    st_got = updown(st_level)
    q_got = after(q_got, st_level)
    q_other = partner(q_got)
    grad_first = query_grad(n_c, sc, cand, count, first, after(packed, (st_level, q_got)), level, got, other)
    st_got = after(st_got, grad_first)
    st_other = partner(st_got)
    grad_second = target_side(
        n_c, sc, second, (q_level, q_got, q_other), (st_level, st_got, st_other)
    )
    return flow.reshape(2, HALF, PADW)[:, :, :TILE], grad_first, grad_second


def solution(mesh):
    in_specs = (
        P("pair", ("groups", "rows"), "cols", None),
        P(),
        P(),
        P(("groups", "rows"), "cols", None),
        P(("groups", "rows"), "cols"),
        P(None, ("groups", "rows", "pair"), "cols"),
    )
    out_specs = (
        P(None, ("groups", "rows", "pair"), "cols"),
        P(("groups", "rows", "pair"), "cols", None),
        P(("groups", "rows", "pair"), "cols", None),
    )
    return jax.shard_map(shards, mesh=mesh, in_specs=in_specs, out_specs=out_specs, check_vma=False)
```

```python
import functools
import math

import jax
import jax.numpy as jnp
from jax import lax
from jax.experimental import pallas as pl
from jax.experimental.pallas import tpu as pltpu
from jax.sharding import PartitionSpec as P

TILE = 30
HALF = 15
PADW = 32
HC = HALF * PADW
BODY = HALF + 2
EXT = HALF + 4
HID = HALF + 2
AXES = ("rows", "cols", "pair")
VMEM = pl.BlockSpec(memory_space=pltpu.VMEM)
SMEM = pl.BlockSpec(memory_space=pltpu.SMEM)
RB = 16
COST = pl.CostEstimate(flops=10**6, bytes_accessed=10**4, transcendentals=0)
ANY = pl.BlockSpec(memory_space=pl.ANY)
HBM = pl.BlockSpec(memory_space=pltpu.HBM)


def send(value, step):
    n_r, n_c = lax.axis_size("rows"), lax.axis_size("cols")
    pairs = []
    for r in range(n_r):
        for k in range(n_c):
            for c in range(2):
                r2, k2, c2 = step(r, k, c)
                if 0 <= r2 < n_r and 0 <= k2 < n_c:
                    pairs.append(((r * n_c + k) * 2 + c, (r2 * n_c + k2) * 2 + c2))
    return lax.ppermute(value, AXES, pairs)


def partner(value):
    return send(value, lambda r, k, c: (r, k, 1 - c))


def updown(value):
    return send(value, lambda r, k, c: (r + 1 - 2 * c, k, c))


def sideways(value):
    if lax.axis_size("cols") == 2:
        return [send(value, lambda r, k, c: (r, 1 - k, c))]
    return [
        send(value, lambda r, k, c: (r, k + 1, c)),
        send(value, lambda r, k, c: (r, k - 1, c)),
    ]


def after(value, *others):
    return lax.optimization_barrier((value, others))[0]


def encode_kernel(frame, n_r, n_c, sc, mine, got, xl, xr, z, w1, w2, out, ext, xcat, hid, hcat):
    core, row, col = sc[0], sc[1], sc[2]
    first_row = 2 * (1 - core)
    use_own = core == frame
    own_rows = mine[pl.ds((BODY - 4) * core, BODY)]
    got_rows = got[pl.ds((BODY - 4) * core, BODY)]
    body = jnp.where(use_own, own_rows, got_rows).astype(jnp.float32)
    slot = jnp.where(use_own, 0, 1)
    rows = pl.ds((BODY - 4) * core, BODY)
    left = jnp.where(col > 0, xl[slot, rows].astype(jnp.float32), 0.0)
    right = jnp.where(col < n_c - 1, xr[slot, rows].astype(jnp.float32), 0.0)
    ext[pl.ds(first_row, BODY), 2 : 2 + TILE] = body
    ext[pl.ds(first_row, BODY), 0:2] = left
    ext[pl.ds(first_row, BODY), 2 + TILE : 4 + TILE] = right
    ext[pl.ds(BODY * core, 2), 0 : 4 + TILE] = z[1 - slot].astype(jnp.float32)
    ch = body.shape[-1]
    for b in range(3):
        xcat[:, b * ch : (b + 1) * ch] = (
            ext[:, b : b + PADW].astype(jnp.bfloat16).reshape(EXT * PADW, ch)
        )
    acc = jnp.zeros((HID * PADW, ch), jnp.float32)
    for a in range(3):
        acc += jnp.dot(
            xcat[a * PADW : (a + HID) * PADW], w1[a], preferred_element_type=jnp.float32
        )
    hr = lax.broadcasted_iota(jnp.int32, (HID, PADW, ch), 0) + (row * TILE + core * HALF - 1)
    hc = lax.broadcasted_iota(jnp.int32, (HID, PADW, ch), 1) + (col * TILE - 1)
    inside = (hr >= 0) & (hr < n_r * TILE) & (hc >= 0) & (hc < n_c * TILE)
    hidden = jnp.where(inside, jnp.maximum(acc, 0.0).reshape(HID, PADW, ch), 0.0)
    hid[0 : HID * PADW] = hidden.reshape(HID * PADW, ch)
    hid[HID * PADW :] = jnp.zeros((8, ch), jnp.float32)
    for b in range(3):
        hcat[:, b * ch : (b + 1) * ch] = hid[b : b + HID * PADW].astype(jnp.bfloat16)
    acc2 = ext[2 : 2 + HALF, 2 : 2 + PADW].reshape(HC, ch)
    for a in range(3):
        acc2 += jnp.dot(hcat[a * PADW : a * PADW + HC], w2[a], preferred_element_type=jnp.float32)
    oc = lax.broadcasted_iota(jnp.int32, (HALF, PADW, ch), 1)
    out[...] = (
        jnp.where(oc < TILE, acc2.reshape(HALF, PADW, ch), 0.0)
        .astype(jnp.bfloat16)
        .reshape(HC, ch)
    )


def fetch_kernel(a, b, a_out, b_out, sems):
    copies = [
        pltpu.make_async_copy(a, a_out, sems.at[0]),
        pltpu.make_async_copy(b, b_out, sems.at[1]),
    ]
    for copy in copies:
        copy.start()
    for copy in copies:
        copy.wait()


def fetch(a, b):
    return pl.pallas_call(
        fetch_kernel,
        out_shape=[pltpu.VMEM(x.shape, x.dtype) for x in (a, b)],
        in_specs=[ANY, ANY],
        out_specs=[VMEM, VMEM],
        scratch_shapes=[pltpu.SemaphoreType.DMA((2,))],
        compiler_params=pltpu.CompilerParams(vmem_limit_bytes=2**20),
        cost_estimate=COST,
        name="fetch_weights",
    )(a, b)


def encode(frame, n_r, n_c, sc, mine, got, xl, xr, z, w1, w2):
    ch = mine.shape[-1]
    return pl.pallas_call(
        functools.partial(encode_kernel, frame, n_r, n_c),
        out_shape=jax.ShapeDtypeStruct((HC, ch), jnp.bfloat16),
        in_specs=[SMEM] + [VMEM] * 7,
        out_specs=VMEM,
        scratch_shapes=[
            pltpu.VMEM((EXT, 40, ch), jnp.float32),
            pltpu.VMEM((EXT * PADW, 3 * ch), jnp.bfloat16),
            pltpu.VMEM((HID * PADW + 8, ch), jnp.float32),
            pltpu.VMEM((HID * PADW, 3 * ch), jnp.bfloat16),
        ],
        compiler_params=pltpu.CompilerParams(vmem_limit_bytes=12 * 2**20),
        cost_estimate=COST,
        name=f"encode_frame{frame}",
    )(sc, mine, got, xl, xr, z, w1, w2)


def load(tiles, buf, sems, at):
    row = 0
    for tile in tiles:
        rows = tile.shape[0]
        pltpu.make_async_copy(tile, buf.at[at, pl.ds(row, rows)], sems.at[at]).start()
        row += rows


def load_rows(level, got, other, buf, sems, core):
    load(level, buf, sems, 1)
    load(got, buf, sems, 2 * core)
    load(other, buf, sems, 2 - 2 * core)


def wait_for(buf, sems, at):
    pltpu.make_async_copy(buf.at[at], buf.at[at], sems.at[at]).wait()


def half_tile(buf, a, j, i):
    return buf[a, pl.ds(pl.multiple_of((2 * j + i) * HC, HC), HC)]


def slot_steps(slot, n_cs, n_c, col):
    dr = slot // n_cs - 1
    j = slot % n_cs
    if n_c == 2:
        dc = jnp.where(j == 0, 0, 1 - 2 * col)
    else:
        dc = jnp.where(j == 0, 0, 2 * j - 3)
    return dr, dc


def listed(slot, n_cs, n_c, col, cand, count):
    dr, dc = slot_steps(slot, n_cs, n_c, col)
    code = 3 * (dr + 1) + dc + 1
    hit = jnp.int32(0)
    for s in range(9):
        hit = jnp.where((cand[s] == code) & (s < count[0]), 1, hit)
    return dr, dc, code, hit


def half_of(dr, i, core):
    return jnp.where(dr == 0, core ^ i, jnp.where(dr < 0, i, 1 - i))


def lanes(rows):
    lane = lax.broadcasted_iota(jnp.int32, (rows, 128), 1)
    return lane, lane % PADW < TILE, lane < HC - 384


def add_tile(c2, a, j, dr, dc, core, q, buf, s_scr, state):
    for i in range(2):
        s_scr[:, i * 512 : i * 512 + HC] = lax.dot_general(
            q[...], half_tile(buf, a, j, i), (((1,), (1,)), ((), ())), preferred_element_type=jnp.float32
        )
    base = [(30 * dr + 15 * half_of(dr, i, core)).astype(jnp.float32) for i in range(2)]
    col_base = (30 * dc).astype(jnp.float32)
    lane, lane_ok, in_row = lanes(RB)
    for g in range(HC // RB):
        rows = slice(g * RB, (g + 1) * RB)
        s = [s_scr[rows, v * 128 : v * 128 + 128] for v in range(8)]
        top = jnp.maximum(
            jnp.maximum(jnp.maximum(s[0], s[1]), s[2]),
            jnp.maximum(jnp.maximum(s[4], s[5]), s[6]),
        )
        top = jnp.maximum(
            jnp.where(lane_ok, top, -jnp.inf),
            jnp.where(lane_ok & in_row, jnp.maximum(s[3], s[7]), -jnp.inf),
        )
        best = jnp.max(top, axis=1, keepdims=True) * c2
        old = state[0, rows]
        new = jnp.maximum(old, best)
        state[0, rows] = new
        factor = jnp.exp2(old - new)
        e = [jnp.exp2(x * c2 - new) for x in s]
        total, weighted = [], []
        for i in range(2):
            e0, e1, e2, e3 = e[4 * i : 4 * i + 4]
            a3 = jnp.where(in_row, e3, 0.0)
            a2 = a3 + e2
            a1 = a2 + e1
            total.append(a1 + e0)
            weighted.append(4.0 * (a1 + a2 + a3))
        both = total[0] + total[1]
        state[1, rows] = state[1, rows] * factor + both
        state[2, rows] = state[2, rows] * factor + (
            weighted[0] + weighted[1] + base[0] * total[0] + base[1] * total[1]
        )
        state[3, rows] = state[3, rows] * factor + col_base * both


def near_kernel(n_c, n_cs, c2, sc, cand, count, q, *refs):
    level, (state, buf, sems, s_scr) = refs[:n_cs], refs[n_cs:]
    core, col = sc[0], sc[2]
    load(level, buf, sems, 0)
    state[0] = jnp.full(state.shape[1:], -jnp.inf, jnp.float32)
    for k in range(1, 4):
        state[k] = jnp.zeros(state.shape[1:], jnp.float32)

    def step(j, carry):
        dr, dc, _, hit = listed(n_cs + j, n_cs, n_c, col, cand, count)

        @pl.when(j == 0)
        def _():
            wait_for(buf, sems, 0)

        @pl.when(hit == 1)
        def _():
            add_tile(c2, 0, j, dr, dc, core, q, buf, s_scr, state)

        return carry

    lax.fori_loop(0, n_cs, step, 0)


def far_kernel(n_c, n_cs, c2, sc, cand, count, q, ctg, begun, *refs):
    got, other = refs[:n_cs], refs[n_cs : 2 * n_cs]
    flow, stats, packed_out, buf, sems, s_scr, state = refs[2 * n_cs :]
    core, col = sc[0], sc[2]
    load(got, buf, sems, core)
    load(other, buf, sems, 1 - core)
    state[...] = begun[...]

    def step(i, carry):
        a, j = i // n_cs, i % n_cs
        dr, dc, _, hit = listed(2 * a * n_cs + j, n_cs, n_c, col, cand, count)

        @pl.when(j == 0)
        def _():
            wait_for(buf, sems, a)

        @pl.when(hit == 1)
        def _():
            add_tile(c2, a, j, dr, dc, core, q, buf, s_scr, state)

        return carry

    lax.fori_loop(0, 2 * n_cs, step, 0)
    wide, ok, _ = lanes(HC)
    norm = state[1]
    n_sum = jnp.sum(jnp.where(ok, norm, 0.0), axis=1, keepdims=True)
    r_sum = jnp.sum(
        jnp.where(ok, state[2] + (wide // PADW).astype(jnp.float32) * norm, 0.0),
        axis=1,
        keepdims=True,
    )
    c_sum = jnp.sum(
        jnp.where(ok, state[3] + (wide % PADW).astype(jnp.float32) * norm, 0.0),
        axis=1,
        keepdims=True,
    )
    cell = lax.broadcasted_iota(jnp.int32, (HC, 128), 0)
    q_row = (cell // PADW + HALF * core).astype(jnp.float32)
    q_col = (cell % PADW).astype(jnp.float32)
    mean_r = r_sum / n_sum
    mean_c = c_sum / n_sum
    pulls = jnp.transpose(
        jnp.concatenate([ctg[...], jnp.zeros((120, HC), jnp.float32)], axis=0)
    )
    scale = 1.0 / (TILE * math.sqrt(q.shape[1]))
    cr = pulls[:, 0:1] * scale
    cc = pulls[:, 1:2] * scale
    shift = cr * mean_r + cc * mean_c
    level2 = jnp.where(q_col < TILE, state[0] + jnp.log2(n_sum), 1e30)
    flags = jnp.zeros((HC, 128), jnp.float32)
    for slot in range(3 * n_cs):
        _, _, code, hit = listed(slot, n_cs, n_c, col, cand, count)
        flags = jnp.where((cell == code) & (hit == 1), 1.0, flags)
    packed = flags
    for k, value in enumerate(
        (level2, cr, cc, shift, flags, (mean_r - q_row) / TILE, (mean_c - q_col) / TILE)
    ):
        packed = jnp.where(wide == k, value, packed)
    packed_out[...] = packed
    turned = jnp.transpose(packed)
    stats[...] = turned[0:8]
    flow[...] = turned[5:7]


def spread(packed, q4):
    for k in range(4):
        q4[k] = jnp.broadcast_to(packed[:, k : k + 1], (HC, 128))


def grad_tile(c2, a, j, dr, dc, core, q, buf, s_scr, d_scr, acc, q4):
    lane, lane_ok, in_row = lanes(RB)
    lane_row = (lane // PADW).astype(jnp.float32)
    lane_col = (lane % PADW + 30 * dc).astype(jnp.float32)
    for i in range(2):
        s_scr[i, :, 0:HC] = lax.dot_general(
            q[...], half_tile(buf, a, j, i), (((1,), (1,)), ((), ())), preferred_element_type=jnp.float32
        )
    for i in range(2):
        base = lane_row + (30 * dr + 15 * half_of(dr, i, core)).astype(jnp.float32)
        for g in range(HC // RB):
            rows = slice(g * RB, (g + 1) * RB)
            lev, gr, gc, sh = (q4[k, rows] for k in range(4))
            pull = gr * base + (gc * lane_col - sh)
            for v in range(4):
                p = jnp.exp2(s_scr[i, rows, v * 128 : v * 128 + 128] * c2 - lev)
                d = jnp.where(lane_ok & in_row if v == 3 else lane_ok, p * pull, 0.0)
                d_scr[i, rows, v * 128 : v * 128 + 128] = d.astype(jnp.bfloat16)
                if v < 3:
                    pull = pull + 4.0 * gr
    acc[...] += sum(
        jnp.dot(d_scr[i, :, 0:HC], half_tile(buf, a, j, i), preferred_element_type=jnp.float32)
        for i in range(2)
    )


def grad_kernel(n_c, n_cs, c2, sc, cand, count, q, packed, *refs):
    level, got, other = refs[:n_cs], refs[n_cs : 2 * n_cs], refs[2 * n_cs : 3 * n_cs]
    out, buf, sems, s_scr, d_scr, q4, acc = refs[3 * n_cs :]
    core, col = sc[0], sc[2]
    load_rows(level, got, other, buf, sems, core)
    acc[...] = jnp.zeros(acc.shape, jnp.float32)
    spread(packed, q4)

    def step(slot, carry):
        a, j = slot // n_cs, slot % n_cs
        dr, dc, _, hit = listed(slot, n_cs, n_c, col, cand, count)

        @pl.when(j == 0)
        def _():
            wait_for(buf, sems, a)

        @pl.when(hit == 1)
        def _():
            grad_tile(c2, a, j, dr, dc, core, q, buf, s_scr, d_scr, acc, q4)

        return carry

    lax.fori_loop(0, 3 * n_cs, step, 0)
    out[...] = acc[...].reshape(HALF, PADW, acc.shape[1])[:, :TILE]


def tiles_call(kernel, n_c, ch, rows, n_cs, out_shape, scratch, vmem_ins, ins, tiles):
    return pl.pallas_call(
        functools.partial(kernel, n_c, n_cs, math.log2(math.e) / math.sqrt(ch)),
        out_shape=out_shape,
        in_specs=[SMEM] * 3 + [VMEM] * vmem_ins + [HBM] * len(tiles),
        out_specs=jax.tree.map(lambda _: VMEM, out_shape),
        scratch_shapes=[
            pltpu.VMEM((rows, n_cs * 2 * HC, ch), jnp.bfloat16),
            pltpu.SemaphoreType.DMA((rows,)),
        ]
        + scratch,
        compiler_params=pltpu.CompilerParams(vmem_limit_bytes=12 * 2**20),
        cost_estimate=COST,
        name=kernel.__name__,
    )(*ins, *tiles)


def query_near(n_c, sc, cand, count, q, level):
    ch, n_cs = q.shape[1], len(level)
    out_shape = jax.ShapeDtypeStruct((4, HC, 128), jnp.float32)
    scratch = [pltpu.VMEM((HC, 1024), jnp.float32)]
    return tiles_call(
        near_kernel, n_c, ch, 1, n_cs, out_shape, scratch, 1, (sc, cand, count, q), level
    )


def query_far(n_c, sc, cand, count, q, ctg, begun, got, other):
    ch, n_cs = q.shape[1], len(got)
    out_shape = (
        jax.ShapeDtypeStruct((2, HC), jnp.float32),
        jax.ShapeDtypeStruct((8, HC), jnp.float32),
        jax.ShapeDtypeStruct((HC, 128), jnp.float32),
    )
    scratch = [pltpu.VMEM((HC, 1024), jnp.float32), pltpu.VMEM((4, HC, 128), jnp.float32)]
    ins = (sc, cand, count, q, ctg, begun)
    return tiles_call(far_kernel, n_c, ch, 2, n_cs, out_shape, scratch, 3, ins, (*got, *other))


def query_grad(n_c, sc, cand, count, q, packed, level, got, other):
    ch, n_cs = q.shape[1], len(level)
    out_shape = jax.ShapeDtypeStruct((HALF, TILE, ch), jnp.float32)
    scratch = [
        pltpu.VMEM((2, HC, 512), jnp.float32),
        pltpu.VMEM((2, HC, 512), jnp.bfloat16),
        pltpu.VMEM((4, HC, 128), jnp.float32),
        pltpu.VMEM((HC, ch), jnp.float32),
    ]
    ins, tiles = (sc, cand, count, q, packed), (*level, *got, *other)
    return tiles_call(grad_kernel, n_c, ch, 3, n_cs, out_shape, scratch, 2, ins, tiles)


def target_tile(c2, a, j, dr, dc, core, tgt, buf, st, s_scr, d_scr, v_scr, acc):
    code = 8 - (3 * (dr + 1) + dc + 1)
    where_at = lax.broadcasted_iota(jnp.int32, (8, HC), 1)
    which = lax.broadcasted_iota(jnp.int32, (8, HC), 0)
    row_4 = st[a, pl.ds(pl.multiple_of(16 * j, 16), 8)]
    flag = jnp.sum(jnp.where((where_at == code) & (which == 4), row_4, 0.0))

    @pl.when(flag > 0.5)
    def _():
        col_t = (lax.broadcasted_iota(jnp.int32, (PADW, HC), 0) - 30 * dc).astype(jnp.float32)
        for i in range(2):
            s_scr[i] = lax.dot_general(
                tgt[...], half_tile(buf, a, j, i), (((1,), (1,)), ((), ())), preferred_element_type=jnp.float32
            )
        for i in range(2):
            four = st[a, pl.ds(pl.multiple_of((2 * j + i) * 8, 8), 8)]
            lev, gr, gc, sh = (four[k : k + 1] for k in range(4))
            v_scr[i] = gc * col_t - sh
            for g in range(HALF):
                rows = slice(g * PADW, (g + 1) * PADW)
                row_t = (g + HALF * core - 30 * dr).astype(jnp.float32)
                p = jnp.exp2(s_scr[i, rows] * c2 - lev)
                d = p * (v_scr[i] + gr * row_t)
                d_scr[i, rows] = d.astype(jnp.bfloat16)
        acc[...] += sum(
            jnp.dot(d_scr[i], half_tile(buf, a, j, i), preferred_element_type=jnp.float32)
            for i in range(2)
        )


def target_near_kernel(n_c, n_cs, c2, sc, tgt, feats, stats, acc, buf, sems, st, st_sems, *scr):
    core, col = sc[0], sc[2]
    load([stats], st, st_sems, 0)
    load([feats], buf, sems, 0)
    acc[...] = jnp.zeros(acc.shape, jnp.float32)
    wait_for(st, st_sems, 0)
    wait_for(buf, sems, 0)

    def step(j, carry):
        dr, dc = slot_steps(n_cs + j, n_cs, n_c, col)
        target_tile(c2, 0, j, dr, dc, core, tgt, buf, st, *scr, acc)
        return carry

    lax.fori_loop(0, n_cs, step, 0)


def target_far_kernel(n_c, n_cs, c2, sc, tgt, begun, f_got, f_other, s_got, s_other, *refs):
    out, buf, sems, st, st_sems, *scr, acc = refs
    core, col = sc[0], sc[2]
    load([s_got], st, st_sems, core)
    load([s_other], st, st_sems, 1 - core)
    load([f_got], buf, sems, core)
    load([f_other], buf, sems, 1 - core)
    acc[...] = begun[...]

    def step(i, carry):
        a, j = i // n_cs, i % n_cs
        dr, dc = slot_steps(2 * a * n_cs + j, n_cs, n_c, col)

        @pl.when(j == 0)
        def _():
            wait_for(st, st_sems, a)
            wait_for(buf, sems, a)

        target_tile(c2, a, j, dr, dc, core, tgt, buf, st, *scr, acc)
        return carry

    lax.fori_loop(0, 2 * n_cs, step, 0)
    out[...] = acc[...].reshape(HALF, PADW, acc.shape[1])[:, :TILE]


def target_call(kernel, n_c, rows, out_shape, extra, vmem_ins, ins, feats, stats):
    n_cs, ch = feats[0].shape[0] // (2 * HC), feats[0].shape[1]
    tiles = [*feats, *stats]
    return pl.pallas_call(
        functools.partial(kernel, n_c, n_cs, math.log2(math.e) / math.sqrt(ch)),
        out_shape=out_shape,
        in_specs=[SMEM] + [VMEM] * vmem_ins + [HBM] * len(tiles),
        out_specs=VMEM,
        scratch_shapes=[
            pltpu.VMEM((rows, n_cs * 2 * HC, ch), jnp.bfloat16),
            pltpu.SemaphoreType.DMA((rows,)),
            pltpu.VMEM((rows, n_cs * 2 * 8, HC), jnp.float32),
            pltpu.SemaphoreType.DMA((rows,)),
            pltpu.VMEM((2, HC, HC), jnp.float32),
            pltpu.VMEM((2, HC, HC), jnp.bfloat16),
            pltpu.VMEM((2, PADW, HC), jnp.float32),
        ]
        + extra,
        compiler_params=pltpu.CompilerParams(vmem_limit_bytes=14 * 2**20),
        cost_estimate=COST,
        name=kernel.__name__,
    )(*ins, *tiles)


def target_near(n_c, sc, tgt, feats, stats):
    out_shape = jax.ShapeDtypeStruct(tgt.shape, jnp.float32)
    return target_call(target_near_kernel, n_c, 1, out_shape, [], 1, (sc, tgt), [feats], [stats])


def target_far(n_c, sc, tgt, begun, feats, stats):
    out_shape = jax.ShapeDtypeStruct((HALF, TILE, tgt.shape[1]), jnp.float32)
    extra = [pltpu.VMEM(tgt.shape, jnp.float32)]
    ins = (sc, tgt, begun)
    return target_call(target_far_kernel, n_c, 2, out_shape, extra, 2, ins, feats, stats)


def shards(frames, conv_first, conv_second, candidates, counts, cotangent):
    mine = frames[0]
    ch = mine.shape[2]
    n_r, n_c = lax.axis_size("rows"), lax.axis_size("cols")
    core, row, col = (lax.axis_index(a) for a in ("pair", "rows", "cols"))
    sc = jnp.stack([core, row, col]).astype(jnp.int32)
    cand, count = candidates.reshape(9), counts.reshape(1)
    ctg = jnp.pad(cotangent, ((0, 6), (0, 0), (0, PADW - TILE))).reshape(8, HC)
    other_frame = partner(mine)
    both = (mine, other_frame)
    if n_c == 2:
        edge = jnp.stack([jnp.where(col == 0, f[:, TILE - 2 :], f[:, :2]) for f in both])
        xl = xr = send(edge, lambda r, k, c: (r, 1 - k, c))
    else:
        xl = send(jnp.stack([f[:, TILE - 2 :] for f in both]), lambda r, k, c: (r, k + 1, c))
        xr = send(jnp.stack([f[:, :2] for f in both]), lambda r, k, c: (r, k - 1, c))
    w1, w2 = fetch(after(conv_first, both), conv_second)
    w1, w2 = w1.reshape(3, 3 * ch, ch), w2.reshape(3, 3 * ch, ch)
    xl_, xr_ = after((xl, xr), w1)
    lines = []
    for i, f in enumerate(both):
        ends = [jnp.where(core == 0, x[:2], x[TILE - 2 :]) for x in (xl_[i], f, xr_[i])]
        ends[0] = jnp.where(col > 0, ends[0], 0)
        ends[2] = jnp.where(col < n_c - 1, ends[2], 0)
        lines.append(jnp.concatenate(ends, axis=1))
    z = send(jnp.stack(lines), lambda r, k, c: (r - 1 + 2 * c, k, 1 - c))
    z = after(z, ctg)
    second = encode(1, n_r, n_c, sc, mine, other_frame, xl, xr, z, w1, w2)
    side = sideways(second)
    own = jnp.concatenate([second, partner(second)])
    first = encode(0, n_r, n_c, sc, mine, other_frame, xl, xr, z, w1, w2)
    own_got = updown(after(own, first))
    side = after(tuple(side), first)
    level = [own] + [jnp.concatenate([x, partner(x)]) for x in side]
    level[1:] = after(tuple(level[1:]), own_got)
    side_got = [updown(t) for t in level[1:]]
    q_side = sideways(after(first, side))
    q_parts = [first, partner(after(first, side))]
    own_other = partner(own_got)
    begun = query_near(n_c, sc, cand, count, after(first, own_other), level)
    side_got = after(tuple(side_got), begun)
    got = [own_got, *side_got]
    other = [own_other] + [partner(t) for t in side_got]
    for x in after(tuple(q_side), side_got):
        q_parts += [x, partner(x)]
    q_level = jnp.concatenate(q_parts)
    begun = after(begun, q_level)
    flow, stats, packed = query_far(n_c, sc, cand, count, first, ctg, begun, got, other)
    st_side = sideways(stats)
    st_parts = [stats, partner(stats)]
    q_got = updown(after(q_level, st_parts[1]))
    for x in st_side:
        st_parts += [x, partner(x)]
    st_level = jnp.concatenate(st_parts)
    st_got = updown(st_level)
    grad_first = query_grad(n_c, sc, cand, count, first, after(packed, st_level), level, got, other)
    q_got, st_got = after((q_got, st_got), grad_first)
    q_other, st_other = partner(q_got), partner(st_got)
    half = target_near(n_c, sc, after(second, (q_got, st_got)), q_level, st_level)
    half = after(half, (q_other, st_other))
    grad_second = target_far(n_c, sc, second, half, (q_got, q_other), (st_got, st_other))
    return flow.reshape(2, HALF, PADW)[:, :, :TILE], grad_first, grad_second


def solution(mesh):
    in_specs = (
        P("pair", ("groups", "rows"), "cols", None),
        P(),
        P(),
        P(("groups", "rows"), "cols", None),
        P(("groups", "rows"), "cols"),
        P(None, ("groups", "rows", "pair"), "cols"),
    )
    out_specs = (
        P(None, ("groups", "rows", "pair"), "cols"),
        P(("groups", "rows", "pair"), "cols", None),
        P(("groups", "rows", "pair"), "cols", None),
    )
    return jax.shard_map(shards, mesh=mesh, in_specs=in_specs, out_specs=out_specs, check_vma=False)
```

```python
import functools
import math

import jax
import jax.numpy as jnp
from jax import lax
from jax.experimental import pallas as pl
from jax.experimental.pallas import tpu as pltpu
from jax.sharding import PartitionSpec as P

TILE = 30
HALF = 15
PADW = 32
HC = HALF * PADW
BODY = HALF + 2
EXT = HALF + 4
HID = HALF + 2
AXES = ("rows", "cols", "pair")
VMEM = pl.BlockSpec(memory_space=pltpu.VMEM)
SMEM = pl.BlockSpec(memory_space=pltpu.SMEM)
RB = 16
COST = pl.CostEstimate(flops=10**6, bytes_accessed=10**4, transcendentals=0)
ANY = pl.BlockSpec(memory_space=pl.ANY)
HBM = pl.BlockSpec(memory_space=pltpu.HBM)


def send(value, step):
    n_r, n_c = lax.axis_size("rows"), lax.axis_size("cols")
    pairs = []
    for r in range(n_r):
        for k in range(n_c):
            for c in range(2):
                r2, k2, c2 = step(r, k, c)
                if 0 <= r2 < n_r and 0 <= k2 < n_c:
                    pairs.append(((r * n_c + k) * 2 + c, (r2 * n_c + k2) * 2 + c2))
    return lax.ppermute(value, AXES, pairs)


def partner(value):
    return send(value, lambda r, k, c: (r, k, 1 - c))


def updown(value):
    return send(value, lambda r, k, c: (r + 1 - 2 * c, k, c))


def sideways(value):
    if lax.axis_size("cols") == 2:
        return [send(value, lambda r, k, c: (r, 1 - k, c))]
    return [
        send(value, lambda r, k, c: (r, k + 1, c)),
        send(value, lambda r, k, c: (r, k - 1, c)),
    ]


def after(value, *others):
    return lax.optimization_barrier((value, others))[0]


def encode_kernel(frame, n_r, n_c, sc, mine, got, xl, xr, z, w1, w2, out, ext, xcat, hid, hcat):
    core, row, col = sc[0], sc[1], sc[2]
    first_row = 2 * (1 - core)
    use_own = core == frame
    own_rows = mine[pl.ds((BODY - 4) * core, BODY)]
    got_rows = got[pl.ds((BODY - 4) * core, BODY)]
    body = jnp.where(use_own, own_rows, got_rows).astype(jnp.float32)
    slot = jnp.where(use_own, 0, 1)
    rows = pl.ds((BODY - 4) * core, BODY)
    left = jnp.where(col > 0, xl[slot, rows].astype(jnp.float32), 0.0)
    right = jnp.where(col < n_c - 1, xr[slot, rows].astype(jnp.float32), 0.0)
    ext[pl.ds(first_row, BODY), 2 : 2 + TILE] = body
    ext[pl.ds(first_row, BODY), 0:2] = left
    ext[pl.ds(first_row, BODY), 2 + TILE : 4 + TILE] = right
    ext[pl.ds(BODY * core, 2), 0 : 4 + TILE] = z[1 - slot].astype(jnp.float32)
    ch = body.shape[-1]
    for b in range(3):
        xcat[:, b * ch : (b + 1) * ch] = (
            ext[:, b : b + PADW].astype(jnp.bfloat16).reshape(EXT * PADW, ch)
        )
    acc = jnp.zeros((HID * PADW, ch), jnp.float32)
    for a in range(3):
        acc += jnp.dot(
            xcat[a * PADW : (a + HID) * PADW], w1[a], preferred_element_type=jnp.float32
        )
    hr = lax.broadcasted_iota(jnp.int32, (HID, PADW, ch), 0) + (row * TILE + core * HALF - 1)
    hc = lax.broadcasted_iota(jnp.int32, (HID, PADW, ch), 1) + (col * TILE - 1)
    inside = (hr >= 0) & (hr < n_r * TILE) & (hc >= 0) & (hc < n_c * TILE)
    hidden = jnp.where(inside, jnp.maximum(acc, 0.0).reshape(HID, PADW, ch), 0.0)
    hid[0 : HID * PADW] = hidden.reshape(HID * PADW, ch)
    hid[HID * PADW :] = jnp.zeros((8, ch), jnp.float32)
    for b in range(3):
        hcat[:, b * ch : (b + 1) * ch] = hid[b : b + HID * PADW].astype(jnp.bfloat16)
    acc2 = ext[2 : 2 + HALF, 2 : 2 + PADW].reshape(HC, ch)
    for a in range(3):
        acc2 += jnp.dot(hcat[a * PADW : a * PADW + HC], w2[a], preferred_element_type=jnp.float32)
    oc = lax.broadcasted_iota(jnp.int32, (HALF, PADW, ch), 1)
    out[...] = (
        jnp.where(oc < TILE, acc2.reshape(HALF, PADW, ch), 0.0)
        .astype(jnp.bfloat16)
        .reshape(HC, ch)
    )


def fetch_kernel(a, b, a_out, b_out, sems):
    copies = [
        pltpu.make_async_copy(a, a_out, sems.at[0]),
        pltpu.make_async_copy(b, b_out, sems.at[1]),
    ]
    for copy in copies:
        copy.start()
    for copy in copies:
        copy.wait()


def fetch(a, b):
    return pl.pallas_call(
        fetch_kernel,
        out_shape=[pltpu.VMEM(x.shape, x.dtype) for x in (a, b)],
        in_specs=[ANY, ANY],
        out_specs=[VMEM, VMEM],
        scratch_shapes=[pltpu.SemaphoreType.DMA((2,))],
        compiler_params=pltpu.CompilerParams(vmem_limit_bytes=2**20),
        cost_estimate=COST,
        name="fetch_weights",
    )(a, b)


def encode(frame, n_r, n_c, sc, mine, got, xl, xr, z, w1, w2):
    ch = mine.shape[-1]
    return pl.pallas_call(
        functools.partial(encode_kernel, frame, n_r, n_c),
        out_shape=jax.ShapeDtypeStruct((HC, ch), jnp.bfloat16),
        in_specs=[SMEM] + [VMEM] * 7,
        out_specs=VMEM,
        scratch_shapes=[
            pltpu.VMEM((EXT, 40, ch), jnp.float32),
            pltpu.VMEM((EXT * PADW, 3 * ch), jnp.bfloat16),
            pltpu.VMEM((HID * PADW + 8, ch), jnp.float32),
            pltpu.VMEM((HID * PADW, 3 * ch), jnp.bfloat16),
        ],
        compiler_params=pltpu.CompilerParams(vmem_limit_bytes=14 * 2**20),
        cost_estimate=COST,
        name=f"encode_frame{frame}",
    )(sc, mine, got, xl, xr, z, w1, w2)


def load(tiles, buf, sems, at):
    pltpu.make_async_copy(tiles, buf.at[at], sems.at[at]).start()


def load_rows(level, got, other, buf, sems, core):
    load(level, buf, sems, 1)
    load(got, buf, sems, 2 * core)
    load(other, buf, sems, 2 - 2 * core)


def wait_for(tiles, buf, sems, at):
    pltpu.make_async_copy(tiles, buf.at[at], sems.at[at]).wait()


def half_tile(buf, a, j, i):
    return buf[a, pl.ds(pl.multiple_of((2 * j + i) * HC, HC), HC)]


def slot_steps(slot, n_cs, n_c, col):
    dr = slot // n_cs - 1
    j = slot % n_cs
    if n_c == 2:
        dc = jnp.where(j == 0, 0, 1 - 2 * col)
    else:
        dc = jnp.where(j == 0, 0, 2 * j - 3)
    return dr, dc


def listed(slot, n_cs, n_c, col, cand, count):
    dr, dc = slot_steps(slot, n_cs, n_c, col)
    code = 3 * (dr + 1) + dc + 1
    hit = jnp.int32(0)
    for s in range(9):
        hit = jnp.where((cand[s] == code) & (s < count[0]), 1, hit)
    return dr, dc, code, hit


def half_of(dr, i, core):
    return jnp.where(dr == 0, core ^ i, jnp.where(dr < 0, i, 1 - i))


def lanes(rows):
    lane = lax.broadcasted_iota(jnp.int32, (rows, 128), 1)
    return lane, lane % PADW < TILE, lane < HC - 384


def add_tile(c2, a, j, dr, dc, core, q, buf, state):
    whole = [
        lax.dot_general(
            q[...], half_tile(buf, a, j, i), (((1,), (1,)), ((), ())), preferred_element_type=jnp.float32
        )
        for i in range(2)
    ]
    base = [(30 * dr + 15 * half_of(dr, i, core)).astype(jnp.float32) for i in range(2)]
    col_base = (30 * dc).astype(jnp.float32)
    lane, lane_ok, in_row = lanes(RB)
    zero = jnp.zeros((RB, 512 - HC), jnp.float32)
    for g in range(HC // RB):
        rows = slice(g * RB, (g + 1) * RB)
        s = []
        for part in whole:
            s += [part[rows, v * 128 : v * 128 + 128] for v in range(3)]
            s.append(jnp.concatenate([part[rows, 384:], zero], axis=1))
        top = jnp.maximum(
            jnp.maximum(jnp.maximum(s[0], s[1]), s[2]),
            jnp.maximum(jnp.maximum(s[4], s[5]), s[6]),
        )
        top = jnp.maximum(
            jnp.where(lane_ok, top, -jnp.inf),
            jnp.where(lane_ok & in_row, jnp.maximum(s[3], s[7]), -jnp.inf),
        )
        best = jnp.max(top, axis=1, keepdims=True) * c2
        old = state[0, rows]
        new = jnp.maximum(old, best)
        state[0, rows] = new
        factor = jnp.exp2(old - new)
        e = [jnp.exp2(x * c2 - new) for x in s]
        total, weighted = [], []
        for i in range(2):
            e0, e1, e2, e3 = e[4 * i : 4 * i + 4]
            a3 = jnp.where(in_row, e3, 0.0)
            a2 = a3 + e2
            a1 = a2 + e1
            total.append(a1 + e0)
            weighted.append(4.0 * (a1 + a2 + a3))
        both = total[0] + total[1]
        state[1, rows] = state[1, rows] * factor + both
        state[2, rows] = state[2, rows] * factor + (
            weighted[0] + weighted[1] + base[0] * total[0] + base[1] * total[1]
        )
        state[3, rows] = state[3, rows] * factor + col_base * both


def near_kernel(n_c, n_cs, c2, sc, cand, count, q, level, state, buf, sems):
    core, col = sc[0], sc[2]
    load(level, buf, sems, 0)
    state[0] = jnp.full(state.shape[1:], -jnp.inf, jnp.float32)
    for k in range(1, 4):
        state[k] = jnp.zeros(state.shape[1:], jnp.float32)

    def step(j, carry):
        dr, dc, _, hit = listed(n_cs + j, n_cs, n_c, col, cand, count)

        @pl.when(j == 0)
        def _():
            wait_for(level, buf, sems, 0)

        @pl.when(hit == 1)
        def _():
            add_tile(c2, 0, j, dr, dc, core, q, buf, state)

        return carry

    lax.fori_loop(0, n_cs, step, 0)


def far_kernel(n_c, n_cs, c2, sc, cand, count, q, ctg, begun, got, other, *refs):
    flow, stats, packed_out, buf, sems, state = refs
    core, col = sc[0], sc[2]
    load(got, buf, sems, core)
    load(other, buf, sems, 1 - core)
    state[...] = begun[...]

    def step(i, carry):
        a, j = i // n_cs, i % n_cs
        dr, dc, _, hit = listed(2 * a * n_cs + j, n_cs, n_c, col, cand, count)

        @pl.when(j == 0)
        def _():
            wait_for(got, buf, sems, a)

        @pl.when(hit == 1)
        def _():
            add_tile(c2, a, j, dr, dc, core, q, buf, state)

        return carry

    lax.fori_loop(0, 2 * n_cs, step, 0)
    wide, ok, _ = lanes(HC)
    norm = state[1]
    n_sum = jnp.sum(jnp.where(ok, norm, 0.0), axis=1, keepdims=True)
    r_sum = jnp.sum(
        jnp.where(ok, state[2] + (wide // PADW).astype(jnp.float32) * norm, 0.0),
        axis=1,
        keepdims=True,
    )
    c_sum = jnp.sum(
        jnp.where(ok, state[3] + (wide % PADW).astype(jnp.float32) * norm, 0.0),
        axis=1,
        keepdims=True,
    )
    cell = lax.broadcasted_iota(jnp.int32, (HC, 128), 0)
    q_row = (cell // PADW + HALF * core).astype(jnp.float32)
    q_col = (cell % PADW).astype(jnp.float32)
    mean_r = r_sum / n_sum
    mean_c = c_sum / n_sum
    pulls = jnp.transpose(
        jnp.concatenate([ctg[...], jnp.zeros((120, HC), jnp.float32)], axis=0)
    )
    scale = 1.0 / (TILE * math.sqrt(q.shape[1]))
    cr = pulls[:, 0:1] * scale
    cc = pulls[:, 1:2] * scale
    shift = cr * mean_r + cc * mean_c
    level2 = jnp.where(q_col < TILE, state[0] + jnp.log2(n_sum), 1e30)
    flags = jnp.zeros((HC, 128), jnp.float32)
    for slot in range(3 * n_cs):
        _, _, code, hit = listed(slot, n_cs, n_c, col, cand, count)
        flags = jnp.where((cell == code) & (hit == 1), 1.0, flags)
    packed = flags
    for k, value in enumerate(
        (level2, cr, cc, shift, flags, (mean_r - q_row) / TILE, (mean_c - q_col) / TILE)
    ):
        packed = jnp.where(wide == k, value, packed)
    packed_out[...] = packed
    turned = jnp.transpose(packed)
    stats[...] = turned[0:8]
    flow[...] = turned[5:7]


def spread(packed, q4):
    for k in range(4):
        q4[k] = jnp.broadcast_to(packed[:, k : k + 1], (HC, 128))


def grad_tile(c2, a, j, dr, dc, core, q, buf, acc, q4):
    lane, lane_ok, _ = lanes(RB)
    lane_row = (lane // PADW).astype(jnp.float32)
    lane_col = (lane % PADW + 30 * dc).astype(jnp.float32)
    for i in range(2):
        tile = half_tile(buf, a, j, i)
        base = lane_row + (30 * dr + 15 * half_of(dr, i, core)).astype(jnp.float32)
        s = lax.dot_general(
            q[...], tile, (((1,), (1,)), ((), ())), preferred_element_type=jnp.float32
        )
        ds = []
        for g in range(HC // RB):
            rows = slice(g * RB, (g + 1) * RB)
            lev, gr, gc, sh = (q4[k, rows] for k in range(4))
            pull = gr * base + (gc * lane_col - sh)
            parts = []
            for v in range(4):
                width = min(128, HC - v * 128)
                p = jnp.exp2(s[rows, v * 128 : v * 128 + width] * c2 - lev[:, :width])
                d = jnp.where(lane_ok[:, :width], p * pull[:, :width], 0.0)
                parts.append(d.astype(jnp.bfloat16))
                if v < 3:
                    pull = pull + 4.0 * gr
            ds.append(jnp.concatenate(parts, axis=1))
        acc[...] += jnp.dot(jnp.concatenate(ds), tile, preferred_element_type=jnp.float32)


def grad_near_kernel(n_c, n_cs, c2, sc, cand, count, q, packed, level, acc, buf, sems, q4):
    core, col = sc[0], sc[2]
    load(level, buf, sems, 0)
    acc[...] = jnp.zeros(acc.shape, jnp.float32)
    spread(packed, q4)
    wait_for(level, buf, sems, 0)

    def step(j, carry):
        dr, dc, _, hit = listed(n_cs + j, n_cs, n_c, col, cand, count)

        @pl.when(hit == 1)
        def _():
            grad_tile(c2, 0, j, dr, dc, core, q, buf, acc, q4)

        return carry

    lax.fori_loop(0, n_cs, step, 0)


def grad_far_kernel(n_c, n_cs, c2, sc, cand, count, q, packed, begun, got, other, *refs):
    out, buf, sems, q4, acc = refs
    core, col = sc[0], sc[2]
    load(got, buf, sems, core)
    load(other, buf, sems, 1 - core)
    acc[...] = begun[...]
    spread(packed, q4)

    def step(i, carry):
        a, j = i // n_cs, i % n_cs
        dr, dc, _, hit = listed(2 * a * n_cs + j, n_cs, n_c, col, cand, count)

        @pl.when(j == 0)
        def _():
            wait_for(got, buf, sems, a)

        @pl.when(hit == 1)
        def _():
            grad_tile(c2, a, j, dr, dc, core, q, buf, acc, q4)

        return carry

    lax.fori_loop(0, 2 * n_cs, step, 0)
    out[...] = acc[...].reshape(HALF, PADW, acc.shape[1])[:, :TILE]


def tiles_call(kernel, n_c, ch, rows, n_cs, out_shape, scratch, vmem_ins, ins, tiles):
    return pl.pallas_call(
        functools.partial(kernel, n_c, n_cs, math.log2(math.e) / math.sqrt(ch)),
        out_shape=out_shape,
        in_specs=[SMEM] * 3 + [VMEM] * vmem_ins + [HBM] * len(tiles),
        out_specs=jax.tree.map(lambda _: VMEM, out_shape),
        scratch_shapes=[
            pltpu.VMEM((rows, n_cs * 2 * HC, ch), jnp.bfloat16),
            pltpu.SemaphoreType.DMA((rows,)),
        ]
        + scratch,
        compiler_params=pltpu.CompilerParams(vmem_limit_bytes=14 * 2**20),
        cost_estimate=COST,
        name=kernel.__name__,
    )(*ins, *tiles)


def query_near(n_c, sc, cand, count, q, level):
    ch, n_cs = q.shape[1], level.shape[0] // (2 * HC)
    out_shape = jax.ShapeDtypeStruct((4, HC, 128), jnp.float32)
    return tiles_call(
        near_kernel, n_c, ch, 1, n_cs, out_shape, [], 1, (sc, cand, count, q), (level,)
    )


def query_far(n_c, sc, cand, count, q, ctg, begun, got, other):
    ch, n_cs = q.shape[1], got.shape[0] // (2 * HC)
    out_shape = (
        jax.ShapeDtypeStruct((2, HC), jnp.float32),
        jax.ShapeDtypeStruct((8, HC), jnp.float32),
        jax.ShapeDtypeStruct((HC, 128), jnp.float32),
    )
    scratch = [pltpu.VMEM((4, HC, 128), jnp.float32)]
    ins = (sc, cand, count, q, ctg, begun)
    return tiles_call(far_kernel, n_c, ch, 2, n_cs, out_shape, scratch, 3, ins, (got, other))


def grad_near(n_c, sc, cand, count, q, packed, level):
    ch, n_cs = q.shape[1], level.shape[0] // (2 * HC)
    out_shape = jax.ShapeDtypeStruct((HC, ch), jnp.float32)
    scratch = [pltpu.VMEM((4, HC, 128), jnp.float32)]
    ins = (sc, cand, count, q, packed)
    return tiles_call(grad_near_kernel, n_c, ch, 1, n_cs, out_shape, scratch, 2, ins, (level,))


def grad_far(n_c, sc, cand, count, q, packed, begun, got, other):
    ch, n_cs = q.shape[1], got.shape[0] // (2 * HC)
    out_shape = jax.ShapeDtypeStruct((HALF, TILE, ch), jnp.float32)
    scratch = [pltpu.VMEM((4, HC, 128), jnp.float32), pltpu.VMEM((HC, ch), jnp.float32)]
    ins = (sc, cand, count, q, packed, begun)
    return tiles_call(grad_far_kernel, n_c, ch, 2, n_cs, out_shape, scratch, 3, ins, (got, other))


def target_kernel(n_c, n_cs, c2, sc, tgt, *refs):
    feats, stats = refs[:3], refs[3:6]
    out, buf, sems, st, st_sems, v_scr, acc = refs[6:]
    core, col = sc[0], sc[2]
    load_rows(*stats, st, st_sems, core)
    load_rows(*feats, buf, sems, core)
    acc[...] = jnp.zeros(acc.shape, jnp.float32)

    def step(slot, carry):
        dr, dc = slot_steps(slot, n_cs, n_c, col)
        a, j = slot // n_cs, slot % n_cs

        @pl.when(j == 0)
        def _():
            wait_for(feats[0], buf, sems, a)
            wait_for(stats[0], st, st_sems, a)

        code = 8 - (3 * (dr + 1) + dc + 1)
        where_at = lax.broadcasted_iota(jnp.int32, (8, HC), 1)
        which = lax.broadcasted_iota(jnp.int32, (8, HC), 0)
        flag = jnp.sum(jnp.where((where_at == code) & (which == 4), st[a, pl.ds(pl.multiple_of(16 * j, 16), 8)], 0.0))

        @pl.when(flag > 0.5)
        def _():
            col_t = (
                lax.broadcasted_iota(jnp.int32, (PADW, HC), 0) - 30 * dc
            ).astype(jnp.float32)
            for i in range(2):
                tile = half_tile(buf, a, j, i)
                four = st[a, pl.ds(pl.multiple_of((2 * j + i) * 8, 8), 8)]
                lev, gr, gc, sh = (four[k : k + 1] for k in range(4))
                v_scr[...] = gc * col_t - sh
                s = lax.dot_general(
                    tgt[...], tile, (((1,), (1,)), ((), ())), preferred_element_type=jnp.float32
                )
                ds = []
                for g in range(HALF):
                    row_t = (g + HALF * core - 30 * dr).astype(jnp.float32)
                    p = jnp.exp2(s[g * PADW : (g + 1) * PADW] * c2 - lev)
                    ds.append((p * (v_scr[...] + gr * row_t)).astype(jnp.bfloat16))
                acc[...] += jnp.dot(jnp.concatenate(ds), tile, preferred_element_type=jnp.float32)

        return carry

    lax.fori_loop(0, 3 * n_cs, step, 0)
    out[...] = acc[...].reshape(HALF, PADW, acc.shape[1])[:, :TILE]


def target_side(n_c, sc, tgt, feats, stats):
    n_cs, ch = feats[0].shape[0] // (2 * HC), tgt.shape[1]
    return pl.pallas_call(
        functools.partial(target_kernel, n_c, n_cs, math.log2(math.e) / math.sqrt(ch)),
        out_shape=jax.ShapeDtypeStruct((HALF, TILE, ch), jnp.float32),
        in_specs=[SMEM, VMEM] + [HBM] * 6,
        out_specs=VMEM,
        scratch_shapes=[
            pltpu.VMEM((3, n_cs * 2 * HC, ch), jnp.bfloat16),
            pltpu.SemaphoreType.DMA((3,)),
            pltpu.VMEM((3, n_cs * 2 * 8, HC), jnp.float32),
            pltpu.SemaphoreType.DMA((3,)),
            pltpu.VMEM((PADW, HC), jnp.float32),
            pltpu.VMEM((HC, ch), jnp.float32),
        ],
        compiler_params=pltpu.CompilerParams(vmem_limit_bytes=14 * 2**20),
        cost_estimate=COST,
        name="target_side",
    )(sc, tgt, *feats, *stats)


def shards(frames, conv_first, conv_second, candidates, counts, cotangent):
    mine = frames[0]
    ch = mine.shape[2]
    n_r, n_c = lax.axis_size("rows"), lax.axis_size("cols")
    core, row, col = (lax.axis_index(a) for a in ("pair", "rows", "cols"))
    sc = jnp.stack([core, row, col]).astype(jnp.int32)
    cand, count = candidates.reshape(9), counts.reshape(1)
    ctg = jnp.pad(cotangent, ((0, 6), (0, 0), (0, PADW - TILE))).reshape(8, HC)
    other_frame = partner(mine)
    both = (mine, other_frame)
    if n_c == 2:
        edge = jnp.stack([jnp.where(col == 0, f[:, TILE - 2 :], f[:, :2]) for f in both])
        xl = xr = send(edge, lambda r, k, c: (r, 1 - k, c))
    else:
        xl = send(jnp.stack([f[:, TILE - 2 :] for f in both]), lambda r, k, c: (r, k + 1, c))
        xr = send(jnp.stack([f[:, :2] for f in both]), lambda r, k, c: (r, k - 1, c))
    w1, w2 = fetch(after(conv_first, both), conv_second)
    w1, w2 = w1.reshape(3, 3 * ch, ch), w2.reshape(3, 3 * ch, ch)
    xl_, xr_ = after((xl, xr), w1)
    lines = []
    for i, f in enumerate(both):
        ends = [jnp.where(core == 0, x[:2], x[TILE - 2 :]) for x in (xl_[i], f, xr_[i])]
        ends[0] = jnp.where(col > 0, ends[0], 0)
        ends[2] = jnp.where(col < n_c - 1, ends[2], 0)
        lines.append(jnp.concatenate(ends, axis=1))
    z = send(jnp.stack(lines), lambda r, k, c: (r - 1 + 2 * c, k, 1 - c))
    second = encode(1, n_r, n_c, sc, mine, other_frame, xl, xr, z, w1, w2)
    side = sideways(second)
    parts = [second, partner(second)]
    first = encode(0, n_r, n_c, sc, mine, other_frame, xl, xr, z, w1, w2)
    side = after(tuple(side), first)
    for x in side:
        parts += [x, partner(x)]
    level = jnp.concatenate(parts)
    got = updown(level)
    q_side = sideways(after(first, side))
    q_parts = [first, partner(after(first, side))]
    begun = query_near(n_c, sc, cand, count, first, level)
    for x in after(tuple(q_side), begun):
        q_parts += [x, partner(x)]
    q_level = jnp.concatenate(q_parts)
    q_got = updown(q_level)
    got = after(got, q_level)
    other = partner(got)
    flow, stats, packed = query_far(n_c, sc, cand, count, first, ctg, begun, got, other)
    st_side = sideways(stats)
    st_parts = [stats, partner(stats)]
    part = grad_near(n_c, sc, cand, count, first, after(packed, st_parts[1]), level)
    for x in after(tuple(st_side), part):
        st_parts += [x, partner(x)]
    st_level = jnp.concatenate(st_parts)
    st_got = updown(st_level)
    q_got = after(q_got, st_level)
    q_other = partner(q_got)
    packed = after(packed, (st_level, q_got))
    grad_first = grad_far(n_c, sc, cand, count, first, packed, part, got, other)
    st_got = after(st_got, grad_first)
    st_other = partner(st_got)
    grad_second = target_side(
        n_c, sc, second, (q_level, q_got, q_other), (st_level, st_got, st_other)
    )
    return flow.reshape(2, HALF, PADW)[:, :, :TILE], grad_first, grad_second


def solution(mesh):
    in_specs = (
        P("pair", ("groups", "rows"), "cols", None),
        P(),
        P(),
        P(("groups", "rows"), "cols", None),
        P(("groups", "rows"), "cols"),
        P(None, ("groups", "rows", "pair"), "cols"),
    )
    out_specs = (
        P(None, ("groups", "rows", "pair"), "cols"),
        P(("groups", "rows", "pair"), "cols", None),
        P(("groups", "rows", "pair"), "cols", None),
    )
    return jax.shard_map(shards, mesh=mesh, in_specs=in_specs, out_specs=out_specs, check_vma=False)
```

```python
import functools
import math

import jax
import jax.numpy as jnp
from jax import lax
from jax.experimental import pallas as pl
from jax.experimental.pallas import tpu as pltpu
from jax.sharding import PartitionSpec as P

TILE = 30
HALF = 15
PADW = 32
HC = HALF * PADW
BODY = HALF + 2
EXT = HALF + 4
HID = HALF + 2
AXES = ("rows", "cols", "pair")
VMEM = pl.BlockSpec(memory_space=pltpu.VMEM)
SMEM = pl.BlockSpec(memory_space=pltpu.SMEM)
RB = 16
COST = pl.CostEstimate(flops=10**6, bytes_accessed=10**4, transcendentals=0)
ANY = pl.BlockSpec(memory_space=pl.ANY)
HBM = pl.BlockSpec(memory_space=pltpu.HBM)


def send(value, step):
    n_r, n_c = lax.axis_size("rows"), lax.axis_size("cols")
    pairs = []
    for r in range(n_r):
        for k in range(n_c):
            for c in range(2):
                r2, k2, c2 = step(r, k, c)
                if 0 <= r2 < n_r and 0 <= k2 < n_c:
                    pairs.append(((r * n_c + k) * 2 + c, (r2 * n_c + k2) * 2 + c2))
    return lax.ppermute(value, AXES, pairs)


def partner(value):
    return send(value, lambda r, k, c: (r, k, 1 - c))


def updown(value):
    return send(value, lambda r, k, c: (r + 1 - 2 * c, k, c))


def sideways(value):
    if lax.axis_size("cols") == 2:
        return [send(value, lambda r, k, c: (r, 1 - k, c))]
    return [
        send(value, lambda r, k, c: (r, k + 1, c)),
        send(value, lambda r, k, c: (r, k - 1, c)),
    ]


def after(value, *others):
    return lax.optimization_barrier((value, others))[0]


def encode_kernel(frame, n_r, n_c, sc, mine, got, xl, xr, z, w1, w2, out, ext, xcat, hid, hcat):
    core, row, col = sc[0], sc[1], sc[2]
    first_row = 2 * (1 - core)
    use_own = core == frame
    own_rows = mine[pl.ds((BODY - 4) * core, BODY)]
    got_rows = got[pl.ds((BODY - 4) * core, BODY)]
    body = jnp.where(use_own, own_rows, got_rows).astype(jnp.float32)
    slot = jnp.where(use_own, 0, 1)
    rows = pl.ds((BODY - 4) * core, BODY)
    left = jnp.where(col > 0, xl[slot, rows].astype(jnp.float32), 0.0)
    right = jnp.where(col < n_c - 1, xr[slot, rows].astype(jnp.float32), 0.0)
    ext[pl.ds(first_row, BODY), 2 : 2 + TILE] = body
    ext[pl.ds(first_row, BODY), 0:2] = left
    ext[pl.ds(first_row, BODY), 2 + TILE : 4 + TILE] = right
    ext[pl.ds(BODY * core, 2), 0 : 4 + TILE] = z[1 - slot].astype(jnp.float32)
    ch = body.shape[-1]
    for b in range(3):
        xcat[:, b * ch : (b + 1) * ch] = (
            ext[:, b : b + PADW].astype(jnp.bfloat16).reshape(EXT * PADW, ch)
        )
    acc = jnp.zeros((HID * PADW, ch), jnp.float32)
    for a in range(3):
        acc += jnp.dot(
            xcat[a * PADW : (a + HID) * PADW], w1[a], preferred_element_type=jnp.float32
        )
    hr = lax.broadcasted_iota(jnp.int32, (HID, PADW, ch), 0) + (row * TILE + core * HALF - 1)
    hc = lax.broadcasted_iota(jnp.int32, (HID, PADW, ch), 1) + (col * TILE - 1)
    inside = (hr >= 0) & (hr < n_r * TILE) & (hc >= 0) & (hc < n_c * TILE)
    hidden = jnp.where(inside, jnp.maximum(acc, 0.0).reshape(HID, PADW, ch), 0.0)
    hid[0 : HID * PADW] = hidden.reshape(HID * PADW, ch)
    hid[HID * PADW :] = jnp.zeros((8, ch), jnp.float32)
    for b in range(3):
        hcat[:, b * ch : (b + 1) * ch] = hid[b : b + HID * PADW].astype(jnp.bfloat16)
    acc2 = ext[2 : 2 + HALF, 2 : 2 + PADW].reshape(HC, ch)
    for a in range(3):
        acc2 += jnp.dot(hcat[a * PADW : a * PADW + HC], w2[a], preferred_element_type=jnp.float32)
    oc = lax.broadcasted_iota(jnp.int32, (HALF, PADW, ch), 1)
    out[...] = (
        jnp.where(oc < TILE, acc2.reshape(HALF, PADW, ch), 0.0)
        .astype(jnp.bfloat16)
        .reshape(HC, ch)
    )


def fetch_kernel(a, b, a_out, b_out, sems):
    copies = [
        pltpu.make_async_copy(a, a_out, sems.at[0]),
        pltpu.make_async_copy(b, b_out, sems.at[1]),
    ]
    for copy in copies:
        copy.start()
    for copy in copies:
        copy.wait()


def fetch(a, b):
    return pl.pallas_call(
        fetch_kernel,
        out_shape=[pltpu.VMEM(x.shape, x.dtype) for x in (a, b)],
        in_specs=[ANY, ANY],
        out_specs=[VMEM, VMEM],
        scratch_shapes=[pltpu.SemaphoreType.DMA((2,))],
        compiler_params=pltpu.CompilerParams(vmem_limit_bytes=2**20),
        cost_estimate=COST,
        name="fetch_weights",
    )(a, b)


def encode(frame, n_r, n_c, sc, mine, got, xl, xr, z, w1, w2):
    ch = mine.shape[-1]
    return pl.pallas_call(
        functools.partial(encode_kernel, frame, n_r, n_c),
        out_shape=jax.ShapeDtypeStruct((HC, ch), jnp.bfloat16),
        in_specs=[SMEM] + [VMEM] * 7,
        out_specs=VMEM,
        scratch_shapes=[
            pltpu.VMEM((EXT, 40, ch), jnp.float32),
            pltpu.VMEM((EXT * PADW, 3 * ch), jnp.bfloat16),
            pltpu.VMEM((HID * PADW + 8, ch), jnp.float32),
            pltpu.VMEM((HID * PADW, 3 * ch), jnp.bfloat16),
        ],
        compiler_params=pltpu.CompilerParams(vmem_limit_bytes=14 * 2**20),
        cost_estimate=COST,
        name=f"encode_frame{frame}",
    )(sc, mine, got, xl, xr, z, w1, w2)


def load(tiles, buf, sems, at):
    pltpu.make_async_copy(tiles, buf.at[at], sems.at[at]).start()


def load_rows(level, got, other, buf, sems, core):
    load(level, buf, sems, 1)
    load(got, buf, sems, 2 * core)
    load(other, buf, sems, 2 - 2 * core)


def wait_for(tiles, buf, sems, at):
    pltpu.make_async_copy(tiles, buf.at[at], sems.at[at]).wait()


def half_tile(buf, a, j, i):
    return buf[a, pl.ds(pl.multiple_of((2 * j + i) * HC, HC), HC)]


def slot_steps(slot, n_cs, n_c, col):
    dr = slot // n_cs - 1
    j = slot % n_cs
    if n_c == 2:
        dc = jnp.where(j == 0, 0, 1 - 2 * col)
    else:
        dc = jnp.where(j == 0, 0, 2 * j - 3)
    return dr, dc


def listed(slot, n_cs, n_c, col, cand, count):
    dr, dc = slot_steps(slot, n_cs, n_c, col)
    code = 3 * (dr + 1) + dc + 1
    hit = jnp.int32(0)
    for s in range(9):
        hit = jnp.where((cand[s] == code) & (s < count[0]), 1, hit)
    return dr, dc, code, hit


def half_of(dr, i, core):
    return jnp.where(dr == 0, core ^ i, jnp.where(dr < 0, i, 1 - i))


def lanes(rows):
    lane = lax.broadcasted_iota(jnp.int32, (rows, 128), 1)
    return lane, lane % PADW < TILE, lane < HC - 384


def add_tile(c2, a, j, dr, dc, core, q, buf, state):
    whole = [
        lax.dot_general(
            q[...], half_tile(buf, a, j, i), (((1,), (1,)), ((), ())), preferred_element_type=jnp.float32
        )
        for i in range(2)
    ]
    base = [(30 * dr + 15 * half_of(dr, i, core)).astype(jnp.float32) for i in range(2)]
    col_base = (30 * dc).astype(jnp.float32)
    lane, lane_ok, in_row = lanes(RB)
    zero = jnp.zeros((RB, 512 - HC), jnp.float32)
    for g in range(HC // RB):
        rows = slice(g * RB, (g + 1) * RB)
        s = []
        for part in whole:
            s += [part[rows, v * 128 : v * 128 + 128] for v in range(3)]
            s.append(jnp.concatenate([part[rows, 384:], zero], axis=1))
        top = jnp.maximum(
            jnp.maximum(jnp.maximum(s[0], s[1]), s[2]),
            jnp.maximum(jnp.maximum(s[4], s[5]), s[6]),
        )
        top = jnp.maximum(
            jnp.where(lane_ok, top, -jnp.inf),
            jnp.where(lane_ok & in_row, jnp.maximum(s[3], s[7]), -jnp.inf),
        )
        best = jnp.max(top, axis=1, keepdims=True) * c2
        old = state[0, rows]
        new = jnp.maximum(old, best)
        state[0, rows] = new
        factor = jnp.exp2(old - new)
        e = [jnp.exp2(x * c2 - new) for x in s]
        total, weighted = [], []
        for i in range(2):
            e0, e1, e2, e3 = e[4 * i : 4 * i + 4]
            a3 = jnp.where(in_row, e3, 0.0)
            a2 = a3 + e2
            a1 = a2 + e1
            total.append(a1 + e0)
            weighted.append(4.0 * (a1 + a2 + a3))
        both = total[0] + total[1]
        state[1, rows] = state[1, rows] * factor + both
        state[2, rows] = state[2, rows] * factor + (
            weighted[0] + weighted[1] + base[0] * total[0] + base[1] * total[1]
        )
        state[3, rows] = state[3, rows] * factor + col_base * both


def near_kernel(n_c, n_cs, c2, sc, cand, count, q, level, state, buf, sems):
    core, col = sc[0], sc[2]
    load(level, buf, sems, 0)
    state[0] = jnp.full(state.shape[1:], -jnp.inf, jnp.float32)
    for k in range(1, 4):
        state[k] = jnp.zeros(state.shape[1:], jnp.float32)

    def step(j, carry):
        dr, dc, _, hit = listed(n_cs + j, n_cs, n_c, col, cand, count)

        @pl.when(j == 0)
        def _():
            wait_for(level, buf, sems, 0)

        @pl.when(hit == 1)
        def _():
            add_tile(c2, 0, j, dr, dc, core, q, buf, state)

        return carry

    lax.fori_loop(0, n_cs, step, 0)


def far_kernel(n_c, n_cs, c2, sc, cand, count, q, ctg, begun, got, other, *refs):
    flow, stats, packed_out, buf, sems, state = refs
    core, col = sc[0], sc[2]
    load(got, buf, sems, core)
    load(other, buf, sems, 1 - core)
    state[...] = begun[...]

    def step(i, carry):
        a, j = i // n_cs, i % n_cs
        dr, dc, _, hit = listed(2 * a * n_cs + j, n_cs, n_c, col, cand, count)

        @pl.when(j == 0)
        def _():
            wait_for(got, buf, sems, a)

        @pl.when(hit == 1)
        def _():
            add_tile(c2, a, j, dr, dc, core, q, buf, state)

        return carry

    lax.fori_loop(0, 2 * n_cs, step, 0)
    where_at = lax.broadcasted_iota(jnp.int32, (128, HC), 0)
    ok = where_at % PADW < TILE
    norm = jnp.transpose(state[1])
    rows = jnp.transpose(state[2]) + (where_at // PADW).astype(jnp.float32) * norm
    cols = jnp.transpose(state[3]) + (where_at % PADW).astype(jnp.float32) * norm
    n_sum, r_sum, c_sum = (
        jnp.sum(jnp.where(ok, x, 0.0), axis=0, keepdims=True) for x in (norm, rows, cols)
    )
    cell = lax.broadcasted_iota(jnp.int32, (1, HC), 1)
    q_row = (cell // PADW + HALF * core).astype(jnp.float32)
    q_col = (cell % PADW).astype(jnp.float32)
    mean_r = r_sum / n_sum
    mean_c = c_sum / n_sum
    scale = 1.0 / (TILE * math.sqrt(q.shape[1]))
    cr = ctg[0:1] * scale
    cc = ctg[1:2] * scale
    shift = cr * mean_r + cc * mean_c
    best = jnp.transpose(state[0])[0:1]
    level2 = jnp.where(q_col < TILE, best + jnp.log2(n_sum), 1e30)
    flags = jnp.zeros((1, HC), jnp.float32)
    for slot in range(3 * n_cs):
        _, _, code, hit = listed(slot, n_cs, n_c, col, cand, count)
        flags = jnp.where((cell == code) & (hit == 1), 1.0, flags)
    flow_r, flow_c = (mean_r - q_row) / TILE, (mean_c - q_col) / TILE
    eight = jnp.concatenate(
        [level2, cr, cc, shift, flags, flow_r, flow_c, jnp.zeros((1, HC), jnp.float32)], axis=0
    )
    stats[...] = eight
    flow[...] = eight[5:7]
    packed_out[...] = jnp.transpose(
        jnp.concatenate([eight, jnp.zeros((120, HC), jnp.float32)], axis=0)
    )


def spread(packed, q4):
    for k in range(4):
        q4[k] = jnp.broadcast_to(packed[:, k : k + 1], (HC, 128))


def grad_tile(c2, a, j, dr, dc, core, q, buf, acc, q4):
    lane, lane_ok, _ = lanes(RB)
    lane_row = (lane // PADW).astype(jnp.float32)
    lane_col = (lane % PADW + 30 * dc).astype(jnp.float32)
    for i in range(2):
        tile = half_tile(buf, a, j, i)
        base = lane_row + (30 * dr + 15 * half_of(dr, i, core)).astype(jnp.float32)
        s = lax.dot_general(
            q[...], tile, (((1,), (1,)), ((), ())), preferred_element_type=jnp.float32
        )
        ds = []
        for g in range(HC // RB):
            rows = slice(g * RB, (g + 1) * RB)
            lev, gr, gc, sh = (q4[k, rows] for k in range(4))
            pull = gr * base + (gc * lane_col - sh)
            parts = []
            for v in range(4):
                width = min(128, HC - v * 128)
                p = jnp.exp2(s[rows, v * 128 : v * 128 + width] * c2 - lev[:, :width])
                d = jnp.where(lane_ok[:, :width], p * pull[:, :width], 0.0)
                parts.append(d.astype(jnp.bfloat16))
                if v < 3:
                    pull = pull + 4.0 * gr
            ds.append(jnp.concatenate(parts, axis=1))
        acc[...] += jnp.dot(jnp.concatenate(ds), tile, preferred_element_type=jnp.float32)


def grad_near_kernel(n_c, n_cs, c2, sc, cand, count, q, packed, level, acc, buf, sems, q4):
    core, col = sc[0], sc[2]
    load(level, buf, sems, 0)
    acc[...] = jnp.zeros(acc.shape, jnp.float32)
    spread(packed, q4)
    wait_for(level, buf, sems, 0)

    def step(j, carry):
        dr, dc, _, hit = listed(n_cs + j, n_cs, n_c, col, cand, count)

        @pl.when(hit == 1)
        def _():
            grad_tile(c2, 0, j, dr, dc, core, q, buf, acc, q4)

        return carry

    lax.fori_loop(0, n_cs, step, 0)


def grad_far_kernel(n_c, n_cs, c2, sc, cand, count, q, packed, begun, got, other, *refs):
    out, buf, sems, q4, acc = refs
    core, col = sc[0], sc[2]
    load(got, buf, sems, core)
    load(other, buf, sems, 1 - core)
    acc[...] = begun[...]
    spread(packed, q4)

    def step(i, carry):
        a, j = i // n_cs, i % n_cs
        dr, dc, _, hit = listed(2 * a * n_cs + j, n_cs, n_c, col, cand, count)

        @pl.when(j == 0)
        def _():
            wait_for(got, buf, sems, a)

        @pl.when(hit == 1)
        def _():
            grad_tile(c2, a, j, dr, dc, core, q, buf, acc, q4)

        return carry

    lax.fori_loop(0, 2 * n_cs, step, 0)
    out[...] = acc[...].reshape(HALF, PADW, acc.shape[1])[:, :TILE]


def tiles_call(kernel, n_c, ch, rows, n_cs, out_shape, scratch, vmem_ins, ins, tiles):
    return pl.pallas_call(
        functools.partial(kernel, n_c, n_cs, math.log2(math.e) / math.sqrt(ch)),
        out_shape=out_shape,
        in_specs=[SMEM] * 3 + [VMEM] * vmem_ins + [HBM] * len(tiles),
        out_specs=jax.tree.map(lambda _: VMEM, out_shape),
        scratch_shapes=[
            pltpu.VMEM((rows, n_cs * 2 * HC, ch), jnp.bfloat16),
            pltpu.SemaphoreType.DMA((rows,)),
        ]
        + scratch,
        compiler_params=pltpu.CompilerParams(vmem_limit_bytes=14 * 2**20),
        cost_estimate=COST,
        name=kernel.__name__,
    )(*ins, *tiles)


def query_near(n_c, sc, cand, count, q, level):
    ch, n_cs = q.shape[1], level.shape[0] // (2 * HC)
    out_shape = jax.ShapeDtypeStruct((4, HC, 128), jnp.float32)
    return tiles_call(
        near_kernel, n_c, ch, 1, n_cs, out_shape, [], 1, (sc, cand, count, q), (level,)
    )


def query_far(n_c, sc, cand, count, q, ctg, begun, got, other):
    ch, n_cs = q.shape[1], got.shape[0] // (2 * HC)
    out_shape = (
        jax.ShapeDtypeStruct((2, HC), jnp.float32),
        jax.ShapeDtypeStruct((8, HC), jnp.float32),
        jax.ShapeDtypeStruct((HC, 128), jnp.float32),
    )
    scratch = [pltpu.VMEM((4, HC, 128), jnp.float32)]
    ins = (sc, cand, count, q, ctg, begun)
    return tiles_call(far_kernel, n_c, ch, 2, n_cs, out_shape, scratch, 3, ins, (got, other))


def grad_near(n_c, sc, cand, count, q, packed, level):
    ch, n_cs = q.shape[1], level.shape[0] // (2 * HC)
    out_shape = jax.ShapeDtypeStruct((HC, ch), jnp.float32)
    scratch = [pltpu.VMEM((4, HC, 128), jnp.float32)]
    ins = (sc, cand, count, q, packed)
    return tiles_call(grad_near_kernel, n_c, ch, 1, n_cs, out_shape, scratch, 2, ins, (level,))


def grad_far(n_c, sc, cand, count, q, packed, begun, got, other):
    ch, n_cs = q.shape[1], got.shape[0] // (2 * HC)
    out_shape = jax.ShapeDtypeStruct((HALF, TILE, ch), jnp.float32)
    scratch = [pltpu.VMEM((4, HC, 128), jnp.float32), pltpu.VMEM((HC, ch), jnp.float32)]
    ins = (sc, cand, count, q, packed, begun)
    return tiles_call(grad_far_kernel, n_c, ch, 2, n_cs, out_shape, scratch, 3, ins, (got, other))


def target_kernel(n_c, n_cs, c2, sc, tgt, *refs):
    feats, stats = refs[:3], refs[3:6]
    out, buf, sems, st, st_sems, v_scr, acc = refs[6:]
    core, col = sc[0], sc[2]
    load_rows(*stats, st, st_sems, core)
    load_rows(*feats, buf, sems, core)
    acc[...] = jnp.zeros(acc.shape, jnp.float32)

    def step(slot, carry):
        dr, dc = slot_steps(slot, n_cs, n_c, col)
        a, j = slot // n_cs, slot % n_cs

        @pl.when(j == 0)
        def _():
            wait_for(feats[0], buf, sems, a)
            wait_for(stats[0], st, st_sems, a)

        code = 8 - (3 * (dr + 1) + dc + 1)
        where_at = lax.broadcasted_iota(jnp.int32, (8, HC), 1)
        which = lax.broadcasted_iota(jnp.int32, (8, HC), 0)
        flag = jnp.sum(jnp.where((where_at == code) & (which == 4), st[a, pl.ds(pl.multiple_of(16 * j, 16), 8)], 0.0))

        @pl.when(flag > 0.5)
        def _():
            col_t = (
                lax.broadcasted_iota(jnp.int32, (PADW, HC), 0) - 30 * dc
            ).astype(jnp.float32)
            for i in range(2):
                tile = half_tile(buf, a, j, i)
                four = st[a, pl.ds(pl.multiple_of((2 * j + i) * 8, 8), 8)]
                lev, gr, gc, sh = (four[k : k + 1] for k in range(4))
                v_scr[...] = gc * col_t - sh
                s = lax.dot_general(
                    tgt[...], tile, (((1,), (1,)), ((), ())), preferred_element_type=jnp.float32
                )
                ds = []
                for g in range(HALF):
                    row_t = (g + HALF * core - 30 * dr).astype(jnp.float32)
                    p = jnp.exp2(s[g * PADW : (g + 1) * PADW] * c2 - lev)
                    ds.append((p * (v_scr[...] + gr * row_t)).astype(jnp.bfloat16))
                acc[...] += jnp.dot(jnp.concatenate(ds), tile, preferred_element_type=jnp.float32)

        return carry

    lax.fori_loop(0, 3 * n_cs, step, 0)
    out[...] = acc[...].reshape(HALF, PADW, acc.shape[1])[:, :TILE]


def target_side(n_c, sc, tgt, feats, stats):
    n_cs, ch = feats[0].shape[0] // (2 * HC), tgt.shape[1]
    return pl.pallas_call(
        functools.partial(target_kernel, n_c, n_cs, math.log2(math.e) / math.sqrt(ch)),
        out_shape=jax.ShapeDtypeStruct((HALF, TILE, ch), jnp.float32),
        in_specs=[SMEM, VMEM] + [HBM] * 6,
        out_specs=VMEM,
        scratch_shapes=[
            pltpu.VMEM((3, n_cs * 2 * HC, ch), jnp.bfloat16),
            pltpu.SemaphoreType.DMA((3,)),
            pltpu.VMEM((3, n_cs * 2 * 8, HC), jnp.float32),
            pltpu.SemaphoreType.DMA((3,)),
            pltpu.VMEM((PADW, HC), jnp.float32),
            pltpu.VMEM((HC, ch), jnp.float32),
        ],
        compiler_params=pltpu.CompilerParams(vmem_limit_bytes=14 * 2**20),
        cost_estimate=COST,
        name="target_side",
    )(sc, tgt, *feats, *stats)


def shards(frames, conv_first, conv_second, candidates, counts, cotangent):
    mine = frames[0]
    ch = mine.shape[2]
    n_r, n_c = lax.axis_size("rows"), lax.axis_size("cols")
    core, row, col = (lax.axis_index(a) for a in ("pair", "rows", "cols"))
    sc = jnp.stack([core, row, col]).astype(jnp.int32)
    cand, count = candidates.reshape(9), counts.reshape(1)
    ctg = jnp.pad(cotangent, ((0, 6), (0, 0), (0, PADW - TILE))).reshape(8, HC)
    other_frame = partner(mine)
    both = (mine, other_frame)
    if n_c == 2:
        edge = jnp.stack([jnp.where(col == 0, f[:, TILE - 2 :], f[:, :2]) for f in both])
        xl = xr = send(edge, lambda r, k, c: (r, 1 - k, c))
    else:
        xl = send(jnp.stack([f[:, TILE - 2 :] for f in both]), lambda r, k, c: (r, k + 1, c))
        xr = send(jnp.stack([f[:, :2] for f in both]), lambda r, k, c: (r, k - 1, c))
    w1, w2 = fetch(after(conv_first, both), conv_second)
    w1, w2 = w1.reshape(3, 3 * ch, ch), w2.reshape(3, 3 * ch, ch)
    xl_, xr_ = after((xl, xr), w1)
    lines = []
    for i, f in enumerate(both):
        ends = [jnp.where(core == 0, x[:2], x[TILE - 2 :]) for x in (xl_[i], f, xr_[i])]
        ends[0] = jnp.where(col > 0, ends[0], 0)
        ends[2] = jnp.where(col < n_c - 1, ends[2], 0)
        lines.append(jnp.concatenate(ends, axis=1))
    z = send(jnp.stack(lines), lambda r, k, c: (r - 1 + 2 * c, k, 1 - c))
    second = encode(1, n_r, n_c, sc, mine, other_frame, xl, xr, z, w1, w2)
    side = sideways(second)
    parts = [second, partner(second)]
    first = encode(0, n_r, n_c, sc, mine, other_frame, xl, xr, z, w1, w2)
    side = after(tuple(side), first)
    for x in side:
        parts += [x, partner(x)]
    level = jnp.concatenate(parts)
    got = updown(level)
    q_side = sideways(after(first, side))
    q_parts = [first, partner(after(first, side))]
    begun = query_near(n_c, sc, cand, count, first, level)
    for x in after(tuple(q_side), begun):
        q_parts += [x, partner(x)]
    q_level = jnp.concatenate(q_parts)
    q_got = updown(q_level)
    got = after(got, q_level)
    other = partner(got)
    flow, stats, packed = query_far(n_c, sc, cand, count, first, ctg, begun, got, other)
    st_side = sideways(stats)
    st_parts = [stats, partner(stats)]
    part = grad_near(n_c, sc, cand, count, first, after(packed, st_parts[1]), level)
    for x in after(tuple(st_side), part):
        st_parts += [x, partner(x)]
    st_level = jnp.concatenate(st_parts)
    st_got = updown(st_level)
    q_got = after(q_got, st_level)
    q_other = partner(q_got)
    packed = after(packed, (st_level, q_got))
    grad_first = grad_far(n_c, sc, cand, count, first, packed, part, got, other)
    st_got = after(st_got, grad_first)
    st_other = partner(st_got)
    grad_second = target_side(
        n_c, sc, second, (q_level, q_got, q_other), (st_level, st_got, st_other)
    )
    return flow.reshape(2, HALF, PADW)[:, :, :TILE], grad_first, grad_second


def solution(mesh):
    in_specs = (
        P("pair", ("groups", "rows"), "cols", None),
        P(),
        P(),
        P(("groups", "rows"), "cols", None),
        P(("groups", "rows"), "cols"),
        P(None, ("groups", "rows", "pair"), "cols"),
    )
    out_specs = (
        P(None, ("groups", "rows", "pair"), "cols"),
        P(("groups", "rows", "pair"), "cols", None),
        P(("groups", "rows", "pair"), "cols", None),
    )
    return jax.shard_map(shards, mesh=mesh, in_specs=in_specs, out_specs=out_specs, check_vma=False)
```

```python
import functools
import math

import jax
import jax.numpy as jnp
from jax import lax
from jax.experimental import pallas as pl
from jax.experimental.pallas import tpu as pltpu
from jax.sharding import PartitionSpec as P

TILE = 30
HALF = 15
PADW = 32
HC = HALF * PADW
BODY = HALF + 2
EXT = HALF + 4
HID = HALF + 2
AXES = ("rows", "cols", "pair")
VMEM = pl.BlockSpec(memory_space=pltpu.VMEM)
SMEM = pl.BlockSpec(memory_space=pltpu.SMEM)
RB = 16
COST = pl.CostEstimate(flops=10**6, bytes_accessed=10**4, transcendentals=0)
ANY = pl.BlockSpec(memory_space=pl.ANY)
LIMIT = 12 * 2**20


def send(value, step):
    n_r, n_c = lax.axis_size("rows"), lax.axis_size("cols")
    pairs = []
    for r in range(n_r):
        for k in range(n_c):
            for c in range(2):
                r2, k2, c2 = step(r, k, c)
                if 0 <= r2 < n_r and 0 <= k2 < n_c:
                    pairs.append(((r * n_c + k) * 2 + c, (r2 * n_c + k2) * 2 + c2))
    return lax.ppermute(value, AXES, pairs)


def partner(value):
    return send(value, lambda r, k, c: (r, k, 1 - c))


def updown(value):
    return send(value, lambda r, k, c: (r + 1 - 2 * c, k, c))


def sideways(value):
    if lax.axis_size("cols") == 2:
        return [send(value, lambda r, k, c: (r, 1 - k, c))]
    return [
        send(value, lambda r, k, c: (r, k + 1, c)),
        send(value, lambda r, k, c: (r, k - 1, c)),
    ]


def after(value, *others):
    return lax.optimization_barrier((value, others))[0]


def encode_kernel(frame, n_r, n_c, sc, mine, got, xl, xr, z, w1, w2, out, ext, xcat, hid, hcat):
    core, row, col = sc[0], sc[1], sc[2]
    first_row = 2 * (1 - core)
    use_own = core == frame
    own_rows = mine[pl.ds((BODY - 4) * core, BODY)]
    got_rows = got[pl.ds((BODY - 4) * core, BODY)]
    body = jnp.where(use_own, own_rows, got_rows).astype(jnp.float32)
    slot = jnp.where(use_own, 0, 1)
    rows = pl.ds((BODY - 4) * core, BODY)
    left = jnp.where(col > 0, xl[slot, rows].astype(jnp.float32), 0.0)
    right = jnp.where(col < n_c - 1, xr[slot, rows].astype(jnp.float32), 0.0)
    ext[pl.ds(first_row, BODY), 2 : 2 + TILE] = body
    ext[pl.ds(first_row, BODY), 0:2] = left
    ext[pl.ds(first_row, BODY), 2 + TILE : 4 + TILE] = right
    ext[pl.ds(BODY * core, 2), 0 : 4 + TILE] = z[1 - slot].astype(jnp.float32)
    ch = body.shape[-1]
    for b in range(3):
        xcat[:, b * ch : (b + 1) * ch] = (
            ext[:, b : b + PADW].astype(jnp.bfloat16).reshape(EXT * PADW, ch)
        )
    acc = jnp.zeros((HID * PADW, ch), jnp.float32)
    for a in range(3):
        acc += jnp.dot(
            xcat[a * PADW : (a + HID) * PADW], w1[a], preferred_element_type=jnp.float32
        )
    hr = lax.broadcasted_iota(jnp.int32, (HID, PADW, ch), 0) + (row * TILE + core * HALF - 1)
    hc = lax.broadcasted_iota(jnp.int32, (HID, PADW, ch), 1) + (col * TILE - 1)
    inside = (hr >= 0) & (hr < n_r * TILE) & (hc >= 0) & (hc < n_c * TILE)
    hidden = jnp.where(inside, jnp.maximum(acc, 0.0).reshape(HID, PADW, ch), 0.0)
    hid[0 : HID * PADW] = hidden.reshape(HID * PADW, ch)
    hid[HID * PADW :] = jnp.zeros((8, ch), jnp.float32)
    for b in range(3):
        hcat[:, b * ch : (b + 1) * ch] = hid[b : b + HID * PADW].astype(jnp.bfloat16)
    acc2 = ext[2 : 2 + HALF, 2 : 2 + PADW].reshape(HC, ch)
    for a in range(3):
        acc2 += jnp.dot(hcat[a * PADW : a * PADW + HC], w2[a], preferred_element_type=jnp.float32)
    oc = lax.broadcasted_iota(jnp.int32, (HALF, PADW, ch), 1)
    out[...] = (
        jnp.where(oc < TILE, acc2.reshape(HALF, PADW, ch), 0.0)
        .astype(jnp.bfloat16)
        .reshape(HC, ch)
    )


def fetch_kernel(a, b, a_out, b_out, sems):
    copies = [
        pltpu.make_async_copy(a, a_out, sems.at[0]),
        pltpu.make_async_copy(b, b_out, sems.at[1]),
    ]
    for copy in copies:
        copy.start()
    for copy in copies:
        copy.wait()


def fetch(a, b):
    return pl.pallas_call(
        fetch_kernel,
        out_shape=[pltpu.VMEM(x.shape, x.dtype) for x in (a, b)],
        in_specs=[ANY, ANY],
        out_specs=[VMEM, VMEM],
        scratch_shapes=[pltpu.SemaphoreType.DMA((2,))],
        compiler_params=pltpu.CompilerParams(vmem_limit_bytes=2**20),
        cost_estimate=COST,
        name="fetch_weights",
    )(a, b)


def encode(frame, n_r, n_c, sc, mine, got, xl, xr, z, w1, w2):
    ch = mine.shape[-1]
    return pl.pallas_call(
        functools.partial(encode_kernel, frame, n_r, n_c),
        out_shape=jax.ShapeDtypeStruct((HC, ch), jnp.bfloat16),
        in_specs=[SMEM] + [VMEM] * 7,
        out_specs=VMEM,
        scratch_shapes=[
            pltpu.VMEM((EXT, 40, ch), jnp.float32),
            pltpu.VMEM((EXT * PADW, 3 * ch), jnp.bfloat16),
            pltpu.VMEM((HID * PADW + 8, ch), jnp.float32),
            pltpu.VMEM((HID * PADW, 3 * ch), jnp.bfloat16),
        ],
        compiler_params=pltpu.CompilerParams(vmem_limit_bytes=LIMIT),
        cost_estimate=COST,
        name=f"encode_frame{frame}",
    )(sc, mine, got, xl, xr, z, w1, w2)


def half_tile(tiles, j, i):
    return tiles[pl.ds(pl.multiple_of((2 * j + i) * HC, HC), HC)]


def slot_steps(slot, n_cs, n_c, col):
    dr = slot // n_cs - 1
    j = slot % n_cs
    if n_c == 2:
        dc = jnp.where(j == 0, 0, 1 - 2 * col)
    else:
        dc = jnp.where(j == 0, 0, 2 * j - 3)
    return dr, dc


def listed(slot, n_cs, n_c, col, cand, count):
    dr, dc = slot_steps(slot, n_cs, n_c, col)
    code = 3 * (dr + 1) + dc + 1
    hit = jnp.int32(0)
    for s in range(9):
        hit = jnp.where((cand[s] == code) & (s < count[0]), 1, hit)
    return dr, dc, code, hit


def half_of(dr, i, core):
    return jnp.where(dr == 0, core ^ i, jnp.where(dr < 0, i, 1 - i))


def lanes(rows):
    lane = lax.broadcasted_iota(jnp.int32, (rows, 128), 1)
    return lane, lane % PADW < TILE, lane < HC - 384


def add_tile(c2, j, dr, dc, core, q, tiles, state):
    whole = [
        lax.dot_general(
            q[...], half_tile(tiles, j, i), (((1,), (1,)), ((), ())), preferred_element_type=jnp.float32
        )
        for i in range(2)
    ]
    base = [(30 * dr + 15 * half_of(dr, i, core)).astype(jnp.float32) for i in range(2)]
    col_base = (30 * dc).astype(jnp.float32)
    lane, lane_ok, in_row = lanes(RB)
    zero = jnp.zeros((RB, 512 - HC), jnp.float32)
    for g in range(HC // RB):
        rows = slice(g * RB, (g + 1) * RB)
        s = []
        for part in whole:
            s += [part[rows, v * 128 : v * 128 + 128] for v in range(3)]
            s.append(jnp.concatenate([part[rows, 384:], zero], axis=1))
        top = jnp.maximum(
            jnp.maximum(jnp.maximum(s[0], s[1]), s[2]),
            jnp.maximum(jnp.maximum(s[4], s[5]), s[6]),
        )
        top = jnp.maximum(
            jnp.where(lane_ok, top, -jnp.inf),
            jnp.where(lane_ok & in_row, jnp.maximum(s[3], s[7]), -jnp.inf),
        )
        best = jnp.max(top, axis=1, keepdims=True) * c2
        old = state[0, rows]
        new = jnp.maximum(old, best)
        state[0, rows] = new
        factor = jnp.exp2(old - new)
        e = [jnp.exp2(x * c2 - new) for x in s]
        total, weighted = [], []
        for i in range(2):
            e0, e1, e2, e3 = e[4 * i : 4 * i + 4]
            a3 = jnp.where(in_row, e3, 0.0)
            a2 = a3 + e2
            a1 = a2 + e1
            total.append(a1 + e0)
            weighted.append(4.0 * (a1 + a2 + a3))
        both = total[0] + total[1]
        state[1, rows] = state[1, rows] * factor + both
        state[2, rows] = state[2, rows] * factor + (
            weighted[0] + weighted[1] + base[0] * total[0] + base[1] * total[1]
        )
        state[3, rows] = state[3, rows] * factor + col_base * both


def near_kernel(n_c, n_cs, c2, sc, cand, count, q, level, state):
    core, col = sc[0], sc[2]
    state[0] = jnp.full(state.shape[1:], -jnp.inf, jnp.float32)
    for k in range(1, 4):
        state[k] = jnp.zeros(state.shape[1:], jnp.float32)

    def step(j, carry):
        dr, dc, _, hit = listed(n_cs + j, n_cs, n_c, col, cand, count)

        @pl.when(hit == 1)
        def _():
            add_tile(c2, j, dr, dc, core, q, level, state)

        return carry

    lax.fori_loop(0, n_cs, step, 0)


def far_kernel(n_c, n_cs, c2, sc, cand, count, q, ctg, begun, got, other, *refs):
    flow, stats, packed_out, state = refs
    core, col = sc[0], sc[2]
    state[...] = begun[...]

    for a, tiles in ((core, got), (1 - core, other)):

        def step(j, carry):
            dr, dc, _, hit = listed(2 * a * n_cs + j, n_cs, n_c, col, cand, count)

            @pl.when(hit == 1)
            def _():
                add_tile(c2, j, dr, dc, core, q, tiles, state)

            return carry

        lax.fori_loop(0, n_cs, step, 0)
    where_at = lax.broadcasted_iota(jnp.int32, (128, HC), 0)
    ok = where_at % PADW < TILE
    norm = jnp.transpose(state[1])
    rows = jnp.transpose(state[2]) + (where_at // PADW).astype(jnp.float32) * norm
    cols = jnp.transpose(state[3]) + (where_at % PADW).astype(jnp.float32) * norm
    n_sum, r_sum, c_sum = (
        jnp.sum(jnp.where(ok, x, 0.0), axis=0, keepdims=True) for x in (norm, rows, cols)
    )
    cell = lax.broadcasted_iota(jnp.int32, (1, HC), 1)
    q_row = (cell // PADW + HALF * core).astype(jnp.float32)
    q_col = (cell % PADW).astype(jnp.float32)
    mean_r = r_sum / n_sum
    mean_c = c_sum / n_sum
    scale = 1.0 / (TILE * math.sqrt(q.shape[1]))
    cr = ctg[0:1] * scale
    cc = ctg[1:2] * scale
    shift = cr * mean_r + cc * mean_c
    best = jnp.transpose(state[0])[0:1]
    level2 = jnp.where(q_col < TILE, best + jnp.log2(n_sum), 1e30)
    flags = jnp.zeros((1, HC), jnp.float32)
    for slot in range(3 * n_cs):
        _, _, code, hit = listed(slot, n_cs, n_c, col, cand, count)
        flags = jnp.where((cell == code) & (hit == 1), 1.0, flags)
    flow_r, flow_c = (mean_r - q_row) / TILE, (mean_c - q_col) / TILE
    eight = jnp.concatenate(
        [level2, cr, cc, shift, flags, flow_r, flow_c, jnp.zeros((1, HC), jnp.float32)], axis=0
    )
    stats[...] = eight
    flow[...] = eight[5:7]
    packed_out[...] = jnp.transpose(
        jnp.concatenate([eight, jnp.zeros((120, HC), jnp.float32)], axis=0)
    )


def spread(packed, q4):
    for k in range(4):
        q4[k] = jnp.broadcast_to(packed[:, k : k + 1], (HC, 128))


def grad_tile(c2, j, dr, dc, core, q, tiles, acc, q4):
    lane, lane_ok, _ = lanes(RB)
    lane_row = (lane // PADW).astype(jnp.float32)
    lane_col = (lane % PADW + 30 * dc).astype(jnp.float32)
    for i in range(2):
        tile = half_tile(tiles, j, i)
        base = lane_row + (30 * dr + 15 * half_of(dr, i, core)).astype(jnp.float32)
        s = lax.dot_general(
            q[...], tile, (((1,), (1,)), ((), ())), preferred_element_type=jnp.float32
        )
        ds = []
        for g in range(HC // RB):
            rows = slice(g * RB, (g + 1) * RB)
            lev, gr, gc, sh = (q4[k, rows] for k in range(4))
            pull = gr * base + (gc * lane_col - sh)
            parts = []
            for v in range(4):
                width = min(128, HC - v * 128)
                p = jnp.exp2(s[rows, v * 128 : v * 128 + width] * c2 - lev[:, :width])
                d = jnp.where(lane_ok[:, :width], p * pull[:, :width], 0.0)
                parts.append(d.astype(jnp.bfloat16))
                if v < 3:
                    pull = pull + 4.0 * gr
            ds.append(jnp.concatenate(parts, axis=1))
        acc[...] += jnp.dot(jnp.concatenate(ds), tile, preferred_element_type=jnp.float32)


def grad_near_kernel(n_c, n_cs, c2, sc, cand, count, q, packed, level, acc, q4):
    core, col = sc[0], sc[2]
    acc[...] = jnp.zeros(acc.shape, jnp.float32)
    spread(packed, q4)

    def step(j, carry):
        dr, dc, _, hit = listed(n_cs + j, n_cs, n_c, col, cand, count)

        @pl.when(hit == 1)
        def _():
            grad_tile(c2, j, dr, dc, core, q, level, acc, q4)

        return carry

    lax.fori_loop(0, n_cs, step, 0)


def grad_far_kernel(n_c, n_cs, c2, sc, cand, count, q, packed, begun, got, other, *refs):
    out, q4, acc = refs
    core, col = sc[0], sc[2]
    acc[...] = begun[...]
    spread(packed, q4)

    for a, tiles in ((core, got), (1 - core, other)):

        def step(j, carry):
            dr, dc, _, hit = listed(2 * a * n_cs + j, n_cs, n_c, col, cand, count)

            @pl.when(hit == 1)
            def _():
                grad_tile(c2, j, dr, dc, core, q, tiles, acc, q4)

            return carry

        lax.fori_loop(0, n_cs, step, 0)
    out[...] = acc[...].reshape(HALF, PADW, acc.shape[1])[:, :TILE]


def tiles_call(kernel, n_c, ch, n_cs, out_shape, scratch, ins, tiles):
    return pl.pallas_call(
        functools.partial(kernel, n_c, n_cs, math.log2(math.e) / math.sqrt(ch)),
        out_shape=out_shape,
        in_specs=[SMEM] * 3 + [VMEM] * (len(ins) - 3 + len(tiles)),
        out_specs=jax.tree.map(lambda _: VMEM, out_shape),
        scratch_shapes=scratch,
        compiler_params=pltpu.CompilerParams(vmem_limit_bytes=LIMIT),
        cost_estimate=COST,
        name=kernel.__name__,
    )(*ins, *tiles)


def query_near(n_c, sc, cand, count, q, level):
    ch, n_cs = q.shape[1], level.shape[0] // (2 * HC)
    out_shape = jax.ShapeDtypeStruct((4, HC, 128), jnp.float32)
    return tiles_call(near_kernel, n_c, ch, n_cs, out_shape, [], (sc, cand, count, q), (level,)
    )


def query_far(n_c, sc, cand, count, q, ctg, begun, got, other):
    ch, n_cs = q.shape[1], got.shape[0] // (2 * HC)
    out_shape = (
        jax.ShapeDtypeStruct((2, HC), jnp.float32),
        jax.ShapeDtypeStruct((8, HC), jnp.float32),
        jax.ShapeDtypeStruct((HC, 128), jnp.float32),
    )
    scratch = [pltpu.VMEM((4, HC, 128), jnp.float32)]
    ins = (sc, cand, count, q, ctg, begun)
    return tiles_call(far_kernel, n_c, ch, n_cs, out_shape, scratch, ins, (got, other))


def grad_near(n_c, sc, cand, count, q, packed, level):
    ch, n_cs = q.shape[1], level.shape[0] // (2 * HC)
    out_shape = jax.ShapeDtypeStruct((HC, ch), jnp.float32)
    scratch = [pltpu.VMEM((4, HC, 128), jnp.float32)]
    ins = (sc, cand, count, q, packed)
    return tiles_call(grad_near_kernel, n_c, ch, n_cs, out_shape, scratch, ins, (level,))


def grad_far(n_c, sc, cand, count, q, packed, begun, got, other):
    ch, n_cs = q.shape[1], got.shape[0] // (2 * HC)
    out_shape = jax.ShapeDtypeStruct((HALF, TILE, ch), jnp.float32)
    scratch = [pltpu.VMEM((4, HC, 128), jnp.float32), pltpu.VMEM((HC, ch), jnp.float32)]
    ins = (sc, cand, count, q, packed, begun)
    return tiles_call(grad_far_kernel, n_c, ch, n_cs, out_shape, scratch, ins, (got, other))


def target_kernel(n_c, n_cs, c2, sc, tgt, *refs):
    feats, stats, (out, v_scr, acc) = refs[:3], refs[3:6], refs[6:]
    core, col = sc[0], sc[2]
    acc[...] = jnp.zeros(acc.shape, jnp.float32)
    for a, tiles, st in zip((1, 2 * core, 2 - 2 * core), feats, stats):

        def step(j, carry):
            dr, dc = slot_steps(a * n_cs + j, n_cs, n_c, col)
            code = 8 - (3 * (dr + 1) + dc + 1)
            where_at = lax.broadcasted_iota(jnp.int32, (8, HC), 1)
            which = lax.broadcasted_iota(jnp.int32, (8, HC), 0)
            flag = jnp.sum(jnp.where((where_at == code) & (which == 4), st[pl.ds(pl.multiple_of(16 * j, 16), 8)], 0.0))

            @pl.when(flag > 0.5)
            def _():
                col_t = (
                    lax.broadcasted_iota(jnp.int32, (PADW, HC), 0) - 30 * dc
                ).astype(jnp.float32)
                for i in range(2):
                    tile = half_tile(tiles, j, i)
                    four = st[pl.ds(pl.multiple_of((2 * j + i) * 8, 8), 8)]
                    lev, gr, gc, sh = (four[k : k + 1] for k in range(4))
                    v_scr[...] = gc * col_t - sh
                    s = lax.dot_general(
                        tgt[...], tile, (((1,), (1,)), ((), ())), preferred_element_type=jnp.float32
                    )
                    ds = []
                    for g in range(HALF):
                        row_t = (g + HALF * core - 30 * dr).astype(jnp.float32)
                        p = jnp.exp2(s[g * PADW : (g + 1) * PADW] * c2 - lev)
                        ds.append((p * (v_scr[...] + gr * row_t)).astype(jnp.bfloat16))
                    acc[...] += jnp.dot(jnp.concatenate(ds), tile, preferred_element_type=jnp.float32)

            return carry

        lax.fori_loop(0, n_cs, step, 0)
    out[...] = acc[...].reshape(HALF, PADW, acc.shape[1])[:, :TILE]


def target_side(n_c, sc, tgt, feats, stats):
    n_cs, ch = feats[0].shape[0] // (2 * HC), tgt.shape[1]
    return pl.pallas_call(
        functools.partial(target_kernel, n_c, n_cs, math.log2(math.e) / math.sqrt(ch)),
        out_shape=jax.ShapeDtypeStruct((HALF, TILE, ch), jnp.float32),
        in_specs=[SMEM] + [VMEM] * 7,
        out_specs=VMEM,
        scratch_shapes=[
            pltpu.VMEM((PADW, HC), jnp.float32),
            pltpu.VMEM((HC, ch), jnp.float32),
        ],
        compiler_params=pltpu.CompilerParams(vmem_limit_bytes=LIMIT),
        cost_estimate=COST,
        name="target_side",
    )(sc, tgt, *feats, *stats)


def shards(frames, conv_first, conv_second, candidates, counts, cotangent):
    mine = frames[0]
    ch = mine.shape[2]
    n_r, n_c = lax.axis_size("rows"), lax.axis_size("cols")
    core, row, col = (lax.axis_index(a) for a in ("pair", "rows", "cols"))
    sc = jnp.stack([core, row, col]).astype(jnp.int32)
    cand, count = candidates.reshape(9), counts.reshape(1)
    ctg = jnp.pad(cotangent, ((0, 6), (0, 0), (0, PADW - TILE))).reshape(8, HC)
    other_frame = partner(mine)
    both = (mine, other_frame)
    if n_c == 2:
        edge = jnp.stack([jnp.where(col == 0, f[:, TILE - 2 :], f[:, :2]) for f in both])
        xl = xr = send(edge, lambda r, k, c: (r, 1 - k, c))
    else:
        xl = send(jnp.stack([f[:, TILE - 2 :] for f in both]), lambda r, k, c: (r, k + 1, c))
        xr = send(jnp.stack([f[:, :2] for f in both]), lambda r, k, c: (r, k - 1, c))
    w1, w2 = fetch(after(conv_first, both), conv_second)
    w1, w2 = w1.reshape(3, 3 * ch, ch), w2.reshape(3, 3 * ch, ch)
    xl_, xr_ = after((xl, xr), w1)
    lines = []
    for i, f in enumerate(both):
        ends = [jnp.where(core == 0, x[:2], x[TILE - 2 :]) for x in (xl_[i], f, xr_[i])]
        ends[0] = jnp.where(col > 0, ends[0], 0)
        ends[2] = jnp.where(col < n_c - 1, ends[2], 0)
        lines.append(jnp.concatenate(ends, axis=1))
    z = send(jnp.stack(lines), lambda r, k, c: (r - 1 + 2 * c, k, 1 - c))
    second = encode(1, n_r, n_c, sc, mine, other_frame, xl, xr, z, w1, w2)
    side = sideways(second)
    parts = [second, partner(second)]
    first = encode(0, n_r, n_c, sc, mine, other_frame, xl, xr, z, w1, w2)
    side = after(tuple(side), first)
    for x in side:
        parts += [x, partner(x)]
    level = jnp.concatenate(parts)
    got = updown(level)
    q_side = sideways(after(first, side))
    q_parts = [first, partner(after(first, side))]
    begun = query_near(n_c, sc, cand, count, first, level)
    for x in after(tuple(q_side), begun):
        q_parts += [x, partner(x)]
    q_level = jnp.concatenate(q_parts)
    q_got = updown(q_level)
    got = after(got, q_level)
    other = partner(got)
    flow, stats, packed = query_far(n_c, sc, cand, count, first, ctg, begun, got, other)
    st_side = sideways(stats)
    st_parts = [stats, partner(stats)]
    part = grad_near(n_c, sc, cand, count, first, after(packed, st_parts[1]), level)
    for x in after(tuple(st_side), part):
        st_parts += [x, partner(x)]
    st_level = jnp.concatenate(st_parts)
    st_got = updown(st_level)
    q_got = after(q_got, st_level)
    q_other = partner(q_got)
    packed = after(packed, (st_level, q_got))
    grad_first = grad_far(n_c, sc, cand, count, first, packed, part, got, other)
    st_got = after(st_got, grad_first)
    st_other = partner(st_got)
    grad_second = target_side(
        n_c, sc, second, (q_level, q_got, q_other), (st_level, st_got, st_other)
    )
    return flow.reshape(2, HALF, PADW)[:, :, :TILE], grad_first, grad_second


def solution(mesh):
    in_specs = (
        P("pair", ("groups", "rows"), "cols", None),
        P(),
        P(),
        P(("groups", "rows"), "cols", None),
        P(("groups", "rows"), "cols"),
        P(None, ("groups", "rows", "pair"), "cols"),
    )
    out_specs = (
        P(None, ("groups", "rows", "pair"), "cols"),
        P(("groups", "rows", "pair"), "cols", None),
        P(("groups", "rows", "pair"), "cols", None),
    )
    return jax.shard_map(shards, mesh=mesh, in_specs=in_specs, out_specs=out_specs, check_vma=False)
```
